32 devices in a mesh: leaf: 8 (over z, x), front: 4 (over y, core).
Axes of the slice: x: 2, y: 2, z: 4, core: 2. Of those that a mesh axis runs over, the one named last changes fastest.
Arguments:
- child_update: bfloat16 [8, 4, 1, 3, 256, 3072], P('leaf', 'front'), may hold values from -60 to 60, as said below
- sep_one: bfloat16 [8, 4, 1, 4, 256, 512], P('leaf', 'front'), may hold values from -60 to 60, as said below
- sep_two: bfloat16 [8, 4, 1, 4, 256, 256], P('leaf', 'front'), may hold values from -60 to 60, as said below
- map_one: int32 [8, 1, 4, 3], replicated, may hold values from 0 to 3, as said below
- map_two: int32 [4, 1, 4, 3], replicated, may hold values from 0 to 3, as said below
- mask_one: int32 [4, 1, 12, 4], replicated, may hold values 0 or 1
- mask_two: int32 [2, 1, 12, 4], replicated, may hold values 0 or 1
Outputs:
- factor_one: float32 [8, 4, 1, 4, 256, 512], P('leaf', 'front')
- factor_two: float32 [8, 4, 1, 4, 256, 256], P('leaf', 'front')
- update_two: bfloat16 [8, 4, 1, 3, 256, 768], P('leaf', 'front')
The draws below stay inside these ranges and needn't reach their ends.
Inputs may be any that keep to these rules, and one draw needn't show every extreme that they name: `child_update`: every child[l,b] is symmetric positive definite. `sep_one`: the top 1024 rows of each front's initial entries form a symmetric positive definite block, and every assembled front is positive definite. `sep_two`: the top 1024 rows of each front's initial entries form a symmetric positive definite block, and every assembled front is positive definite. `map_one`: for each child, batch and j the 3 entries are distinct; the two children 2p and 2p + 1 leave out different slots, so every parent tile receives one or two child tiles. `map_two`: for each first-level front, batch and j the 3 entries are distinct; fronts 2q and 2q + 1 leave out different slots, so every parent tile receives one or two child tiles.
All inputs are finite; a program needn't handle non-finite values.
Results may differ from the reference program's by a relative error of at most 0.0047.
Values may be sent and summed in bfloat16 or wider, within the bound.
No kernel may reach another device: no remote copies, remote signals or barrier semaphores. Data moves between devices by JAX's collectives and lax.ppermute only.
A program may use at most 192 MiB of HBM per device.

```python
import math
import jax
import jax.numpy as jnp
from jax import lax

TILE = 256
ST = 4
UT = 12
BATCH = 1
S = 1024
U = 3072
F = 4096
PT = 4
CT = 3
N_LEAF = 8
N_FRONT = 4


def spread_block(key, matrix_order, diagonal_shift, gram_weight):
    key_factor = jax.random.fold_in(key, 0)
    factor_draw = jax.random.normal(key_factor, (BATCH, matrix_order, matrix_order), jnp.float32)
    scaled = factor_draw
    gram = jnp.einsum('bik,bjk->bij', scaled, scaled, precision=lax.Precision.HIGHEST) * (gram_weight / matrix_order)
    gram = 0.5 * (gram + jnp.swapaxes(gram, 1, 2))
    identity = jnp.eye(matrix_order, dtype=jnp.float32)
    return gram + diagonal_shift * identity[None, :, :]


def draw_child_update(key, part):

    def single(leaf_number):
        return spread_block(jax.random.fold_in(key, leaf_number), U, 0.5, 2.5)
    stacked = lax.map(single, jnp.arange(N_LEAF))
    shaped = stacked.reshape(N_LEAF, BATCH, CT, N_FRONT, TILE, U)
    return jnp.transpose(shaped, (0, 3, 1, 2, 4, 5)).astype(jnp.bfloat16)


def draw_entries(key, groups, strength):
    fronts = N_LEAF // groups
    deviation = strength / (math.sqrt(U) + math.sqrt(S))

    def single(front_number):
        key_top, key_low = jax.random.split(jax.random.fold_in(key, front_number))
        separator_block = spread_block(key_top, S, 2.5, 2.5)
        coupling = deviation * jax.random.normal(key_low, (BATCH, U, S), jnp.float32)
        return jnp.concatenate([separator_block, coupling], axis=1)
    stacked = lax.map(single, jnp.arange(fronts))
    shaped = stacked.reshape(fronts, BATCH, PT, N_FRONT, TILE, groups, S // groups)
    return jnp.transpose(shaped, (0, 5, 3, 1, 2, 4, 6)).reshape(N_LEAF, N_FRONT, BATCH, PT, TILE, S // groups)


def draw_sep_one(key, part):
    return draw_entries(jax.random.fold_in(key, 11), 2, 1.0).astype(jnp.bfloat16)


def draw_sep_two(key, part):
    return draw_entries(jax.random.fold_in(key, 23), 4, 0.8).astype(jnp.bfloat16)


def draw_tile_maps(key, fronts):
    key_first, key_offset, key_order = jax.random.split(key, 3)
    omitted_first = jax.random.randint(key_first, (fronts, BATCH, N_FRONT), 0, PT)
    offset_draw = jax.random.randint(key_offset, (fronts, BATCH, N_FRONT), 1, PT)
    second = (omitted_first + offset_draw) % PT
    omitted = jnp.stack([omitted_first, second], axis=1)
    order_keys = jax.random.split(key_order, fronts * 2 * BATCH * N_FRONT)
    ordering = jax.vmap(lambda single_key: jax.random.permutation(single_key, CT))(order_keys)
    ordering = ordering.reshape(fronts, 2, BATCH, N_FRONT, CT)
    slots = (omitted[..., None] + 1 + ordering) % PT
    return slots.reshape(2 * fronts, BATCH, N_FRONT, CT).astype(jnp.int32)


def draw_map_one(key, part):
    return draw_tile_maps(jax.random.fold_in(key, 37), N_LEAF // 2)


def draw_map_two(key, part):
    return draw_tile_maps(jax.random.fold_in(key, 41), N_LEAF // 4)


def place_ends(values, stream_key, low, top_value):
    longest = values.shape.index(max(values.shape))
    spots = []
    for shift in (0, 1):
        where = [jax.random.randint(jax.random.fold_in(stream_key, axis), (), 0, length) for axis, length in enumerate(values.shape)]
        where[longest] = (where[longest] + shift) % values.shape[longest]
        spots.append(tuple(where))
    return values.at[spots[0]].set(low).at[spots[1]].set(top_value)


def setup_inputs(seed: int = 0) -> dict:
    streams_of = jax.random.split(jax.random.key(seed), 8)
    child_update = draw_child_update(jax.random.fold_in(streams_of[7], 71), 0)
    sep_one = draw_sep_one(jax.random.fold_in(streams_of[7], 71), 0)
    sep_two = draw_sep_two(jax.random.fold_in(streams_of[7], 71), 0)
    map_one = draw_map_one(jax.random.fold_in(streams_of[7], 71), 0)
    map_two = draw_map_two(jax.random.fold_in(streams_of[7], 71), 0)
    mask_one = place_ends((jax.random.randint(streams_of[5], (N_LEAF // 2, BATCH, UT, ST), 0, 2) < 1).astype(jnp.int32), jax.random.fold_in(streams_of[5], 1), 0, 1)
    mask_two = place_ends((jax.random.randint(streams_of[6], (N_LEAF // 4, BATCH, UT, ST), 0, 2) < 1).astype(jnp.int32), jax.random.fold_in(streams_of[6], 1), 0, 1)
    return {"child_update": child_update, "sep_one": sep_one, "sep_two": sep_two, "map_one": map_one, "map_two": map_two, "mask_one": mask_one, "mask_two": mask_two}


def tile_targets(tile_map):
    slots = jnp.swapaxes(tile_map, -1, -2)
    offsets = jnp.arange(N_FRONT, dtype=jnp.int32)
    return (slots * N_FRONT + offsets).reshape(slots.shape[:-2] + (UT,)).astype(jnp.int32)

def extend_add(update, targets):
    within = jnp.arange(TILE, dtype=jnp.int32)
    positions = (targets[:, None] * TILE + within[None, :]).reshape(U).astype(jnp.int32)
    canvas = jnp.zeros((F, F), jnp.float32)
    return canvas.at[positions[:, None], positions[None, :]].add(update.astype(jnp.float32))

def assemble_front(first_child, second_child, first_targets, second_targets, initial, tile_mask):
    canvas = extend_add(first_child, first_targets) + extend_add(second_child, second_targets)
    mask_full = jnp.repeat(jnp.repeat(tile_mask.astype(jnp.float32), TILE, axis=0), TILE, axis=1)
    coupling = initial[S:].astype(jnp.float32) * mask_full
    columns = jnp.concatenate([initial[:S].astype(jnp.float32), coupling], axis=0)
    canvas = canvas.at[:, :S].add(columns)
    canvas = canvas.at[:S, S:].add(coupling.T)
    return canvas

def factor_front(canvas):
    lower_factor = jnp.linalg.cholesky(canvas[:S, :S])
    panel_full = lax.linalg.triangular_solve(lower_factor, canvas[S:, :S], left_side=False, lower=True, transpose_a=True)
    panel_round = panel_full.astype(jnp.bfloat16)
    trailing = canvas[S:, S:] - jnp.dot(panel_round.astype(jnp.float32), panel_round.T.astype(jnp.float32), preferred_element_type=jnp.float32)
    return (jnp.concatenate([lower_factor, panel_full], axis=0), trailing.astype(jnp.bfloat16))

def factor_level(children, targets, initial, tile_mask):
    fronts = initial.shape[0]
    count = fronts * BATCH
    inputs = (children[0::2].reshape(count, U, U), children[1::2].reshape(count, U, U), targets[0::2].reshape(count, UT), targets[1::2].reshape(count, UT), initial.reshape(count, F, S), tile_mask.reshape(count, UT, ST))

    def single(packed):
        return factor_front(assemble_front(*packed))
    factors, updates = lax.map(single, inputs)
    return (factors.reshape(fronts, BATCH, F, S), updates.reshape(fronts, BATCH, U, U))

def unpack_entries(entries, groups):
    fronts = N_LEAF // groups
    shaped = entries.reshape(fronts, groups, N_FRONT, BATCH, PT, TILE, S // groups)
    return jnp.transpose(shaped, (0, 3, 4, 2, 5, 1, 6)).reshape(fronts, BATCH, F, S)

def pack_columns(matrix, groups, row_tiles):
    fronts = matrix.shape[0]
    width = matrix.shape[-1]
    shaped = matrix.reshape(fronts, BATCH, row_tiles, N_FRONT, TILE, groups, width // groups)
    return jnp.transpose(shaped, (0, 5, 3, 1, 2, 4, 6)).reshape(fronts * groups, N_FRONT, BATCH, row_tiles, TILE, width // groups)

def reference(child_update, sep_one, sep_two, map_one, map_two, mask_one, mask_two):
    children = jnp.transpose(child_update, (0, 2, 3, 1, 4, 5)).reshape(N_LEAF, BATCH, U, U)
    target_one = tile_targets(map_one)
    target_two = tile_targets(map_two)
    orig_one = unpack_entries(sep_one, 2)
    orig_two = unpack_entries(sep_two, 4)
    factors_one, update_one = factor_level(children, target_one, orig_one, mask_one)
    factors_two, update_full = factor_level(update_one, target_two, orig_two, mask_two)
    factor_one = pack_columns(factors_one, 2, PT)
    factor_two = pack_columns(factors_two, 4, PT)
    update_two = pack_columns(update_full, 4, CT)
    return (factor_one, factor_two, update_two)
```

```python
import jax
import jax.numpy as jnp
from jax import lax
from jax.experimental import pallas as pl
from jax.experimental.pallas import tpu as pltpu
from jax.sharding import PartitionSpec as P

TILE = 256
ST = 4
UT = 12
FT = 16
S = 1024
U = 3072
F = 4096
BLK = 128
GRP = 8
NT = (((1,), (1,)), ((), ()))


def halves(x):
    high = x.astype(jnp.bfloat16)
    low = (x - high.astype(jnp.float32)).astype(jnp.bfloat16)
    return high, low


def left_parts(x):
    high, low = halves(x)
    return jnp.concatenate([high, low, high], axis=1)


def right_rows(x):
    high, low = halves(x)
    return jnp.concatenate([high, high, low], axis=0)


def right_lanes(x):
    high, low = halves(x)
    return jnp.concatenate([high, high, low], axis=1)


def dot_rows(left, right):
    return jnp.dot(left, right, preferred_element_type=jnp.float32)


def dot_lanes(left, right):
    return lax.dot_general(left, right, NT, preferred_element_type=jnp.float32)


def spread_row(ref, index):
    return jnp.broadcast_to(ref[index], (GRP, BLK))


def factor_diagonal(block, done_ref, pivot_ref, rows_ref):
    steps = BLK // GRP
    row_id = lax.broadcasted_iota(jnp.int32, (GRP, BLK), 0)
    lane_id = lax.broadcasted_iota(jnp.int32, (GRP, BLK), 1)
    matrix = [block[GRP * g : GRP * (g + 1), :] for g in range(steps)]
    inverse = [jnp.where(lane_id == row_id + GRP * g, 1.0, 0.0).astype(jnp.float32) for g in range(steps)]
    for g in range(steps):
        first = GRP * g
        slot = g % 2
        current = matrix[g]
        rows_ref[slot, :, 0:BLK] = current
        rows_ref[slot, :, BLK:] = inverse[g]
        for i in range(GRP):
            pivot_ref[slot, i] = jnp.broadcast_to(current[:, first + i : first + i + 1], (GRP, BLK))
        entry = {}
        for m in range(GRP):
            for i in range(m + 1):
                entry[m, i] = jnp.broadcast_to(pivot_ref[slot, i, m : m + 1, :], (GRP, BLK))
                entry[i, m] = entry[m, i]
        left = [jnp.broadcast_to(rows_ref[slot, m : m + 1, 0:BLK], (GRP, BLK)) for m in range(GRP)]
        right = [jnp.broadcast_to(rows_ref[slot, m : m + 1, BLK:], (GRP, BLK)) for m in range(GRP)]
        for i in range(GRP):
            root = lax.rsqrt(entry[i, i])
            scale = root * root
            done_ref[first + i : first + i + 1, 0:BLK] = (left[i] * root)[0:1]
            done_ref[first + i : first + i + 1, BLK:] = (right[i] * root)[0:1]
            left[i] = left[i] * scale
            right[i] = right[i] * scale
            scaled = {c: entry[i, c] * scale for c in range(i + 1, GRP)}
            for m in range(GRP):
                if m == i:
                    continue
                weight = entry[m, i]
                left[m] = left[m] - weight * left[i]
                right[m] = right[m] - weight * right[i]
                for c in range(i + 1, GRP):
                    if m > c:
                        continue
                    entry[m, c] = entry[m, c] - weight * scaled[c]
            for m in range(i + 1, GRP):
                for c in range(i + 1, m):
                    entry[m, c] = entry[c, m]
            for c in range(i + 1, GRP):
                entry[i, c] = scaled[c]
        for later in range(g + 1, steps):
            rows = matrix[later]
            total_left, total_right = None, None
            for i in range(GRP):
                weight = jnp.broadcast_to(rows[:, first + i : first + i + 1], (GRP, BLK))
                part_left, part_right = weight * left[i], weight * right[i]
                total_left = part_left if total_left is None else total_left + part_left
                total_right = part_right if total_right is None else total_right + part_right
            matrix[later] = rows - total_left
            inverse[later] = inverse[later] - total_right


def cholesky_kernel(pivot_ref, lower_ref, inverse_ref, work, done, block_inverse, entries, rows):
    order = pivot_ref.shape[0]
    blocks = order // BLK
    work[...] = pivot_ref[...]
    lower_ref[...] = jnp.zeros_like(lower_ref)
    row_id = lax.broadcasted_iota(jnp.int32, (BLK, BLK), 0)
    lane_id = lax.broadcasted_iota(jnp.int32, (BLK, BLK), 1)

    def step(k, carry):
        start = pl.multiple_of(k * BLK, BLK)
        span = pl.ds(start, BLK)
        factor_diagonal(work[span, span], done, entries, rows)
        upper = jnp.where(lane_id >= row_id, done[:, 0:BLK], 0.0)
        lower_ref[span, span] = upper.T
        block_inverse[k] = done[:, BLK:]
        for fixed in range(blocks - 1):
            after = (fixed + 1) * BLK

            @pl.when(k == fixed)
            def _():
                strip = dot_rows(
                    left_parts(done[:, BLK:]), right_rows(work[after - BLK : after, after:])
                )
                column = strip.T
                lower_ref[after:, after - BLK : after] = column
                left = left_parts(column)
                right = right_rows(strip)
                width = order - after
                for top in range(0, width, TILE):
                    high = min(TILE, width - top)
                    work[after + top : after + top + high, after + top :] = work[
                        after + top : after + top + high, after + top :
                    ] - dot_rows(left[top : top + high], right[:, top:])

        return carry

    lax.fori_loop(0, blocks, step, 0)
    for tile in range(order // TILE):
        base = tile * TILE
        first, second = block_inverse[2 * tile], block_inverse[2 * tile + 1]
        corner = lower_ref[base + BLK : base + TILE, base : base + BLK]
        mixed = dot_rows(left_parts(corner), right_rows(first))
        mixed = -dot_rows(left_parts(second), right_rows(mixed))
        inverse_ref[tile, 0:BLK, 0:BLK] = first
        inverse_ref[tile, 0:BLK, BLK:] = jnp.zeros((BLK, BLK), jnp.float32)
        inverse_ref[tile, BLK:, 0:BLK] = mixed
        inverse_ref[tile, BLK:, BLK:] = second


def cholesky(pivot):
    order = pivot.shape[0]
    return pl.pallas_call(
        cholesky_kernel,
        out_shape=(
            jax.ShapeDtypeStruct((order, order), jnp.float32),
            jax.ShapeDtypeStruct((order // TILE, TILE, TILE), jnp.float32),
        ),
        in_specs=[pl.BlockSpec(memory_space=pltpu.VMEM)],
        out_specs=(pl.BlockSpec(memory_space=pltpu.VMEM), pl.BlockSpec(memory_space=pltpu.VMEM)),
        scratch_shapes=[
            pltpu.VMEM((order, order), jnp.float32),
            pltpu.VMEM((BLK, 2 * BLK), jnp.float32),
            pltpu.VMEM((order // BLK, BLK, BLK), jnp.float32),
            pltpu.VMEM((2, GRP, GRP, BLK), jnp.float32),
            pltpu.VMEM((2, GRP, 2 * BLK), jnp.float32),
        ],
        compiler_params=pltpu.CompilerParams(vmem_limit_bytes=40 * 2**20),
        name="cholesky",
    )(pivot)


def panel_kernel(coupling_ref, lower_ref, inverse_ref, panel_ref):
    order = lower_ref.shape[0]
    solved = []
    for k in range(order // TILE):
        span = slice(k * TILE, (k + 1) * TILE)
        rest = coupling_ref[:, span]
        if k:
            left = jnp.concatenate([part[0] for part in solved], axis=1)
            low = jnp.concatenate([part[1] for part in solved], axis=1)
            high_lower, low_lower = halves(lower_ref[span, 0 : k * TILE])
            rest = rest - dot_lanes(
                jnp.concatenate([left, low, left], axis=1),
                jnp.concatenate([high_lower, high_lower, low_lower], axis=1),
            )
        block = dot_lanes(left_parts(rest), right_lanes(inverse_ref[k]))
        panel_ref[:, span] = block
        solved.append(halves(block))


def solve_panel(coupling, lower, inverse):
    spec = pl.BlockSpec(memory_space=pltpu.VMEM)
    return pl.pallas_call(
        panel_kernel,
        out_shape=jax.ShapeDtypeStruct(coupling.shape, jnp.float32),
        in_specs=[spec, spec, spec],
        out_specs=spec,
        compiler_params=pltpu.CompilerParams(vmem_limit_bytes=40 * 2**20),
        name="panel",
    )(coupling, lower, inverse)


def swapped(value, axis, apart):
    mask = 2**apart
    pairs = [(source, source ^ mask) for source in range(lax.axis_size(axis))]
    return lax.ppermute(value, axis, pairs)


def place_tiles(blocks, row_source, row_live, col_source, col_live):
    taken = jnp.take(blocks, row_source, axis=0)
    taken = jnp.take(taken, col_source, axis=2)
    keep = jnp.logical_and(row_live[:, None, None, None], col_live[None, None, :, None])
    return jnp.where(keep, taken.astype(jnp.float32), 0.0)


def place_child(child_rows, tile_map, column):
    batch_count = child_rows.shape[0]
    local_tiles = child_rows.shape[1]
    groups = tile_map.shape[1]
    slot_count = FT // groups
    own_slots = lax.dynamic_index_in_dim(tile_map, column, 1, keepdims=False)
    row_hit = own_slots[..., None] == jnp.arange(slot_count, dtype=jnp.int32)
    row_source = jnp.sum(
        row_hit.astype(jnp.int32) * jnp.arange(local_tiles, dtype=jnp.int32)[None, :, None], axis=1
    )
    row_live = jnp.any(row_hit, axis=1)
    targets = (jnp.swapaxes(tile_map, 1, 2) * groups + jnp.arange(groups, dtype=jnp.int32)).reshape(
        batch_count, UT
    )
    col_hit = targets[..., None] == jnp.arange(FT, dtype=jnp.int32)
    col_source = jnp.sum(
        col_hit.astype(jnp.int32) * jnp.arange(UT, dtype=jnp.int32)[None, :, None], axis=1
    )
    col_live = jnp.any(col_hit, axis=1)
    blocks = child_rows.reshape(batch_count, local_tiles, TILE, UT, TILE)
    placed = jax.vmap(place_tiles)(blocks, row_source, row_live, col_source, col_live)
    return placed.reshape(batch_count, slot_count, TILE, F)


def join_halves(mine, other, position):
    lower_first = jnp.concatenate([mine, other], axis=-1)
    upper_first = jnp.concatenate([other, mine], axis=-1)
    return jnp.where(position == 0, lower_first, upper_first)


def add_initial(canvas, initial, mask_front, column):
    batch_count = canvas.shape[0]
    slot_count = canvas.shape[1]
    groups = lax.axis_size("front")
    mask_rows = mask_front.reshape(batch_count, slot_count - 1, groups, ST)
    mask_rows = lax.dynamic_index_in_dim(mask_rows, column, 2, keepdims=False).astype(jnp.float32)
    mask_all = jnp.concatenate([jnp.ones((batch_count, 1, ST), jnp.float32), mask_rows], axis=1)
    weighted = initial.astype(jnp.float32).reshape(batch_count, slot_count, TILE, ST, TILE)
    weighted = (weighted * mask_all[:, :, None, :, None]).reshape(batch_count, slot_count, TILE, S)
    return jnp.concatenate([canvas[:, :, :, :S] + weighted, canvas[:, :, :, S:]], axis=-1)


def factor_front(canvas, column):
    batch_count = canvas.shape[0]
    local_tiles = canvas.shape[1] - 1
    groups = lax.axis_size("front")
    pivot_piece = canvas[:, :1, :, :S]
    pivot_all = lax.all_gather(pivot_piece[None], "front", axis=0, tiled=True)
    pivot_block = jnp.moveaxis(pivot_all, 0, 2).reshape(batch_count, S, S)
    lower_factor, inverse = (
        jnp.stack(parts) for parts in zip(*[cholesky(pivot_block[b]) for b in range(batch_count)])
    )
    coupling = canvas[:, 1:, :, :S].reshape(batch_count, local_tiles * TILE, S)
    panel_full = jnp.stack(
        [solve_panel(coupling[b], lower_factor[b], inverse[b]) for b in range(batch_count)]
    )
    panel_round = panel_full.astype(jnp.bfloat16)
    shared = lax.all_gather(
        panel_round.reshape(batch_count, local_tiles, TILE, S)[None], "front", axis=0, tiled=True
    )
    ordered = jnp.transpose(shared, (1, 2, 0, 3, 4)).reshape(batch_count, U, S)
    own_lower = lax.dynamic_index_in_dim(
        lower_factor.reshape(batch_count, groups, TILE, S), column, 1, keepdims=True
    )
    factor_rows = jnp.concatenate(
        [own_lower, panel_full.reshape(batch_count, local_tiles, TILE, S)], axis=1
    )
    trailing = canvas[:, 1:, :, S:].reshape(batch_count, local_tiles * TILE, U)
    product = jnp.einsum("brk,bnk->brn", panel_round, ordered, preferred_element_type=jnp.float32)
    update = (trailing - product).astype(jnp.bfloat16)
    return (factor_rows, update)


def body(child_update, sep_one, sep_two, map_one, map_two, mask_one, mask_two):
    column = lax.axis_index("front")
    leaf_index = lax.axis_index("leaf")
    half_index = leaf_index % 2
    quarter_index = leaf_index % 4
    pair_index = leaf_index // 2
    quad_index = leaf_index // 4
    side_index = pair_index % 2
    child_rows = child_update[0, 0]
    batch_count = child_rows.shape[0]
    local_tiles = child_rows.shape[1]
    entries_one = sep_one[0, 0]
    entries_two = sep_two[0, 0]
    peer_rows, peer_one, peer_two = swapped((child_rows, entries_one, entries_two), "leaf", 0)
    map_own = lax.dynamic_index_in_dim(map_one, leaf_index, 0, keepdims=False)
    map_peer = lax.dynamic_index_in_dim(map_one, jnp.bitwise_xor(leaf_index, 1), 0, keepdims=False)
    front_first = place_child(child_rows, map_own, column) + place_child(
        peer_rows, map_peer, column
    )
    initial_one = join_halves(entries_one, peer_one, half_index)
    mask_front = lax.dynamic_index_in_dim(mask_one, pair_index, 0, keepdims=False)
    front_first = add_initial(front_first, initial_one, mask_front, column)
    factor_rows_one, update_one = factor_front(front_first, column)
    factor_one = lax.dynamic_slice_in_dim(factor_rows_one, half_index * (S // 2), S // 2, 3)
    entries_half = join_halves(entries_two, peer_two, quarter_index % 2)
    update_far, entries_far = swapped((update_one, entries_half), "leaf", 1)
    map_near = lax.dynamic_index_in_dim(map_two, pair_index, 0, keepdims=False)
    map_far = lax.dynamic_index_in_dim(map_two, jnp.bitwise_xor(pair_index, 1), 0, keepdims=False)
    near_rows = update_one.reshape(batch_count, local_tiles, TILE, U)
    far_rows = update_far.reshape(batch_count, local_tiles, TILE, U)
    front_second = place_child(near_rows, map_near, column) + place_child(far_rows, map_far, column)
    initial_two = join_halves(entries_half, entries_far, side_index)
    mask_second = lax.dynamic_index_in_dim(mask_two, quad_index, 0, keepdims=False)
    front_second = add_initial(front_second, initial_two, mask_second, column)
    factor_rows_two, update_last = factor_front(front_second, column)
    update_last = lax.dynamic_slice_in_dim(update_last, quarter_index * (U // 4), U // 4, 2)
    factor_two = lax.dynamic_slice_in_dim(factor_rows_two, quarter_index * (S // 4), S // 4, 3)
    update_two = update_last.reshape(batch_count, local_tiles, TILE, U // 4)
    return (factor_one[None, None], factor_two[None, None], update_two[None, None])


def solution(mesh):
    return jax.shard_map(
        body,
        mesh=mesh,
        in_specs=(
            P("leaf", "front", None, None, None, None),
            P("leaf", "front", None, None, None, None),
            P("leaf", "front", None, None, None, None),
            P(),
            P(),
            P(),
            P(),
        ),
        out_specs=(
            P("leaf", "front", None, None, None, None),
            P("leaf", "front", None, None, None, None),
            P("leaf", "front", None, None, None, None),
        ),
        check_vma=False,
    )
```

```python
import jax
import jax.numpy as jnp
from jax import lax
from jax.experimental import pallas as pl
from jax.experimental.pallas import tpu as pltpu
from jax.sharding import PartitionSpec as P

S = 1024
BLK = 128
GRP = 8
TILE = 256
NT = (((1,), (1,)), ((), ()))


def halves(x):
    high = x.astype(jnp.bfloat16)
    low = (x - high.astype(jnp.float32)).astype(jnp.bfloat16)
    return high, low


def left_parts(x):
    high, low = halves(x)
    return jnp.concatenate([high, low, high], axis=1)


def right_rows(x):
    high, low = halves(x)
    return jnp.concatenate([high, high, low], axis=0)


def right_lanes(x):
    high, low = halves(x)
    return jnp.concatenate([high, high, low], axis=1)


def dot_rows(left, right):
    return jnp.dot(left, right, preferred_element_type=jnp.float32)


def dot_lanes(left, right):
    return lax.dot_general(left, right, NT, preferred_element_type=jnp.float32)


def spread_row(ref, index):
    return jnp.broadcast_to(ref[index], (GRP, BLK))


def factor_diagonal(block, done_ref, pivot_ref, rows_ref):
    steps = BLK // GRP
    row_id = lax.broadcasted_iota(jnp.int32, (GRP, BLK), 0)
    lane_id = lax.broadcasted_iota(jnp.int32, (GRP, BLK), 1)
    matrix = [block[GRP * g : GRP * (g + 1), :] for g in range(steps)]
    inverse = [jnp.where(lane_id == row_id + GRP * g, 1.0, 0.0).astype(jnp.float32) for g in range(steps)]
    for g in range(steps):
        first = GRP * g
        slot = g % 2
        current = matrix[g]
        rows_ref[slot, :, 0:BLK] = current
        rows_ref[slot, :, BLK:] = inverse[g]
        for i in range(GRP):
            pivot_ref[slot, i] = jnp.broadcast_to(current[:, first + i : first + i + 1], (GRP, BLK))
        entry = {}
        for m in range(GRP):
            for i in range(m + 1):
                entry[m, i] = jnp.broadcast_to(pivot_ref[slot, i, m : m + 1, :], (GRP, BLK))
                entry[i, m] = entry[m, i]
        left = [jnp.broadcast_to(rows_ref[slot, m : m + 1, 0:BLK], (GRP, BLK)) for m in range(GRP)]
        right = [jnp.broadcast_to(rows_ref[slot, m : m + 1, BLK:], (GRP, BLK)) for m in range(GRP)]
        for i in range(GRP):
            root = lax.rsqrt(entry[i, i])
            scale = root * root
            done_ref[first + i : first + i + 1, 0:BLK] = (left[i] * root)[0:1]
            done_ref[first + i : first + i + 1, BLK:] = (right[i] * root)[0:1]
            left[i] = left[i] * scale
            right[i] = right[i] * scale
            scaled = {c: entry[i, c] * scale for c in range(i + 1, GRP)}
            for m in range(GRP):
                if m == i:
                    continue
                weight = entry[m, i]
                left[m] = left[m] - weight * left[i]
                right[m] = right[m] - weight * right[i]
                for c in range(i + 1, GRP):
                    if m > c:
                        continue
                    entry[m, c] = entry[m, c] - weight * scaled[c]
            for m in range(i + 1, GRP):
                for c in range(i + 1, m):
                    entry[m, c] = entry[c, m]
            for c in range(i + 1, GRP):
                entry[i, c] = scaled[c]
        for later in range(g + 1, steps):
            rows = matrix[later]
            total_left, total_right = None, None
            for i in range(GRP):
                weight = jnp.broadcast_to(rows[:, first + i : first + i + 1], (GRP, BLK))
                part_left, part_right = weight * left[i], weight * right[i]
                total_left = part_left if total_left is None else total_left + part_left
                total_right = part_right if total_right is None else total_right + part_right
            matrix[later] = rows - total_left
            inverse[later] = inverse[later] - total_right


def cholesky_kernel(pivot_ref, lower_ref, inverse_ref, work, done, block_inverse, entries, rows):
    order = pivot_ref.shape[0]
    blocks = order // BLK
    work[...] = pivot_ref[...]
    lower_ref[...] = jnp.zeros_like(lower_ref)
    row_id = lax.broadcasted_iota(jnp.int32, (BLK, BLK), 0)
    lane_id = lax.broadcasted_iota(jnp.int32, (BLK, BLK), 1)

    def step(k, carry):
        start = pl.multiple_of(k * BLK, BLK)
        span = pl.ds(start, BLK)
        factor_diagonal(work[span, span], done, entries, rows)
        upper = jnp.where(lane_id >= row_id, done[:, 0:BLK], 0.0)
        lower_ref[span, span] = upper.T
        block_inverse[k] = done[:, BLK:]
        for fixed in range(blocks - 1):
            after = (fixed + 1) * BLK

            @pl.when(k == fixed)
            def _():
                strip = dot_rows(
                    left_parts(done[:, BLK:]), right_rows(work[after - BLK : after, after:])
                )
                column = strip.T
                lower_ref[after:, after - BLK : after] = column
                left = left_parts(column)
                right = right_rows(strip)
                width = order - after
                for top in range(0, width, TILE):
                    high = min(TILE, width - top)
                    work[after + top : after + top + high, after + top :] = work[
                        after + top : after + top + high, after + top :
                    ] - dot_rows(left[top : top + high], right[:, top:])

        return carry

    lax.fori_loop(0, blocks, step, 0)
    for tile in range(order // TILE):
        base = tile * TILE
        first, second = block_inverse[2 * tile], block_inverse[2 * tile + 1]
        corner = lower_ref[base + BLK : base + TILE, base : base + BLK]
        mixed = dot_rows(left_parts(corner), right_rows(first))
        mixed = -dot_rows(left_parts(second), right_rows(mixed))
        inverse_ref[tile, 0:BLK, 0:BLK] = first
        inverse_ref[tile, 0:BLK, BLK:] = jnp.zeros((BLK, BLK), jnp.float32)
        inverse_ref[tile, BLK:, 0:BLK] = mixed
        inverse_ref[tile, BLK:, BLK:] = second


def cholesky(pivot):
    order = pivot.shape[0]
    return pl.pallas_call(
        cholesky_kernel,
        out_shape=(
            jax.ShapeDtypeStruct((order, order), jnp.float32),
            jax.ShapeDtypeStruct((order // TILE, TILE, TILE), jnp.float32),
        ),
        in_specs=[pl.BlockSpec(memory_space=pltpu.VMEM)],
        out_specs=(pl.BlockSpec(memory_space=pltpu.VMEM), pl.BlockSpec(memory_space=pltpu.VMEM)),
        scratch_shapes=[
            pltpu.VMEM((order, order), jnp.float32),
            pltpu.VMEM((BLK, 2 * BLK), jnp.float32),
            pltpu.VMEM((order // BLK, BLK, BLK), jnp.float32),
            pltpu.VMEM((2, GRP, GRP, BLK), jnp.float32),
            pltpu.VMEM((2, GRP, 2 * BLK), jnp.float32),
        ],
        compiler_params=pltpu.CompilerParams(vmem_limit_bytes=40 * 2**20),
        name="cholesky",
    )(pivot)


VMEM = pl.BlockSpec(memory_space=pltpu.VMEM)
SMEM = pl.BlockSpec(memory_space=pltpu.SMEM)
ANY = pl.BlockSpec(memory_space=pl.ANY)
GROUPS = 4
PARAMS = pltpu.CompilerParams(vmem_limit_bytes=48 * 2**20)


def swapped(value, axis, apart):
    mask = 2**apart
    pairs = [(source, source ^ mask) for source in range(lax.axis_size(axis))]
    return lax.ppermute(value, axis, pairs)


def find_tile(map_ref, owner, group, slot, count):
    base = (owner * GROUPS + group) * count
    found = jnp.int32(-1)
    for s in range(count):
        found = jnp.where(map_ref[base + s] == slot, jnp.int32(s), found)
    return found


def column_targets(half, side):
    targets = []
    for part in (side, 1 - side):
        targets.append(2 * part + 1 - half)
        targets += [4 + 3 * (2 * part + half) + i for i in range(3)]
    return targets


def share_place(target, half):
    place = jnp.int32(0)
    for other in column_targets(half, 0):
        earlier = jnp.logical_and((other & 3) == (target & 3), other < target)
        place = place + earlier.astype(jnp.int32)
    return place


def start_tile(live, source, zero, target, sem):
    @pl.when(live)
    def _():
        pltpu.make_async_copy(source, target, sem).start()

    @pl.when(jnp.logical_not(live))
    def _():
        pltpu.make_async_copy(zero, target, sem).start()


def pick_separator_kernel(ids_ref, map_ref, child_ref, entries_ref, pivot_ref, coupling_ref, zero, sems, entry_sems):
    count = child_ref.shape[0]
    leaf, column = ids_ref[0], ids_ref[1]
    width = GROUPS * TILE
    first_entries = pltpu.make_async_copy(entries_ref.at[0], pivot_ref.at[:, pl.ds(width, width // 2)], entry_sems.at[0])
    other_entries = pltpu.make_async_copy(
        entries_ref.at[pl.ds(1, count)], coupling_ref.at[:, :, pl.ds(width, width // 2)], entry_sems.at[1]
    )
    first_entries.start()
    zero[...] = jnp.zeros_like(zero)
    waits = []
    for slot in range(count + 1):
        row = find_tile(map_ref, leaf, column, slot, count)
        for group in range(GROUPS):
            place = find_tile(map_ref, leaf, group, 0, count)
            live = jnp.logical_and(row >= 0, place >= 0)
            source = child_ref.at[
                jnp.maximum(row, 0),
                :,
                pl.ds(pl.multiple_of((jnp.maximum(place, 0) * GROUPS + group) * TILE, TILE), TILE),
            ]
            span = pl.ds(group * TILE, TILE)
            target = pivot_ref.at[:, span] if slot == 0 else coupling_ref.at[slot - 1, :, span]
            sem = sems.at[slot * GROUPS + group]
            start_tile(live, source, zero, target, sem)
            waits.append(pltpu.make_async_copy(zero, target, sem))
    other_entries.start()
    for wait in waits:
        wait.wait()
    first_entries.wait()
    other_entries.wait()


def pick_separator(ids, child_map, child, entries):
    count, _, _ = child.shape
    width = GROUPS * TILE + entries.shape[-1]
    return pl.pallas_call(
        pick_separator_kernel,
        out_shape=(
            jax.ShapeDtypeStruct((TILE, width), child.dtype),
            jax.ShapeDtypeStruct((count, TILE, width), child.dtype),
        ),
        in_specs=[SMEM, SMEM, ANY, ANY],
        out_specs=(ANY, ANY),
        scratch_shapes=[
            pltpu.VMEM((TILE, TILE), child.dtype),
            pltpu.SemaphoreType.DMA(((count + 1) * GROUPS,)),
            pltpu.SemaphoreType.DMA((2,)),
        ],
        compiler_params=pltpu.CompilerParams(vmem_limit_bytes=4 * 2**20),
        name="pick_separator",
    )(ids, child_map, child, entries)


def pick_trailing_kernel(ids_ref, map_ref, next_ref, child_ref, send_ref, keep_ref, zero, sems):
    count = child_ref.shape[0]
    leaf, column = ids_ref[0], ids_ref[1]
    pair = leaf >> 1
    zero[...] = jnp.zeros_like(zero)
    rows = [find_tile(map_ref, leaf, column, slot, count) for slot in range(1, count + 1)]
    waits = []
    for which, (device, out_ref) in enumerate(((leaf ^ 1, send_ref), (leaf, keep_ref))):
        for position, target in enumerate(column_targets(device & 1, (device >> 1) & 1)):
            group = target & 3
            update = find_tile(next_ref, pair, group, target >> 2, count)
            place = find_tile(map_ref, leaf, group, update + 1, count)
            column_live = jnp.logical_and(update >= 0, place >= 0)
            source_span = pl.ds(pl.multiple_of((jnp.maximum(place, 0) * GROUPS + group) * TILE, TILE), TILE)
            for slot, row in enumerate(rows):
                live = jnp.logical_and(column_live, row >= 0)
                source = child_ref.at[jnp.maximum(row, 0), :, source_span]
                goal = out_ref.at[slot, :, pl.ds(position * TILE, TILE)]
                sem = sems.at[(which * 8 + position) * count + slot]
                start_tile(live, source, zero, goal, sem)
                waits.append(pltpu.make_async_copy(zero, goal, sem))
    for wait in waits:
        wait.wait()


def pick_trailing(ids, child_map, next_map, child):
    count = child.shape[0]
    shape = jax.ShapeDtypeStruct((count, TILE, 8 * TILE), child.dtype)
    return pl.pallas_call(
        pick_trailing_kernel,
        out_shape=(shape, shape),
        in_specs=[SMEM, SMEM, SMEM, ANY],
        out_specs=(ANY, ANY),
        scratch_shapes=[pltpu.VMEM((TILE, TILE), child.dtype), pltpu.SemaphoreType.DMA((16 * count,))],
        compiler_params=pltpu.CompilerParams(vmem_limit_bytes=4 * 2**20),
        name="pick_trailing",
    )(ids, child_map, next_map, child)


def solve_blocks(coupling_ref, lower_ref, inverse_ref, panel_ref):
    order = lower_ref.shape[0]
    solved = []
    for k in range(order // TILE):
        span = slice(k * TILE, (k + 1) * TILE)
        rest = coupling_ref[:, span]
        if k:
            left = jnp.concatenate([part[0] for part in solved], axis=1)
            low = jnp.concatenate([part[1] for part in solved], axis=1)
            high_lower, low_lower = halves(lower_ref[span, 0 : k * TILE])
            rest = rest - dot_lanes(
                jnp.concatenate([left, low, left], axis=1),
                jnp.concatenate([high_lower, high_lower, low_lower], axis=1),
            )
        block = dot_lanes(left_parts(rest), right_lanes(inverse_ref[k]))
        panel_ref[:, span] = block
        solved.append(halves(block))
    return jnp.concatenate([part[0] for part in solved], axis=1)


def write_factor(column, offset, lower_ref, panel, factor_ref):
    width = factor_ref.shape[-1]
    rows = pl.ds(pl.multiple_of(column * TILE, TILE), TILE)
    span = pl.ds(pl.multiple_of(offset * width, width), width)
    factor_ref[0] = lower_ref[rows, span]
    for s in range(factor_ref.shape[0] - 1):
        factor_ref[s + 1] = panel[s * TILE : (s + 1) * TILE, span]


def panel_one_kernel(
    ids_ref, mask_ref, next_ref, mine_ref, peer_ref, lower_ref, inverse_ref, factor_ref, round_ref, share_ref, coupling, panel
):
    leaf, column = ids_ref[0], ids_ref[1]
    half, pair = leaf & 1, leaf >> 1
    count = mine_ref.shape[0]
    order = lower_ref.shape[0]
    for s in range(count):
        for tile in range(order // TILE):
            span = slice(tile * TILE, (tile + 1) * TILE)
            where = order + (tile % 2) * TILE
            weight = mask_ref[((pair * count + s) * GROUPS + column) * GROUPS + tile].astype(jnp.float32)
            mine = mine_ref[s, :, where : where + TILE].astype(jnp.float32)
            peer = peer_ref[s, :, where : where + TILE].astype(jnp.float32)
            own_first = half == tile // 2
            entry = jnp.where(own_first, mine, peer)
            coupling[s * TILE : (s + 1) * TILE, span] = (
                mine_ref[s, :, span].astype(jnp.float32) + peer_ref[s, :, span].astype(jnp.float32) + entry * weight
            )
    rounded = solve_blocks(coupling, lower_ref, inverse_ref, panel)
    for s in range(count):
        round_ref[s] = rounded[s * TILE : (s + 1) * TILE]
    write_factor(column, half, lower_ref, panel, factor_ref)
    for a in range(2):
        slot = jnp.int32(0)
        for target in column_targets(half, 0):
            hit = jnp.logical_and((target & 3) == column, share_place(target, half) == a)
            slot = jnp.where(hit, target >> 2, slot)
        tile = find_tile(next_ref, pair, column, slot, count)
        share_ref[a] = round_ref[jnp.maximum(tile, 0)]


def panel_one(ids, mask, next_map, mine, peer, lower, inverse):
    count = mine.shape[0]
    order = lower.shape[0]
    return pl.pallas_call(
        panel_one_kernel,
        out_shape=(
            jax.ShapeDtypeStruct((count + 1, TILE, order // 2), jnp.float32),
            jax.ShapeDtypeStruct((count, TILE, order), jnp.bfloat16),
            jax.ShapeDtypeStruct((2, TILE, order), jnp.bfloat16),
        ),
        in_specs=[SMEM, SMEM, SMEM, VMEM, VMEM, VMEM, VMEM],
        out_specs=(VMEM, VMEM, VMEM),
        scratch_shapes=[
            pltpu.VMEM((count * TILE, order), jnp.float32),
            pltpu.VMEM((count * TILE, order), jnp.float32),
        ],
        compiler_params=PARAMS,
        name="panel_one",
    )(ids, mask, next_map, mine, peer, lower, inverse)


def panel_two_kernel(ids_ref, own_ref, x_ref, z_ref, both_ref, lower_ref, inverse_ref, factor_ref, round_ref, share_ref, coupling, panel):
    leaf, column = ids_ref[0], ids_ref[1]
    half, side = leaf & 1, (leaf >> 1) & 1
    quarter = leaf & 3
    count = round_ref.shape[0]
    for place, ref in (
        (2 * side + 1 - half, own_ref),
        (2 * side + half, x_ref),
        (2 * (1 - side) + 1 - half, z_ref),
        (2 * (1 - side) + half, both_ref),
    ):
        coupling[:, pl.ds(pl.multiple_of(place * TILE, TILE), TILE)] = ref[...]
    rounded = solve_blocks(coupling, lower_ref, inverse_ref, panel)
    for s in range(count):
        round_ref[s] = rounded[s * TILE : (s + 1) * TILE]
    write_factor(column, quarter, lower_ref, panel, factor_ref)
    chosen = jnp.int32(0)
    for i in range(3):
        tile = 3 * quarter + i
        chosen = jnp.where((tile & 3) == column, tile >> 2, chosen)
    share_ref[...] = round_ref[chosen]


def panel_two(ids, parts, lower, inverse):
    rows = parts[0].shape[0]
    count = rows // TILE
    order = lower.shape[0]
    return pl.pallas_call(
        panel_two_kernel,
        out_shape=(
            jax.ShapeDtypeStruct((count + 1, TILE, order // 4), jnp.float32),
            jax.ShapeDtypeStruct((count, TILE, order), jnp.bfloat16),
            jax.ShapeDtypeStruct((TILE, order), jnp.bfloat16),
        ),
        in_specs=[SMEM] + [VMEM] * 6,
        out_specs=(VMEM, VMEM, VMEM),
        scratch_shapes=[pltpu.VMEM((rows, order), jnp.float32), pltpu.VMEM((rows, order), jnp.float32)],
        compiler_params=PARAMS,
        name="panel_two",
    )(ids, *parts, lower, inverse)


def update_one_kernel(
    ids_ref, next_ref, keep_ref, peer_ref, round_ref, shared_ref,
    far_pivot_ref, far_coupling_ref, far_trailing_ref, near_pivot_ref, near_coupling_ref, near_trailing_ref, tiles
):
    leaf, column = ids_ref[0], ids_ref[1]
    half, side, pair = leaf & 1, (leaf >> 1) & 1, leaf >> 1
    count = keep_ref.shape[0]
    step = pl.program_id(0)
    group = 1 - step // 4
    inner = step % 4
    targets = column_targets(half, side)
    target = targets[0]
    for position in range(1, 8):
        target = jnp.where(group * 4 + inner == position, targets[position], target)
    live = find_tile(next_ref, pair, target & 3, target >> 2, count) >= 0
    shared = shared_ref[(target & 3) * 2 + share_place(target, half)]
    for s in range(count):
        value = keep_ref[s].astype(jnp.float32) + peer_ref[s].astype(jnp.float32) - dot_lanes(round_ref[s], shared)
        tiles[s] = jnp.where(live, value, 0.0).astype(jnp.bfloat16)
    tiles[count] = jnp.zeros_like(tiles[count])

    def placed(slot):
        row = find_tile(next_ref, pair, column, slot, count)
        return tiles[jnp.where(row < 0, count, row)]

    for which, pivot_ref, coupling_ref, trailing_ref in (
        (1, far_pivot_ref, far_coupling_ref, far_trailing_ref),
        (0, near_pivot_ref, near_coupling_ref, near_trailing_ref),
    ):

        @pl.when(jnp.logical_and(group == which, inner == 0))
        def _():
            pivot_ref[...] = placed(0)
            for slot in range(1, count + 1):
                coupling_ref[slot - 1] = placed(slot)

        @pl.when(jnp.logical_and(group == which, inner > 0))
        def _():
            for slot in range(1, count + 1):
                trailing_ref[slot - 1] = placed(slot)


def update_one(ids, next_map, keep, peer, rounded, shared):
    count, _, order = rounded.shape
    column_of = lambda step: (0, 0, (1 - step // 4) * 4 + step % 4)
    far_of = lambda step: (0, 0, jnp.clip(step - 1, 0, 2))
    near_of = lambda step: (0, 0, jnp.clip(step - 5, 0, 2))
    fixed2 = lambda step: (0, 0)
    fixed3 = lambda step: (0, 0, 0)
    tile_spec = pl.BlockSpec((TILE, TILE), fixed2)
    coupling_spec = pl.BlockSpec((count, TILE, TILE), fixed3)
    shapes = (
        jax.ShapeDtypeStruct((TILE, TILE), jnp.bfloat16),
        jax.ShapeDtypeStruct((count, TILE, TILE), jnp.bfloat16),
        jax.ShapeDtypeStruct((count, TILE, 3 * TILE), jnp.bfloat16),
    )
    return pl.pallas_call(
        update_one_kernel,
        grid=(8,),
        out_shape=shapes + shapes,
        in_specs=[
            SMEM,
            SMEM,
            pl.BlockSpec((count, TILE, TILE), column_of),
            pl.BlockSpec((count, TILE, TILE), column_of),
            VMEM,
            VMEM,
        ],
        out_specs=(
            tile_spec, coupling_spec, pl.BlockSpec((count, TILE, TILE), far_of),
            tile_spec, coupling_spec, pl.BlockSpec((count, TILE, TILE), near_of),
        ),
        scratch_shapes=[pltpu.VMEM((count + 1, TILE, TILE), jnp.bfloat16)],
        compiler_params=PARAMS,
        name="update_one",
    )(ids, next_map, keep, peer, rounded, shared)


def update_two_kernel(ids_ref, near_ref, far_ref, round_ref, shared_ref, out_ref):
    quarter = ids_ref[0] & 3
    for i in range(3):
        shared = shared_ref[(3 * quarter + i) & 3]
        span = slice(i * TILE, (i + 1) * TILE)
        for s in range(near_ref.shape[0]):
            total = near_ref[s, :, span].astype(jnp.float32) + far_ref[s, :, span].astype(jnp.float32)
            out_ref[s, :, span] = (total - dot_lanes(round_ref[s], shared)).astype(jnp.bfloat16)


def update_two(ids, near, far, rounded, shared):
    return pl.pallas_call(
        update_two_kernel,
        out_shape=jax.ShapeDtypeStruct(near.shape, jnp.bfloat16),
        in_specs=[SMEM, VMEM, VMEM, VMEM, VMEM],
        out_specs=VMEM,
        compiler_params=PARAMS,
        name="update_two",
    )(ids, near, far, rounded, shared)


def in_order(mine, other, mine_first):
    return jnp.where(
        mine_first, jnp.concatenate([mine, other], axis=-1), jnp.concatenate([other, mine], axis=-1)
    )


def body(child_update, sep_one, sep_two, map_one, map_two, mask_one, mask_two):
    column = lax.axis_index("front")
    leaf = lax.axis_index("leaf")
    half, side, pair, quad = leaf & 1, (leaf >> 1) & 1, leaf >> 1, leaf >> 2
    ids = jnp.stack([leaf, column]).astype(jnp.int32)
    child = child_update[0, 0, 0]
    entries_one = sep_one[0, 0, 0]
    entries_two = sep_two[0, 0, 0]
    count = child.shape[0]
    maps_one = map_one.reshape(-1)
    maps_two = map_two.reshape(-1)

    pivot_mine, coupling_mine = pick_separator(ids, maps_one, child, entries_one)
    pivot_peer = swapped(pivot_mine, "leaf", 0)
    coupling_peer = swapped(coupling_mine, "leaf", 0)
    send, keep = pick_trailing(ids, maps_one, maps_two, child)
    trailing_peer = swapped(send, "leaf", 0)
    entries_near = swapped(entries_two, "leaf", 0)

    wide = pivot_mine.astype(jnp.float32)
    wide_peer = pivot_peer.astype(jnp.float32)
    pivot_rows = wide[:, :S] + wide_peer[:, :S] + in_order(wide[:, S:], wide_peer[:, S:], half == 0)
    pivot = lax.all_gather(pivot_rows, "front", axis=0, tiled=True)
    lower, inverse = cholesky(pivot)
    factor_one, rounded, share = panel_one(
        ids, mask_one.reshape(-1), maps_two, coupling_mine, coupling_peer, lower, inverse
    )
    shared = lax.all_gather(share, "front", axis=0, tiled=True)
    far_pivot, far_coupling, far_trailing, near_pivot, near_coupling, near_trailing = update_one(
        ids, maps_two, keep, trailing_peer, rounded, shared
    )

    pivot_far = swapped(far_pivot, "leaf", 1)
    coupling_far = swapped(far_coupling, "leaf", 1)
    trailing_far = swapped(far_trailing, "leaf", 1)
    pivot_tile = (
        near_pivot.astype(jnp.float32) + pivot_far.astype(jnp.float32) + entries_near[0].astype(jnp.float32)
    )
    pivot_pair = in_order(pivot_tile, swapped(pivot_tile, "leaf", 0), half == 1)
    pivot_rows = in_order(pivot_pair, swapped(pivot_pair, "leaf", 1), side == 0)
    pivot = lax.all_gather(pivot_rows, "front", axis=0, tiled=True)
    mask_second = lax.dynamic_index_in_dim(mask_two, quad, 0, keepdims=False).reshape(count, GROUPS, -1)
    mask_second = lax.dynamic_index_in_dim(mask_second, column, 1, keepdims=False)
    mask_second = lax.dynamic_index_in_dim(mask_second, 2 * side + 1 - half, 1, keepdims=False)
    coupling = (
        near_coupling.astype(jnp.float32)
        + coupling_far.astype(jnp.float32)
        + entries_near[1:].astype(jnp.float32) * mask_second.astype(jnp.float32)[:, None, None]
    ).reshape(count * TILE, TILE)
    coupling_x = swapped(coupling, "leaf", 0)
    coupling_z, coupling_xz = swapped((coupling, coupling_x), "leaf", 1)
    lower, inverse = cholesky(pivot)
    factor_two, rounded, share = panel_two(
        ids, (coupling, coupling_x, coupling_z, coupling_xz), lower, inverse
    )
    shared = lax.all_gather(share[None], "front", axis=0, tiled=True)
    update = update_two(ids, near_trailing, trailing_far, rounded, shared)
    return (factor_one[None, None, None], factor_two[None, None, None], update[None, None, None])


def solution(mesh):
    split = P("leaf", "front", None, None, None, None)
    return jax.shard_map(
        body,
        mesh=mesh,
        in_specs=(split, split, split, P(), P(), P(), P()),
        out_specs=(split, split, split),
        check_vma=False,
    )
```

```python
import functools

import jax
import jax.numpy as jnp
from jax import lax
from jax.experimental import pallas as pl
from jax.experimental.pallas import tpu as pltpu
from jax.sharding import PartitionSpec as P

VMEM = pl.BlockSpec(memory_space=pltpu.VMEM)
SMEM = pl.BlockSpec(memory_space=pltpu.SMEM)
ANY = pl.BlockSpec(memory_space=pl.ANY)
GROUPS = 4
PARAMS = pltpu.CompilerParams(vmem_limit_bytes=32 * 2**20)
BLK = 128
GRP = 8
TILE = 256
NT = (((1,), (1,)), ((), ()))


def halves(x):
    high = x.astype(jnp.bfloat16)
    low = (x - high.astype(jnp.float32)).astype(jnp.bfloat16)
    return high, low


def left_parts(x):
    high, low = halves(x)
    return jnp.concatenate([high, low, high], axis=1)


def right_rows(x):
    high, low = halves(x)
    return jnp.concatenate([high, high, low], axis=0)


def right_lanes(x):
    high, low = halves(x)
    return jnp.concatenate([high, high, low], axis=1)


def dot_rows(left, right):
    return jnp.dot(left, right, preferred_element_type=jnp.float32)


def dot_lanes(left, right):
    return lax.dot_general(left, right, NT, preferred_element_type=jnp.float32)


def spread_row(ref, index):
    return jnp.broadcast_to(ref[index], (GRP, BLK))


def factor_diagonal(block, done_ref, pivot_ref, rows_ref):
    steps = BLK // GRP
    row_id = lax.broadcasted_iota(jnp.int32, (GRP, BLK), 0)
    lane_id = lax.broadcasted_iota(jnp.int32, (GRP, BLK), 1)
    matrix = [block[GRP * g : GRP * (g + 1), :] for g in range(steps)]
    inverse = [jnp.where(lane_id == row_id + GRP * g, 1.0, 0.0).astype(jnp.float32) for g in range(steps)]
    for g in range(steps):
        first = GRP * g
        slot = g % 2
        current = matrix[g]
        rows_ref[slot, :, 0:BLK] = current
        rows_ref[slot, :, BLK:] = inverse[g]
        for i in range(GRP):
            pivot_ref[slot, i] = jnp.broadcast_to(current[:, first + i : first + i + 1], (GRP, BLK))
        entry = {}
        for m in range(GRP):
            for i in range(m + 1):
                entry[m, i] = jnp.broadcast_to(pivot_ref[slot, i, m : m + 1, :], (GRP, BLK))
                entry[i, m] = entry[m, i]
        left = [jnp.broadcast_to(rows_ref[slot, m : m + 1, 0:BLK], (GRP, BLK)) for m in range(GRP)]
        right = [jnp.broadcast_to(rows_ref[slot, m : m + 1, BLK:], (GRP, BLK)) for m in range(GRP)]
        for i in range(GRP):
            root = lax.rsqrt(entry[i, i])
            scale = root * root
            done_ref[first + i : first + i + 1, 0:BLK] = (left[i] * root)[0:1]
            done_ref[first + i : first + i + 1, BLK:] = (right[i] * root)[0:1]
            left[i] = left[i] * scale
            right[i] = right[i] * scale
            scaled = {c: entry[i, c] * scale for c in range(i + 1, GRP)}
            for m in range(GRP):
                if m == i:
                    continue
                weight = entry[m, i]
                left[m] = left[m] - weight * left[i]
                right[m] = right[m] - weight * right[i]
                for c in range(i + 1, GRP):
                    if m > c:
                        continue
                    entry[m, c] = entry[m, c] - weight * scaled[c]
            for m in range(i + 1, GRP):
                for c in range(i + 1, m):
                    entry[m, c] = entry[c, m]
            for c in range(i + 1, GRP):
                entry[i, c] = scaled[c]
        for later in range(g + 1, steps):
            rows = matrix[later]
            total_left, total_right = None, None
            for i in range(GRP):
                weight = jnp.broadcast_to(rows[:, first + i : first + i + 1], (GRP, BLK))
                part_left, part_right = weight * left[i], weight * right[i]
                total_left = part_left if total_left is None else total_left + part_left
                total_right = part_right if total_right is None else total_right + part_right
            matrix[later] = rows - total_left
            inverse[later] = inverse[later] - total_right


def fill_one(ids_ref, packs, work):
    leaf, column = ids_ref[0], ids_ref[1]
    half = leaf & 1
    order = work.shape[1]
    own, core, y, y_core, x, x_core = packs[:6]
    for apart, mine, peers in (
        (0, own, (x,)),
        (1, core, (x_core,)),
        (2, y, packs[6:8]),
        (3, y_core, packs[8:10]),
    ):
        base = (column ^ apart) * TILE
        height = TILE // len(peers)
        for part, peer in enumerate(peers):
            rows = pl.ds(pl.multiple_of(base + part * height, height), height)
            piece = slice(part * height, (part + 1) * height)
            work[rows, :] = mine[piece, 0:order].astype(jnp.float32) + peer[:, 0:order].astype(jnp.float32)
            for place, ref, span in ((half, mine, piece), (1 - half, peer, slice(None))):
                columns = pl.ds(pl.multiple_of(place * (order // 2), order // 2), order // 2)
                work[rows, columns] = work[rows, columns] + ref[span, order:].astype(jnp.float32)


def fill_two(ids_ref, packs, work):
    leaf, column = ids_ref[0], ids_ref[1]
    half, side = leaf & 1, (leaf >> 1) & 1
    own, core, y, y_core, x, x_core = packs[:6]
    for apart, mine, peers in (
        (0, own, (x,)),
        (1, core, (x_core,)),
        (2, y, packs[6:8]),
        (3, y_core, packs[8:10]),
    ):
        base = (column ^ apart) * TILE
        for refs, last in (((mine,), 1 - half), (peers, half)):
            height = TILE // len(refs)
            for part, ref in enumerate(refs):
                rows = pl.ds(pl.multiple_of(base + part * height, height), height)
                for position, place in ((0, 2 * side + last), (1, 2 * (1 - side) + last)):
                    columns = pl.ds(pl.multiple_of(place * TILE, TILE), TILE)
                    work[rows, columns] = ref[:, position * TILE : (position + 1) * TILE]


def cholesky_kernel(fill, ids_ref, *refs):
    packs = refs[:10]
    lower_ref, inverse_ref, work, done, block_inverse, entries, rows = refs[10:]
    order = work.shape[0]
    blocks = order // BLK
    fill(ids_ref, packs, work)
    lower_ref[...] = jnp.zeros_like(lower_ref)
    row_id = lax.broadcasted_iota(jnp.int32, (BLK, BLK), 0)
    lane_id = lax.broadcasted_iota(jnp.int32, (BLK, BLK), 1)

    def step(k, carry):
        start = pl.multiple_of(k * BLK, BLK)
        span = pl.ds(start, BLK)
        factor_diagonal(work[span, span], done, entries, rows)
        upper = jnp.where(lane_id >= row_id, done[:, 0:BLK], 0.0)
        lower_ref[span, span] = upper.T
        block_inverse[k] = done[:, BLK:]
        for fixed in range(blocks - 1):
            after = (fixed + 1) * BLK

            @pl.when(k == fixed)
            def _():
                strip = dot_rows(
                    left_parts(done[:, BLK:]), right_rows(work[after - BLK : after, after:])
                )
                column = strip.T
                lower_ref[after:, after - BLK : after] = column
                left = left_parts(column)
                right = right_rows(strip)
                width = order - after
                for top in range(0, width, TILE):
                    high = min(TILE, width - top)
                    work[after + top : after + top + high, after + top :] = work[
                        after + top : after + top + high, after + top :
                    ] - dot_rows(left[top : top + high], right[:, top:])

        return carry

    lax.fori_loop(0, blocks, step, 0)
    for tile in range(order // TILE):
        base = tile * TILE
        first, second = block_inverse[2 * tile], block_inverse[2 * tile + 1]
        corner = lower_ref[base + BLK : base + TILE, base : base + BLK]
        mixed = dot_rows(left_parts(corner), right_rows(first))
        mixed = -dot_rows(left_parts(second), right_rows(mixed))
        inverse_ref[tile, 0:BLK, 0:BLK] = first
        inverse_ref[tile, 0:BLK, BLK:] = jnp.zeros((BLK, BLK), jnp.float32)
        inverse_ref[tile, BLK:, 0:BLK] = mixed
        inverse_ref[tile, BLK:, BLK:] = second


def cholesky(ids, packs, fill, order):
    return pl.pallas_call(
        functools.partial(cholesky_kernel, fill),
        out_shape=(
            jax.ShapeDtypeStruct((order, order), jnp.float32),
            jax.ShapeDtypeStruct((order // TILE, TILE, TILE), jnp.float32),
        ),
        in_specs=[SMEM] + [VMEM] * len(packs),
        out_specs=(VMEM, VMEM),
        scratch_shapes=[
            pltpu.VMEM((order, order), jnp.float32),
            pltpu.VMEM((BLK, 2 * BLK), jnp.float32),
            pltpu.VMEM((order // BLK, BLK, BLK), jnp.float32),
            pltpu.VMEM((2, GRP, GRP, BLK), jnp.float32),
            pltpu.VMEM((2, GRP, 2 * BLK), jnp.float32),
        ],
        compiler_params=pltpu.CompilerParams(vmem_limit_bytes=32 * 2**20),
        cost_estimate=pl.CostEstimate(flops=4 * 10**10, bytes_accessed=10**8, transcendentals=0),
        name="cholesky",
    )(ids, *packs)


def swapped(value, axis, apart):
    mask = 2**apart
    pairs = [(source, source ^ mask) for source in range(lax.axis_size(axis))]
    return lax.ppermute(value, axis, pairs)


def find_tile(map_ref, owner, group, slot, count):
    base = (owner * GROUPS + group) * count
    found = jnp.int32(-1)
    for s in range(count):
        found = jnp.where(map_ref[base + s] == slot, jnp.int32(s), found)
    return found


def column_targets(half, side):
    targets = []
    for part in (side, 1 - side):
        targets.append(2 * part + 1 - half)
        targets += [4 + 3 * (2 * part + half) + i for i in range(3)]
    return targets


def share_place(target, half):
    place = jnp.int32(0)
    for other in column_targets(half, 0):
        earlier = jnp.logical_and((other & 3) == (target & 3), other < target)
        place = place + earlier.astype(jnp.int32)
    return place


def start_tile(live, source, zero, target, sem):
    @pl.when(live)
    def _():
        pltpu.make_async_copy(source, target, sem).start()

    @pl.when(jnp.logical_not(live))
    def _():
        pltpu.make_async_copy(zero, target, sem).start()


def pick_separator_kernel(ids_ref, map_ref, child_ref, entries_ref, pivot_ref, coupling_ref, zero, sems, entry_sems):
    count = child_ref.shape[0]
    leaf, column = ids_ref[0], ids_ref[1]
    width = GROUPS * TILE
    first_entries = pltpu.make_async_copy(entries_ref.at[0], pivot_ref.at[:, pl.ds(width, width // 2)], entry_sems.at[0])
    other_entries = pltpu.make_async_copy(
        entries_ref.at[pl.ds(1, count)], coupling_ref.at[:, :, pl.ds(width, width // 2)], entry_sems.at[1]
    )
    first_entries.start()
    zero[...] = jnp.zeros_like(zero)
    waits = []
    for slot in range(count + 1):
        row = find_tile(map_ref, leaf, column, slot, count)
        for group in range(GROUPS):
            place = find_tile(map_ref, leaf, group, 0, count)
            live = jnp.logical_and(row >= 0, place >= 0)
            source = child_ref.at[
                jnp.maximum(row, 0),
                :,
                pl.ds(pl.multiple_of((jnp.maximum(place, 0) * GROUPS + group) * TILE, TILE), TILE),
            ]
            span = pl.ds(group * TILE, TILE)
            target = pivot_ref.at[:, span] if slot == 0 else coupling_ref.at[slot - 1, :, span]
            sem = sems.at[slot * GROUPS + group]
            start_tile(live, source, zero, target, sem)
            waits.append(pltpu.make_async_copy(zero, target, sem))
    other_entries.start()
    for wait in waits:
        wait.wait()
    first_entries.wait()
    other_entries.wait()


def pick_separator(ids, child_map, child, entries):
    count, _, _ = child.shape
    width = GROUPS * TILE + entries.shape[-1]
    return pl.pallas_call(
        pick_separator_kernel,
        out_shape=(
            jax.ShapeDtypeStruct((TILE, width), child.dtype),
            jax.ShapeDtypeStruct((count, TILE, width), child.dtype),
        ),
        in_specs=[SMEM, SMEM, ANY, ANY],
        out_specs=(ANY, ANY),
        scratch_shapes=[
            pltpu.VMEM((TILE, TILE), child.dtype),
            pltpu.SemaphoreType.DMA(((count + 1) * GROUPS,)),
            pltpu.SemaphoreType.DMA((2,)),
        ],
        compiler_params=pltpu.CompilerParams(vmem_limit_bytes=56 * 2**20),
        name="pick_separator",
    )(ids, child_map, child, entries)


def pick_trailing_kernel(ids_ref, map_ref, next_ref, child_ref, *refs):
    outs, (zero, sems) = refs[:6], refs[6:]
    count = child_ref.shape[0]
    leaf, column = ids_ref[0], ids_ref[1]
    pair = leaf >> 1
    zero[...] = jnp.zeros_like(zero)
    rows = [find_tile(map_ref, leaf, column, slot, count) for slot in range(1, count + 1)]
    waits = []
    for which, device in enumerate((leaf ^ 1, leaf)):
        for position, target in enumerate(column_targets(device & 1, (device >> 1) & 1)):
            group = target & 3
            update = find_tile(next_ref, pair, group, target >> 2, count)
            place = find_tile(map_ref, leaf, group, update + 1, count)
            column_live = jnp.logical_and(update >= 0, place >= 0)
            source_span = pl.ds(pl.multiple_of((jnp.maximum(place, 0) * GROUPS + group) * TILE, TILE), TILE)
            for slot, row in enumerate(rows):
                live = jnp.logical_and(column_live, row >= 0)
                source = child_ref.at[jnp.maximum(row, 0), :, source_span]
                if position % 4 == 0:
                    goal = outs[3 * which].at[slot, :, pl.ds(position // 4 * TILE, TILE)]
                else:
                    goal = outs[3 * which + 1 + position // 4].at[slot, :, pl.ds((position % 4 - 1) * TILE, TILE)]
                sem = sems.at[(which * 8 + position) * count + slot]
                start_tile(live, source, zero, goal, sem)
                waits.append(pltpu.make_async_copy(zero, goal, sem))
    for wait in waits:
        wait.wait()


def pick_trailing(ids, child_map, next_map, child):
    count = child.shape[0]
    shapes = tuple(jax.ShapeDtypeStruct((count, TILE, width * TILE), child.dtype) for width in (2, 3, 3))
    return pl.pallas_call(
        pick_trailing_kernel,
        out_shape=shapes + shapes,
        in_specs=[SMEM, SMEM, SMEM, ANY],
        out_specs=(ANY,) * 6,
        scratch_shapes=[pltpu.VMEM((TILE, TILE), child.dtype), pltpu.SemaphoreType.DMA((16 * count,))],
        compiler_params=pltpu.CompilerParams(vmem_limit_bytes=56 * 2**20),
        name="pick_trailing",
    )(ids, child_map, next_map, child)


def solve_blocks(coupling_ref, lower_ref, inverse_ref, panel_ref):
    order = lower_ref.shape[0]
    solved = []
    for k in range(order // TILE):
        span = slice(k * TILE, (k + 1) * TILE)
        rest = coupling_ref[:, span]
        if k:
            left = jnp.concatenate([part[0] for part in solved], axis=1)
            low = jnp.concatenate([part[1] for part in solved], axis=1)
            high_lower, low_lower = halves(lower_ref[span, 0 : k * TILE])
            rest = rest - dot_lanes(
                jnp.concatenate([left, low, left], axis=1),
                jnp.concatenate([high_lower, high_lower, low_lower], axis=1),
            )
        block = dot_lanes(left_parts(rest), right_lanes(inverse_ref[k]))
        panel_ref[:, span] = block
        solved.append(halves(block))
    return jnp.concatenate([part[0] for part in solved], axis=1)


def write_factor(column, offset, lower_ref, panel, factor_ref):
    width = factor_ref.shape[-1]
    rows = pl.ds(pl.multiple_of(column * TILE, TILE), TILE)
    span = pl.ds(pl.multiple_of(offset * width, width), width)
    factor_ref[0] = lower_ref[rows, span]
    for s in range(factor_ref.shape[0] - 1):
        factor_ref[s + 1] = panel[s * TILE : (s + 1) * TILE, span]


def panel_one_kernel(
    ids_ref, mask_ref, next_ref, mine_ref, peer_ref, lower_ref, inverse_ref, factor_ref, round_ref, share_ref, coupling, panel
):
    leaf, column = ids_ref[0], ids_ref[1]
    half, pair = leaf & 1, leaf >> 1
    count = mine_ref.shape[0]
    order = lower_ref.shape[0]
    for s in range(count):
        for tile in range(order // TILE):
            span = slice(tile * TILE, (tile + 1) * TILE)
            where = order + (tile % 2) * TILE
            weight = mask_ref[((pair * count + s) * GROUPS + column) * GROUPS + tile].astype(jnp.float32)
            mine = mine_ref[s, :, where : where + TILE].astype(jnp.float32)
            peer = peer_ref[s, :, where : where + TILE].astype(jnp.float32)
            own_first = half == tile // 2
            entry = jnp.where(own_first, mine, peer)
            coupling[s * TILE : (s + 1) * TILE, span] = (
                mine_ref[s, :, span].astype(jnp.float32) + peer_ref[s, :, span].astype(jnp.float32) + entry * weight
            )
    rounded = solve_blocks(coupling, lower_ref, inverse_ref, panel)
    for s in range(count):
        round_ref[s] = rounded[s * TILE : (s + 1) * TILE]
    write_factor(column, half, lower_ref, panel, factor_ref)
    for a in range(2):
        slot = jnp.int32(0)
        for target in column_targets(half, 0):
            hit = jnp.logical_and((target & 3) == column, share_place(target, half) == a)
            slot = jnp.where(hit, target >> 2, slot)
        tile = find_tile(next_ref, pair, column, slot, count)
        share_ref[a] = round_ref[jnp.maximum(tile, 0)]


def panel_one(ids, mask, next_map, mine, peer, lower, inverse):
    count = mine.shape[0]
    order = lower.shape[0]
    return pl.pallas_call(
        panel_one_kernel,
        out_shape=(
            jax.ShapeDtypeStruct((count + 1, TILE, order // 2), jnp.float32),
            jax.ShapeDtypeStruct((count, TILE, order), jnp.bfloat16),
            jax.ShapeDtypeStruct((2, TILE, order), jnp.bfloat16),
        ),
        in_specs=[SMEM, SMEM, SMEM, VMEM, VMEM, VMEM, VMEM],
        out_specs=(VMEM, VMEM, VMEM),
        scratch_shapes=[
            pltpu.VMEM((count * TILE, order), jnp.float32),
            pltpu.VMEM((count * TILE, order), jnp.float32),
        ],
        compiler_params=PARAMS,
        cost_estimate=pl.CostEstimate(flops=10**10, bytes_accessed=2 * 10**7, transcendentals=0),
        name="panel_one",
    )(ids, mask, next_map, mine, peer, lower, inverse)


def panel_two_kernel(ids_ref, own_ref, x_ref, z_ref, both_ref, lower_ref, inverse_ref, factor_ref, round_ref, share_ref, coupling, panel):
    leaf, column = ids_ref[0], ids_ref[1]
    half, side = leaf & 1, (leaf >> 1) & 1
    quarter = leaf & 3
    count = round_ref.shape[0]
    for place, ref in (
        (2 * side + 1 - half, own_ref),
        (2 * side + half, x_ref),
        (2 * (1 - side) + 1 - half, z_ref),
        (2 * (1 - side) + half, both_ref),
    ):
        coupling[:, pl.ds(pl.multiple_of(place * TILE, TILE), TILE)] = ref[...]
    rounded = solve_blocks(coupling, lower_ref, inverse_ref, panel)
    for s in range(count):
        round_ref[s] = rounded[s * TILE : (s + 1) * TILE]
    write_factor(column, quarter, lower_ref, panel, factor_ref)
    chosen = jnp.int32(0)
    for i in range(3):
        tile = 3 * quarter + i
        chosen = jnp.where((tile & 3) == column, tile >> 2, chosen)
    share_ref[...] = round_ref[chosen]


def panel_two(ids, parts, lower, inverse):
    rows = parts[0].shape[0]
    count = rows // TILE
    order = lower.shape[0]
    return pl.pallas_call(
        panel_two_kernel,
        out_shape=(
            jax.ShapeDtypeStruct((count + 1, TILE, order // 4), jnp.float32),
            jax.ShapeDtypeStruct((count, TILE, order), jnp.bfloat16),
            jax.ShapeDtypeStruct((TILE, order), jnp.bfloat16),
        ),
        in_specs=[SMEM] + [VMEM] * 6,
        out_specs=(VMEM, VMEM, VMEM),
        scratch_shapes=[pltpu.VMEM((rows, order), jnp.float32), pltpu.VMEM((rows, order), jnp.float32)],
        compiler_params=PARAMS,
        cost_estimate=pl.CostEstimate(flops=10**10, bytes_accessed=2 * 10**7, transcendentals=0),
        name="panel_two",
    )(ids, *parts, lower, inverse)


def start_shared(ids_ref, positions, shared_ref, taken, sems):
    leaf = ids_ref[0]
    half, side = leaf & 1, (leaf >> 1) & 1
    targets = column_targets(half, side)
    copies = []
    for i, position in enumerate(positions):
        target = targets[position]
        source = shared_ref.at[(target & 3) * 2 + share_place(target, half)]
        copies.append(pltpu.make_async_copy(source, taken.at[i], sems.at[i]))
        copies[-1].start()
    return copies


def update_columns(ids_ref, next_ref, positions, copies, keep_ref, peer_ref, round_ref, taken, tiles, write):
    leaf, column = ids_ref[0], ids_ref[1]
    half, side, pair = leaf & 1, (leaf >> 1) & 1, leaf >> 1
    count = keep_ref.shape[0]
    targets = column_targets(half, side)
    rows = [find_tile(next_ref, pair, column, slot, count) for slot in range(count + 1)]
    tiles[:, count] = jnp.zeros_like(tiles[:, count])
    for i, position in enumerate(positions):
        target = targets[position]
        live = find_tile(next_ref, pair, target & 3, target >> 2, count) >= 0
        span = slice(i * TILE, (i + 1) * TILE)
        copies[i].wait()
        for s in range(count):
            value = keep_ref[s, :, span].astype(jnp.float32) + peer_ref[s, :, span].astype(jnp.float32)
            value = value - dot_lanes(round_ref[s], taken[i])
            tiles[i, s] = jnp.where(live, value, 0.0).astype(jnp.bfloat16)
        for slot, row in enumerate(rows):
            write(i, slot, lambda row=row: tiles[i, jnp.where(row < 0, count, row)])


def update_separator_kernel(
    ids_ref, next_ref, keep_ref, peer_ref, round_ref, shared_ref, pivot_ref, near_ref, far_ref, taken, tiles, sems
):
    def write(i, slot, tile):
        if slot == 0:
            pivot_ref[:, i * TILE : (i + 1) * TILE] = tile()
        else:
            (near_ref, far_ref)[i][slot - 1] = tile()

    copies = start_shared(ids_ref, (0, 4), shared_ref, taken, sems)
    update_columns(ids_ref, next_ref, (0, 4), copies, keep_ref, peer_ref, round_ref, taken, tiles, write)


def update_separator(ids, next_map, keep, peer, rounded, shared):
    count, _, order = rounded.shape
    tile = jax.ShapeDtypeStruct((count, TILE, TILE), jnp.bfloat16)
    return pl.pallas_call(
        update_separator_kernel,
        out_shape=(jax.ShapeDtypeStruct((TILE, 2 * TILE), jnp.bfloat16), tile, tile),
        in_specs=[SMEM, SMEM, VMEM, VMEM, VMEM, ANY],
        out_specs=(VMEM, VMEM, VMEM),
        scratch_shapes=[
            pltpu.VMEM((2, TILE, order), jnp.bfloat16),
            pltpu.VMEM((2, count + 1, TILE, TILE), jnp.bfloat16),
            pltpu.SemaphoreType.DMA((2,)),
        ],
        compiler_params=pltpu.CompilerParams(vmem_limit_bytes=24 * 2**20),
        cost_estimate=pl.CostEstimate(flops=3 * 10**9, bytes_accessed=10**7, transcendentals=0),
        name="update_separator",
    )(ids, next_map, keep, peer, rounded, shared)


def update_trailing_kernel(
    positions, ids_ref, next_ref, keep_ref, peer_ref, round_ref, shared_ref, out_ref, taken, tiles, sems
):
    def write(i, slot, tile):
        if slot:
            out_ref[slot - 1, :, i * TILE : (i + 1) * TILE] = tile()

    copies = start_shared(ids_ref, positions, shared_ref, taken, sems)
    update_columns(ids_ref, next_ref, positions, copies, keep_ref, peer_ref, round_ref, taken, tiles, write)


def update_trailing(ids, next_map, keep, peer, rounded, shared, positions):
    count, _, order = rounded.shape
    width = len(positions)
    return pl.pallas_call(
        functools.partial(update_trailing_kernel, positions),
        out_shape=jax.ShapeDtypeStruct((count, TILE, width * TILE), jnp.bfloat16),
        in_specs=[SMEM, SMEM, VMEM, VMEM, VMEM, ANY],
        out_specs=VMEM,
        scratch_shapes=[
            pltpu.VMEM((width, TILE, order), jnp.bfloat16),
            pltpu.VMEM((width, count + 1, TILE, TILE), jnp.bfloat16),
            pltpu.SemaphoreType.DMA((width,)),
        ],
        compiler_params=pltpu.CompilerParams(vmem_limit_bytes=24 * 2**20),
        cost_estimate=pl.CostEstimate(flops=4 * 10**9, bytes_accessed=12 * 10**6, transcendentals=0),
        name="update_trailing",
    )(ids, next_map, keep, peer, rounded, shared)


def update_two_kernel(ids_ref, near_ref, far_ref, round_ref, shared_ref, out_ref):
    quarter = ids_ref[0] & 3
    for i in range(3):
        shared = shared_ref[(3 * quarter + i) & 3]
        span = slice(i * TILE, (i + 1) * TILE)
        for s in range(near_ref.shape[0]):
            total = near_ref[s, :, span].astype(jnp.float32) + far_ref[s, :, span].astype(jnp.float32)
            out_ref[s, :, span] = (total - dot_lanes(round_ref[s], shared)).astype(jnp.bfloat16)


def update_two(ids, near, far, rounded, shared):
    return pl.pallas_call(
        update_two_kernel,
        out_shape=jax.ShapeDtypeStruct(near.shape, jnp.bfloat16),
        in_specs=[SMEM, VMEM, VMEM, VMEM, VMEM],
        out_specs=VMEM,
        compiler_params=PARAMS,
        cost_estimate=pl.CostEstimate(flops=2 * 10**9, bytes_accessed=10**7, transcendentals=0),
        name="update_two",
    )(ids, near, far, rounded, shared)


def over_square(pack):
    half = pack.shape[0] // 2
    x, y, core = swapped(pack, "leaf", 0), swapped(pack, "front", 1), swapped(pack, "front", 0)
    top = swapped(y[:half], "leaf", 0)
    low = swapped(x[half:], "front", 1)
    x_core, y_core = swapped(x, "front", 0), swapped(y, "front", 0)
    top_core, low_core = swapped(top, "front", 0), swapped(low, "front", 0)
    return (pack, core, y, y_core, x, x_core, top, low, top_core, low_core)


def after(value, *earlier):
    return lax.optimization_barrier((value, *earlier))[0]


def body(child_update, sep_one, sep_two, map_one, map_two, mask_one, mask_two):
    column = lax.axis_index("front")
    leaf = lax.axis_index("leaf")
    half, side, quad = leaf & 1, (leaf >> 1) & 1, leaf >> 2
    ids = jnp.stack([leaf, column]).astype(jnp.int32)
    child = child_update[0, 0, 0]
    entries_one = sep_one[0, 0, 0]
    entries_two = sep_two[0, 0, 0]
    count = child.shape[0]
    order = GROUPS * TILE
    maps_one = map_one.reshape(-1)
    maps_two = map_two.reshape(-1)

    pivot_mine, coupling_mine = pick_separator(ids, maps_one, child, entries_one)
    packs = over_square(pivot_mine)
    coupling_peer = swapped(after(coupling_mine, packs[4]), "leaf", 0)
    sep_send, near_send, far_send, sep_keep, near_keep, far_keep = pick_trailing(ids, maps_one, maps_two, child)
    sep_peer = swapped(after(sep_send, packs[6]), "leaf", 0)
    far_peer = swapped(after(far_send, packs[6]), "leaf", 0)
    entries_near = swapped(after(entries_two, packs[6]), "leaf", 0)
    entries_far = swapped(entries_near[0], "leaf", 1)

    lower, inverse = cholesky(ids, packs, fill_one, order)
    factor_one, rounded, share = panel_one(
        ids, mask_one.reshape(-1), maps_two, coupling_mine, coupling_peer, lower, inverse
    )
    shared = lax.all_gather(after(share, sep_peer), "front", axis=0, tiled=True)
    pivot_own, near_coupling, far_coupling = update_separator(ids, maps_two, sep_keep, sep_peer, rounded, shared)

    pivot_far = swapped(pivot_own, "leaf", 1)
    pivot_tile = (
        pivot_own.astype(jnp.float32)
        + jnp.concatenate([pivot_far[:, TILE:], pivot_far[:, :TILE]], axis=1).astype(jnp.float32)
        + jnp.concatenate([entries_near[0], entries_far], axis=1).astype(jnp.float32)
    )
    packs = over_square(pivot_tile)
    far_trailing = update_trailing(
        ids, maps_two, far_keep, far_peer, after(rounded, pivot_far), shared, (5, 6, 7)
    )
    coupling_far = swapped(after(far_coupling, pivot_far), "leaf", 1)
    mask_second = lax.dynamic_index_in_dim(mask_two, quad, 0, keepdims=False).reshape(count, GROUPS, -1)
    mask_second = lax.dynamic_index_in_dim(mask_second, column, 1, keepdims=False)
    mask_second = lax.dynamic_index_in_dim(mask_second, 2 * side + 1 - half, 1, keepdims=False)
    coupling = (
        near_coupling.astype(jnp.float32)
        + coupling_far.astype(jnp.float32)
        + entries_near[1:].astype(jnp.float32) * mask_second.astype(jnp.float32)[:, None, None]
    ).reshape(count * TILE, TILE)
    coupling_x = swapped(after(coupling, packs[6]), "leaf", 0)
    coupling_z, coupling_xz = swapped((coupling, coupling_x), "leaf", 1)
    trailing_far = swapped(after(far_trailing, coupling_x), "leaf", 1)
    near_peer = swapped(after(near_send, coupling_x), "leaf", 0)
    lower, inverse = cholesky(ids, packs, fill_two, order)
    factor_two, rounded_two, share = panel_two(
        ids, (after(coupling, near_peer, trailing_far), coupling_x, coupling_z, coupling_xz), lower, inverse
    )
    near_trailing = update_trailing(ids, maps_two, near_keep, near_peer, rounded, shared, (1, 2, 3))
    shared = lax.all_gather(share[None], "front", axis=0, tiled=True)
    update = update_two(ids, near_trailing, trailing_far, rounded_two, shared)
    return (factor_one[None, None, None], factor_two[None, None, None], update[None, None, None])


def solution(mesh):
    split = P("leaf", "front", None, None, None, None)
    return jax.shard_map(
        body,
        mesh=mesh,
        in_specs=(split, split, split, P(), P(), P(), P()),
        out_specs=(split, split, split),
        check_vma=False,
    )
```

```python
import functools

import jax
import jax.numpy as jnp
from jax import lax
from jax.experimental import pallas as pl
from jax.experimental.pallas import tpu as pltpu
from jax.sharding import PartitionSpec as P

VMEM = pl.BlockSpec(memory_space=pltpu.VMEM)
SMEM = pl.BlockSpec(memory_space=pltpu.SMEM)
ANY = pl.BlockSpec(memory_space=pl.ANY)
GROUPS = 4
PARAMS = pltpu.CompilerParams(vmem_limit_bytes=32 * 2**20)
BLK = 128
GRP = 8
TILE = 256
NT = (((1,), (1,)), ((), ()))


def halves(x):
    high = x.astype(jnp.bfloat16)
    low = (x - high.astype(jnp.float32)).astype(jnp.bfloat16)
    return high, low


def left_parts(x):
    high, low = halves(x)
    return jnp.concatenate([high, low, high], axis=1)


def right_rows(x):
    high, low = halves(x)
    return jnp.concatenate([high, high, low], axis=0)


def right_lanes(x):
    high, low = halves(x)
    return jnp.concatenate([high, high, low], axis=1)


def dot_rows(left, right):
    return jnp.dot(left, right, preferred_element_type=jnp.float32)


def dot_lanes(left, right):
    return lax.dot_general(left, right, NT, preferred_element_type=jnp.float32)


def spread_row(ref, index):
    return jnp.broadcast_to(ref[index], (GRP, BLK))


def factor_diagonal(block, done_ref, pivot_ref, rows_ref):
    steps = BLK // GRP
    row_id = lax.broadcasted_iota(jnp.int32, (GRP, BLK), 0)
    lane_id = lax.broadcasted_iota(jnp.int32, (GRP, BLK), 1)
    matrix = [block[GRP * g : GRP * (g + 1), :] for g in range(steps)]
    inverse = [jnp.where(lane_id == row_id + GRP * g, 1.0, 0.0).astype(jnp.float32) for g in range(steps)]
    for g in range(steps):
        first = GRP * g
        slot = g % 2
        current = matrix[g]
        rows_ref[slot, :, 0:BLK] = current
        rows_ref[slot, :, BLK:] = inverse[g]
        for i in range(GRP):
            pivot_ref[slot, i] = jnp.broadcast_to(current[:, first + i : first + i + 1], (GRP, BLK))
        entry = {}
        for m in range(GRP):
            for i in range(m + 1):
                entry[m, i] = jnp.broadcast_to(pivot_ref[slot, i, m : m + 1, :], (GRP, BLK))
                entry[i, m] = entry[m, i]
        left = [jnp.broadcast_to(rows_ref[slot, m : m + 1, 0:BLK], (GRP, BLK)) for m in range(GRP)]
        right = [jnp.broadcast_to(rows_ref[slot, m : m + 1, BLK:], (GRP, BLK)) for m in range(GRP)]
        for i in range(GRP):
            root = lax.rsqrt(entry[i, i])
            scale = root * root
            done_ref[first + i : first + i + 1, 0:BLK] = (left[i] * root)[0:1]
            done_ref[first + i : first + i + 1, BLK:] = (right[i] * root)[0:1]
            left[i] = left[i] * scale
            right[i] = right[i] * scale
            scaled = {c: entry[i, c] * scale for c in range(i + 1, GRP)}
            for m in range(GRP):
                if m == i:
                    continue
                weight = entry[m, i]
                left[m] = left[m] - weight * left[i]
                right[m] = right[m] - weight * right[i]
                for c in range(i + 1, GRP):
                    if m > c:
                        continue
                    entry[m, c] = entry[m, c] - weight * scaled[c]
            for m in range(i + 1, GRP):
                for c in range(i + 1, m):
                    entry[m, c] = entry[c, m]
            for c in range(i + 1, GRP):
                entry[i, c] = scaled[c]
        for later in range(g + 1, steps):
            rows = matrix[later]
            total_left, total_right = None, None
            for i in range(GRP):
                weight = jnp.broadcast_to(rows[:, first + i : first + i + 1], (GRP, BLK))
                part_left, part_right = weight * left[i], weight * right[i]
                total_left = part_left if total_left is None else total_left + part_left
                total_right = part_right if total_right is None else total_right + part_right
            matrix[later] = rows - total_left
            inverse[later] = inverse[later] - total_right


def fill_one(ids_ref, packs, work):
    leaf, column = ids_ref[0], ids_ref[1]
    half = leaf & 1
    order = work.shape[1]
    own, core, y, y_core, x, x_core = packs[:6]
    for apart, mine, peers in (
        (0, own, (x,)),
        (1, core, (x_core,)),
        (2, y, packs[6:8]),
        (3, y_core, packs[8:10]),
    ):
        base = (column ^ apart) * TILE
        height = TILE // len(peers)
        for part, peer in enumerate(peers):
            rows = pl.ds(pl.multiple_of(base + part * height, height), height)
            piece = slice(part * height, (part + 1) * height)
            work[rows, :] = mine[piece, 0:order].astype(jnp.float32) + peer[:, 0:order].astype(jnp.float32)
            for place, ref, span in ((half, mine, piece), (1 - half, peer, slice(None))):
                columns = pl.ds(pl.multiple_of(place * (order // 2), order // 2), order // 2)
                work[rows, columns] = work[rows, columns] + ref[span, order:].astype(jnp.float32)


def fill_two(ids_ref, packs, work):
    leaf, column = ids_ref[0], ids_ref[1]
    half, side = leaf & 1, (leaf >> 1) & 1
    own, core, y, y_core, x, x_core = packs[:6]
    for apart, mine, peers in (
        (0, own, (x,)),
        (1, core, (x_core,)),
        (2, y, packs[6:8]),
        (3, y_core, packs[8:10]),
    ):
        base = (column ^ apart) * TILE
        for refs, last in (((mine,), 1 - half), (peers, half)):
            height = TILE // len(refs)
            for part, ref in enumerate(refs):
                rows = pl.ds(pl.multiple_of(base + part * height, height), height)
                for position, place in ((0, 2 * side + last), (1, 2 * (1 - side) + last)):
                    columns = pl.ds(pl.multiple_of(place * TILE, TILE), TILE)
                    work[rows, columns] = ref[:, position * TILE : (position + 1) * TILE]


def cholesky_kernel(fill, ids_ref, *refs):
    packs = refs[:10]
    lower_ref, inverse_ref, work, done, block_inverse, entries, rows = refs[10:]
    order = work.shape[0]
    blocks = order // BLK
    fill(ids_ref, packs, work)
    lower_ref[...] = jnp.zeros_like(lower_ref)
    row_id = lax.broadcasted_iota(jnp.int32, (BLK, BLK), 0)
    lane_id = lax.broadcasted_iota(jnp.int32, (BLK, BLK), 1)

    def step(k, carry):
        start = pl.multiple_of(k * BLK, BLK)
        span = pl.ds(start, BLK)
        factor_diagonal(work[span, span], done, entries, rows)
        upper = jnp.where(lane_id >= row_id, done[:, 0:BLK], 0.0)
        lower_ref[span, span] = upper.T
        block_inverse[k] = done[:, BLK:]
        for fixed in range(blocks - 1):
            after = (fixed + 1) * BLK

            @pl.when(k == fixed)
            def _():
                strip = dot_rows(
                    left_parts(done[:, BLK:]), right_rows(work[after - BLK : after, after:])
                )
                column = strip.T
                lower_ref[after:, after - BLK : after] = column
                left = left_parts(column)
                right = right_rows(strip)
                width = order - after
                for top in range(0, width, TILE):
                    high = min(TILE, width - top)
                    work[after + top : after + top + high, after + top :] = work[
                        after + top : after + top + high, after + top :
                    ] - dot_rows(left[top : top + high], right[:, top:])

        return carry

    lax.fori_loop(0, blocks, step, 0)
    for tile in range(order // TILE):
        base = tile * TILE
        first, second = block_inverse[2 * tile], block_inverse[2 * tile + 1]
        corner = lower_ref[base + BLK : base + TILE, base : base + BLK]
        mixed = dot_rows(left_parts(corner), right_rows(first))
        mixed = -dot_rows(left_parts(second), right_rows(mixed))
        inverse_ref[tile, 0:BLK, 0:BLK] = first
        inverse_ref[tile, 0:BLK, BLK:] = jnp.zeros((BLK, BLK), jnp.float32)
        inverse_ref[tile, BLK:, 0:BLK] = mixed
        inverse_ref[tile, BLK:, BLK:] = second


def cholesky(ids, packs, fill, order):
    return pl.pallas_call(
        functools.partial(cholesky_kernel, fill),
        out_shape=(
            jax.ShapeDtypeStruct((order, order), jnp.float32),
            jax.ShapeDtypeStruct((order // TILE, TILE, TILE), jnp.float32),
        ),
        in_specs=[SMEM] + [VMEM] * len(packs),
        out_specs=(VMEM, VMEM),
        scratch_shapes=[
            pltpu.VMEM((order, order), jnp.float32),
            pltpu.VMEM((BLK, 2 * BLK), jnp.float32),
            pltpu.VMEM((order // BLK, BLK, BLK), jnp.float32),
            pltpu.VMEM((2, GRP, GRP, BLK), jnp.float32),
            pltpu.VMEM((2, GRP, 2 * BLK), jnp.float32),
        ],
        compiler_params=pltpu.CompilerParams(vmem_limit_bytes=32 * 2**20),
        cost_estimate=pl.CostEstimate(flops=4 * 10**10, bytes_accessed=10**8, transcendentals=0),
        name="cholesky",
    )(ids, *packs)


def swapped(value, axis, apart):
    mask = 2**apart
    pairs = [(source, source ^ mask) for source in range(lax.axis_size(axis))]
    return lax.ppermute(value, axis, pairs)


def find_tile(map_ref, owner, group, slot, count):
    found = jnp.int32(-1)
    for s in range(count):
        found = jnp.where(map_ref[owner, group, s] == slot, jnp.int32(s), found)
    return found


def column_targets(half, side):
    targets = []
    for part in (side, 1 - side):
        targets.append(2 * part + 1 - half)
        targets += [4 + 3 * (2 * part + half) + i for i in range(3)]
    return targets


def share_place(target, half):
    place = jnp.int32(0)
    for other in column_targets(half, 0):
        earlier = jnp.logical_and((other & 3) == (target & 3), other < target)
        place = place + earlier.astype(jnp.int32)
    return place


def move_tile(live, source, target, sem):
    @pl.when(live)
    def _():
        pltpu.make_async_copy(source, target, sem).start()

    @pl.when(jnp.logical_not(live))
    def _():
        target[...] = jnp.zeros(target.shape, target.dtype)

    def wait():
        @pl.when(live)
        def _():
            pltpu.make_async_copy(source, target, sem).wait()

    return wait


def move_separator(leaf, column, map_ref, child_ref, slots, target_of, sems):
    count = child_ref.shape[0]
    waits = []
    for slot in slots:
        row = find_tile(map_ref, leaf, column, slot, count)
        for group in range(GROUPS):
            place = find_tile(map_ref, leaf, group, 0, count)
            live = jnp.logical_and(row >= 0, place >= 0)
            span = pl.ds(pl.multiple_of((jnp.maximum(place, 0) * GROUPS + group) * TILE, TILE), TILE)
            source = child_ref.at[jnp.maximum(row, 0), :, span]
            target = target_of(slot).at[:, pl.ds(group * TILE, TILE)]
            waits.append(move_tile(live, source, target, sems.at[len(waits)]))
    return waits


def pick_pivot_kernel(ids_ref, map_ref, child_ref, entries_ref, pivot_ref, sems, entry_sem):
    width = GROUPS * TILE
    entries = pltpu.make_async_copy(entries_ref.at[0], pivot_ref.at[:, pl.ds(width, width // 2)], entry_sem.at[0])
    entries.start()
    waits = move_separator(ids_ref[0], ids_ref[1], map_ref, child_ref, (0,), lambda slot: pivot_ref, sems)
    for wait in waits:
        wait()
    entries.wait()


def pick_pivot(ids, child_map, child, entries):
    width = GROUPS * TILE + entries.shape[-1]
    return pl.pallas_call(
        pick_pivot_kernel,
        out_shape=jax.ShapeDtypeStruct((TILE, width), child.dtype),
        in_specs=[SMEM, SMEM, ANY, ANY],
        out_specs=VMEM,
        scratch_shapes=[pltpu.SemaphoreType.DMA((GROUPS,)), pltpu.SemaphoreType.DMA((1,))],
        compiler_params=pltpu.CompilerParams(vmem_limit_bytes=56 * 2**20),
        name="pick_pivot",
    )(ids, child_map, child, entries)


def pick_rest_kernel(ids_ref, map_ref, next_ref, child_ref, entries_ref, coupling_ref, *refs):
    outs, (first_sems, sems, entry_sem) = refs[:6], refs[6:]
    count = child_ref.shape[0]
    width = GROUPS * TILE
    leaf, column = ids_ref[0], ids_ref[1]
    pair = leaf >> 1
    entries = pltpu.make_async_copy(
        entries_ref.at[pl.ds(1, count)], coupling_ref.at[:, :, pl.ds(width, width // 2)], entry_sem.at[0]
    )
    entries.start()
    slots = range(1, count + 1)
    waits = move_separator(
        leaf, column, map_ref, child_ref, slots, lambda slot: coupling_ref.at[slot - 1], first_sems
    )
    rows = [find_tile(map_ref, leaf, column, slot, count) for slot in slots]
    used = 0
    for which, device in enumerate((leaf ^ 1, leaf)):
        for position, target in enumerate(column_targets(device & 1, (device >> 1) & 1)):
            group = target & 3
            update = find_tile(next_ref, pair, group, target >> 2, count)
            place = find_tile(map_ref, leaf, group, update + 1, count)
            column_live = jnp.logical_and(update >= 0, place >= 0)
            source_span = pl.ds(pl.multiple_of((jnp.maximum(place, 0) * GROUPS + group) * TILE, TILE), TILE)
            for slot, row in enumerate(rows):
                live = jnp.logical_and(column_live, row >= 0)
                source = child_ref.at[jnp.maximum(row, 0), :, source_span]
                if position % 4 == 0:
                    goal = outs[3 * which].at[slot, :, pl.ds(position // 4 * TILE, TILE)]
                else:
                    goal = outs[3 * which + 1 + position // 4].at[slot, :, pl.ds((position % 4 - 1) * TILE, TILE)]
                waits.append(move_tile(live, source, goal, sems.at[used]))
                used += 1
    for wait in waits:
        wait()
    entries.wait()


def pick_rest(ids, child_map, next_map, child, entries):
    count = child.shape[0]
    wide = GROUPS * TILE + entries.shape[-1]
    widths = (wide,) + (2 * TILE, 3 * TILE, 3 * TILE) * 2
    return pl.pallas_call(
        pick_rest_kernel,
        out_shape=tuple(jax.ShapeDtypeStruct((count, TILE, width), child.dtype) for width in widths),
        in_specs=[SMEM, SMEM, SMEM, ANY, ANY],
        out_specs=(VMEM,) * 7,
        scratch_shapes=[
            pltpu.SemaphoreType.DMA((GROUPS * count,)),
            pltpu.SemaphoreType.DMA((16 * count,)),
            pltpu.SemaphoreType.DMA((1,)),
        ],
        compiler_params=pltpu.CompilerParams(vmem_limit_bytes=56 * 2**20),
        cost_estimate=pl.CostEstimate(flops=0, bytes_accessed=2 * 10**7, transcendentals=0),
        name="pick_rest",
    )(ids, child_map, next_map, child, entries)


def solve_blocks(coupling_ref, lower_ref, inverse_ref, panel_ref):
    order = lower_ref.shape[0]
    solved = []
    for k in range(order // TILE):
        span = slice(k * TILE, (k + 1) * TILE)
        rest = coupling_ref[:, span]
        if k:
            left = jnp.concatenate([part[0] for part in solved], axis=1)
            low = jnp.concatenate([part[1] for part in solved], axis=1)
            high_lower, low_lower = halves(lower_ref[span, 0 : k * TILE])
            rest = rest - dot_lanes(
                jnp.concatenate([left, low, left], axis=1),
                jnp.concatenate([high_lower, high_lower, low_lower], axis=1),
            )
        block = dot_lanes(left_parts(rest), right_lanes(inverse_ref[k]))
        panel_ref[:, span] = block
        solved.append(halves(block))
    return jnp.concatenate([part[0] for part in solved], axis=1)


def write_factor(column, offset, lower_ref, panel, factor_ref):
    width = factor_ref.shape[-1]
    rows = pl.ds(pl.multiple_of(column * TILE, TILE), TILE)
    span = pl.ds(pl.multiple_of(offset * width, width), width)
    factor_ref[0] = lower_ref[rows, span]
    for s in range(factor_ref.shape[0] - 1):
        factor_ref[s + 1] = panel[s * TILE : (s + 1) * TILE, span]


def panel_one_kernel(
    ids_ref, mask_ref, next_ref, mine_ref, peer_ref, lower_ref, inverse_ref, factor_ref, round_ref, share_ref, coupling, panel
):
    leaf, column = ids_ref[0], ids_ref[1]
    half, pair = leaf & 1, leaf >> 1
    count = mine_ref.shape[0]
    order = lower_ref.shape[0]
    for s in range(count):
        for tile in range(order // TILE):
            span = slice(tile * TILE, (tile + 1) * TILE)
            where = order + (tile % 2) * TILE
            weight = mask_ref[((pair * count + s) * GROUPS + column) * GROUPS + tile].astype(jnp.float32)
            mine = mine_ref[s, :, where : where + TILE].astype(jnp.float32)
            peer = peer_ref[s, :, where : where + TILE].astype(jnp.float32)
            own_first = half == tile // 2
            entry = jnp.where(own_first, mine, peer)
            coupling[s * TILE : (s + 1) * TILE, span] = (
                mine_ref[s, :, span].astype(jnp.float32) + peer_ref[s, :, span].astype(jnp.float32) + entry * weight
            )
    rounded = solve_blocks(coupling, lower_ref, inverse_ref, panel)
    for s in range(count):
        round_ref[s] = rounded[s * TILE : (s + 1) * TILE]
    write_factor(column, half, lower_ref, panel, factor_ref)
    for a in range(2):
        slot = jnp.int32(0)
        for target in column_targets(half, 0):
            hit = jnp.logical_and((target & 3) == column, share_place(target, half) == a)
            slot = jnp.where(hit, target >> 2, slot)
        tile = find_tile(next_ref, pair, column, slot, count)
        share_ref[a] = round_ref[jnp.maximum(tile, 0)]


def panel_one(ids, mask, next_map, mine, peer, lower, inverse):
    count = mine.shape[0]
    order = lower.shape[0]
    return pl.pallas_call(
        panel_one_kernel,
        out_shape=(
            jax.ShapeDtypeStruct((count + 1, TILE, order // 2), jnp.float32),
            jax.ShapeDtypeStruct((count, TILE, order), jnp.bfloat16),
            jax.ShapeDtypeStruct((2, TILE, order), jnp.bfloat16),
        ),
        in_specs=[SMEM, SMEM, SMEM, VMEM, VMEM, VMEM, VMEM],
        out_specs=(VMEM, VMEM, VMEM),
        scratch_shapes=[
            pltpu.VMEM((count * TILE, order), jnp.float32),
            pltpu.VMEM((count * TILE, order), jnp.float32),
        ],
        compiler_params=PARAMS,
        cost_estimate=pl.CostEstimate(flops=10**10, bytes_accessed=2 * 10**7, transcendentals=0),
        name="panel_one",
    )(ids, mask, next_map, mine, peer, lower, inverse)


def panel_two_kernel(ids_ref, own_ref, x_ref, z_ref, both_ref, lower_ref, inverse_ref, factor_ref, round_ref, share_ref, coupling, panel):
    leaf, column = ids_ref[0], ids_ref[1]
    half, side = leaf & 1, (leaf >> 1) & 1
    quarter = leaf & 3
    count = round_ref.shape[0]
    for place, ref in (
        (2 * side + 1 - half, own_ref),
        (2 * side + half, x_ref),
        (2 * (1 - side) + 1 - half, z_ref),
        (2 * (1 - side) + half, both_ref),
    ):
        coupling[:, pl.ds(pl.multiple_of(place * TILE, TILE), TILE)] = ref[...]
    rounded = solve_blocks(coupling, lower_ref, inverse_ref, panel)
    for s in range(count):
        round_ref[s] = rounded[s * TILE : (s + 1) * TILE]
    write_factor(column, quarter, lower_ref, panel, factor_ref)
    chosen = jnp.int32(0)
    for i in range(3):
        tile = 3 * quarter + i
        chosen = jnp.where((tile & 3) == column, tile >> 2, chosen)
    share_ref[...] = round_ref[chosen]


def panel_two(ids, parts, lower, inverse):
    rows = parts[0].shape[0]
    count = rows // TILE
    order = lower.shape[0]
    return pl.pallas_call(
        panel_two_kernel,
        out_shape=(
            jax.ShapeDtypeStruct((count + 1, TILE, order // 4), jnp.float32),
            jax.ShapeDtypeStruct((count, TILE, order), jnp.bfloat16),
            jax.ShapeDtypeStruct((TILE, order), jnp.bfloat16),
        ),
        in_specs=[SMEM] + [VMEM] * 6,
        out_specs=(VMEM, VMEM, VMEM),
        scratch_shapes=[pltpu.VMEM((rows, order), jnp.float32), pltpu.VMEM((rows, order), jnp.float32)],
        compiler_params=PARAMS,
        cost_estimate=pl.CostEstimate(flops=10**10, bytes_accessed=2 * 10**7, transcendentals=0),
        name="panel_two",
    )(ids, *parts, lower, inverse)


def start_shared(ids_ref, positions, shared_ref, taken, sems):
    leaf = ids_ref[0]
    half, side = leaf & 1, (leaf >> 1) & 1
    targets = column_targets(half, side)
    copies = []
    for i, position in enumerate(positions):
        target = targets[position]
        source = shared_ref.at[(target & 3) * 2 + share_place(target, half)]
        copies.append(pltpu.make_async_copy(source, taken.at[i], sems.at[i]))
        copies[-1].start()
    return copies


def update_columns(ids_ref, next_ref, positions, copies, keep_ref, peer_ref, round_ref, taken, tiles, write):
    leaf, column = ids_ref[0], ids_ref[1]
    half, side, pair = leaf & 1, (leaf >> 1) & 1, leaf >> 1
    count = keep_ref.shape[0]
    targets = column_targets(half, side)
    rows = [find_tile(next_ref, pair, column, slot, count) for slot in range(count + 1)]
    tiles[:, count] = jnp.zeros_like(tiles[:, count])
    for i, position in enumerate(positions):
        target = targets[position]
        live = find_tile(next_ref, pair, target & 3, target >> 2, count) >= 0
        span = slice(i * TILE, (i + 1) * TILE)
        copies[i].wait()
        for s in range(count):
            value = keep_ref[s, :, span].astype(jnp.float32) + peer_ref[s, :, span].astype(jnp.float32)
            value = value - dot_lanes(round_ref[s], taken[i])
            tiles[i, s] = jnp.where(live, value, 0.0).astype(jnp.bfloat16)
        for slot, row in enumerate(rows):
            write(i, slot, lambda row=row: tiles[i, jnp.where(row < 0, count, row)])


def update_separator_kernel(
    ids_ref, next_ref, keep_ref, peer_ref, round_ref, shared_ref, pivot_ref, near_ref, far_ref, taken, tiles, sems
):
    def write(i, slot, tile):
        if slot == 0:
            pivot_ref[:, i * TILE : (i + 1) * TILE] = tile()
        else:
            (near_ref, far_ref)[i][slot - 1] = tile()

    copies = start_shared(ids_ref, (0, 4), shared_ref, taken, sems)
    update_columns(ids_ref, next_ref, (0, 4), copies, keep_ref, peer_ref, round_ref, taken, tiles, write)


def update_separator(ids, next_map, keep, peer, rounded, shared):
    count, _, order = rounded.shape
    tile = jax.ShapeDtypeStruct((count, TILE, TILE), jnp.bfloat16)
    return pl.pallas_call(
        update_separator_kernel,
        out_shape=(jax.ShapeDtypeStruct((TILE, 2 * TILE), jnp.bfloat16), tile, tile),
        in_specs=[SMEM, SMEM, VMEM, VMEM, VMEM, ANY],
        out_specs=(VMEM, VMEM, VMEM),
        scratch_shapes=[
            pltpu.VMEM((2, TILE, order), jnp.bfloat16),
            pltpu.VMEM((2, count + 1, TILE, TILE), jnp.bfloat16),
            pltpu.SemaphoreType.DMA((2,)),
        ],
        compiler_params=pltpu.CompilerParams(vmem_limit_bytes=56 * 2**20),
        cost_estimate=pl.CostEstimate(flops=3 * 10**9, bytes_accessed=10**7, transcendentals=0),
        name="update_separator",
    )(ids, next_map, keep, peer, rounded, shared)


def update_trailing_kernel(
    positions, ids_ref, next_ref, keep_ref, peer_ref, round_ref, shared_ref, out_ref, taken, tiles, sems
):
    def write(i, slot, tile):
        if slot:
            out_ref[slot - 1, :, i * TILE : (i + 1) * TILE] = tile()

    copies = start_shared(ids_ref, positions, shared_ref, taken, sems)
    update_columns(ids_ref, next_ref, positions, copies, keep_ref, peer_ref, round_ref, taken, tiles, write)


def update_trailing(ids, next_map, keep, peer, rounded, shared, positions):
    count, _, order = rounded.shape
    width = len(positions)
    return pl.pallas_call(
        functools.partial(update_trailing_kernel, positions),
        out_shape=jax.ShapeDtypeStruct((count, TILE, width * TILE), jnp.bfloat16),
        in_specs=[SMEM, SMEM, VMEM, VMEM, VMEM, ANY],
        out_specs=VMEM,
        scratch_shapes=[
            pltpu.VMEM((width, TILE, order), jnp.bfloat16),
            pltpu.VMEM((width, count + 1, TILE, TILE), jnp.bfloat16),
            pltpu.SemaphoreType.DMA((width,)),
        ],
        compiler_params=pltpu.CompilerParams(vmem_limit_bytes=56 * 2**20),
        cost_estimate=pl.CostEstimate(flops=4 * 10**9, bytes_accessed=12 * 10**6, transcendentals=0),
        name="update_trailing",
    )(ids, next_map, keep, peer, rounded, shared)


def update_two_kernel(ids_ref, near_ref, far_ref, round_ref, shared_ref, out_ref):
    quarter = ids_ref[0] & 3
    for i in range(3):
        shared = shared_ref[(3 * quarter + i) & 3]
        span = slice(i * TILE, (i + 1) * TILE)
        for s in range(near_ref.shape[0]):
            total = near_ref[s, :, span].astype(jnp.float32) + far_ref[s, :, span].astype(jnp.float32)
            out_ref[s, :, span] = (total - dot_lanes(round_ref[s], shared)).astype(jnp.bfloat16)


def update_two(ids, near, far, rounded, shared):
    return pl.pallas_call(
        update_two_kernel,
        out_shape=jax.ShapeDtypeStruct(near.shape, jnp.bfloat16),
        in_specs=[SMEM, VMEM, VMEM, VMEM, VMEM],
        out_specs=VMEM,
        compiler_params=PARAMS,
        cost_estimate=pl.CostEstimate(flops=2 * 10**9, bytes_accessed=10**7, transcendentals=0),
        name="update_two",
    )(ids, near, far, rounded, shared)


def over_square(pack):
    half = pack.shape[0] // 2
    x, y, core = swapped(pack, "leaf", 0), swapped(pack, "front", 1), swapped(pack, "front", 0)
    top = swapped(y[:half], "leaf", 0)
    low = swapped(x[half:], "front", 1)
    x_core, y_core = swapped(x, "front", 0), swapped(y, "front", 0)
    top_core, low_core = swapped(top, "front", 0), swapped(low, "front", 0)
    return (pack, core, y, y_core, x, x_core, top, low, top_core, low_core)


def after(value, *earlier):
    return lax.optimization_barrier((value, *earlier))[0]


def body(child_update, sep_one, sep_two, map_one, map_two, mask_one, mask_two):
    column = lax.axis_index("front")
    leaf = lax.axis_index("leaf")
    half, side, quad = leaf & 1, (leaf >> 1) & 1, leaf >> 2
    ids = jnp.stack([leaf, column]).astype(jnp.int32)
    child = child_update[0, 0, 0]
    entries_one = sep_one[0, 0, 0]
    entries_two = sep_two[0, 0, 0]
    count = child.shape[0]
    order = GROUPS * TILE
    maps_one = map_one[:, 0]
    maps_two = map_two[:, 0]

    packs = over_square(pick_pivot(ids, maps_one, child, entries_one))
    coupling_mine, sep_send, near_send, far_send, sep_keep, near_keep, far_keep = pick_rest(
        ids, maps_one, maps_two, child, entries_one
    )
    coupling_peer = swapped(after(coupling_mine, packs[4]), "leaf", 0)
    sep_peer = swapped(after(sep_send, packs[6]), "leaf", 0)
    far_peer = swapped(after(far_send, packs[6]), "leaf", 0)
    entries_near = swapped(after(entries_two, packs[6]), "leaf", 0)
    entries_far = swapped(entries_near[0], "leaf", 1)

    lower, inverse = cholesky(ids, packs, fill_one, order)
    factor_one, rounded, share = panel_one(
        ids, mask_one.reshape(-1), maps_two, coupling_mine, coupling_peer, lower, inverse
    )
    shared = lax.all_gather(after(share, sep_peer), "front", axis=0, tiled=True)
    pivot_own, near_coupling, far_coupling = update_separator(
        ids, maps_two, after(sep_keep, far_peer), sep_peer, rounded, shared
    )

    pivot_far = swapped(pivot_own, "leaf", 1)
    pivot_tile = (
        pivot_own.astype(jnp.float32)
        + jnp.concatenate([pivot_far[:, TILE:], pivot_far[:, :TILE]], axis=1).astype(jnp.float32)
        + jnp.concatenate([entries_near[0], entries_far], axis=1).astype(jnp.float32)
    )
    packs = over_square(pivot_tile)
    far_trailing = update_trailing(
        ids, maps_two, far_keep, far_peer, after(rounded, pivot_far), shared, (5, 6, 7)
    )
    coupling_far = swapped(after(far_coupling, pivot_far), "leaf", 1)
    mask_second = lax.dynamic_index_in_dim(mask_two, quad, 0, keepdims=False).reshape(count, GROUPS, -1)
    mask_second = lax.dynamic_index_in_dim(mask_second, column, 1, keepdims=False)
    mask_second = lax.dynamic_index_in_dim(mask_second, 2 * side + 1 - half, 1, keepdims=False)
    coupling = (
        near_coupling.astype(jnp.float32)
        + coupling_far.astype(jnp.float32)
        + entries_near[1:].astype(jnp.float32) * mask_second.astype(jnp.float32)[:, None, None]
    ).reshape(count * TILE, TILE)
    coupling_x = swapped(after(coupling, packs[6]), "leaf", 0)
    coupling_z = swapped(coupling, "leaf", 1)
    coupling_xz = swapped(coupling_x, "leaf", 1)
    trailing_far = swapped(after(far_trailing, coupling_x), "leaf", 1)
    near_peer = swapped(after(near_send, coupling_x), "leaf", 0)
    lower, inverse = cholesky(ids, packs, fill_two, order)
    factor_two, rounded_two, share = panel_two(
        ids, (after(coupling, near_peer), coupling_x, coupling_z, coupling_xz), lower, inverse
    )
    near_trailing = update_trailing(ids, maps_two, near_keep, near_peer, rounded, shared, (1, 2, 3))
    shared = lax.all_gather(after(share, trailing_far)[None], "front", axis=0, tiled=True)
    update = update_two(ids, near_trailing, trailing_far, rounded_two, shared)
    return (factor_one[None, None, None], factor_two[None, None, None], update[None, None, None])


def solution(mesh):
    split = P("leaf", "front", None, None, None, None)
    return jax.shard_map(
        body,
        mesh=mesh,
        in_specs=(split, split, split, P(), P(), P(), P()),
        out_specs=(split, split, split),
        check_vma=False,
    )
```

```python
import functools

import jax
import jax.numpy as jnp
from jax import lax
from jax.experimental import pallas as pl
from jax.experimental.pallas import tpu as pltpu
from jax.sharding import PartitionSpec as P

VMEM = pl.BlockSpec(memory_space=pltpu.VMEM)
SMEM = pl.BlockSpec(memory_space=pltpu.SMEM)
ANY = pl.BlockSpec(memory_space=pl.ANY)
GROUPS = 4
PARAMS = pltpu.CompilerParams(vmem_limit_bytes=32 * 2**20)
BLK = 128
GRP = 8
TILE = 256
NT = (((1,), (1,)), ((), ()))


def halves(x):
    high = x.astype(jnp.bfloat16)
    low = (x - high.astype(jnp.float32)).astype(jnp.bfloat16)
    return high, low


def left_parts(x):
    high, low = halves(x)
    return jnp.concatenate([high, low, high], axis=1)


def right_rows(x):
    high, low = halves(x)
    return jnp.concatenate([high, high, low], axis=0)


def right_lanes(x):
    high, low = halves(x)
    return jnp.concatenate([high, high, low], axis=1)


def dot_rows(left, right):
    return jnp.dot(left, right, preferred_element_type=jnp.float32)


def dot_lanes(left, right):
    return lax.dot_general(left, right, NT, preferred_element_type=jnp.float32)


def spread_row(ref, index):
    return jnp.broadcast_to(ref[index], (GRP, BLK))


def factor_diagonal(block, done_ref, pivot_ref, rows_ref):
    steps = BLK // GRP
    row_id = lax.broadcasted_iota(jnp.int32, (GRP, BLK), 0)
    lane_id = lax.broadcasted_iota(jnp.int32, (GRP, BLK), 1)
    matrix = [block[GRP * g : GRP * (g + 1), :] for g in range(steps)]
    inverse = [jnp.where(lane_id == row_id + GRP * g, 1.0, 0.0).astype(jnp.float32) for g in range(steps)]
    for g in range(steps):
        first = GRP * g
        slot = g % 2
        current = matrix[g]
        rows_ref[slot, :, 0:BLK] = current
        rows_ref[slot, :, BLK:] = inverse[g]
        for i in range(GRP):
            pivot_ref[slot, i] = jnp.broadcast_to(current[:, first + i : first + i + 1], (GRP, BLK))
        entry = {}
        for m in range(GRP):
            for i in range(m + 1):
                entry[m, i] = jnp.broadcast_to(pivot_ref[slot, i, m : m + 1, :], (GRP, BLK))
                entry[i, m] = entry[m, i]
        left = [jnp.broadcast_to(rows_ref[slot, m : m + 1, 0:BLK], (GRP, BLK)) for m in range(GRP)]
        right = [jnp.broadcast_to(rows_ref[slot, m : m + 1, BLK:], (GRP, BLK)) for m in range(GRP)]
        for i in range(GRP):
            root = lax.rsqrt(entry[i, i])
            scale = root * root
            done_ref[first + i : first + i + 1, 0:BLK] = (left[i] * root)[0:1]
            done_ref[first + i : first + i + 1, BLK:] = (right[i] * root)[0:1]
            left[i] = left[i] * scale
            right[i] = right[i] * scale
            scaled = {c: entry[i, c] * scale for c in range(i + 1, GRP)}
            for m in range(GRP):
                if m == i:
                    continue
                weight = entry[m, i]
                left[m] = left[m] - weight * left[i]
                right[m] = right[m] - weight * right[i]
                for c in range(i + 1, GRP):
                    if m > c:
                        continue
                    entry[m, c] = entry[m, c] - weight * scaled[c]
            for m in range(i + 1, GRP):
                for c in range(i + 1, m):
                    entry[m, c] = entry[c, m]
            for c in range(i + 1, GRP):
                entry[i, c] = scaled[c]
        for later in range(g + 1, steps):
            rows = matrix[later]
            total_left, total_right = None, None
            for i in range(GRP):
                weight = jnp.broadcast_to(rows[:, first + i : first + i + 1], (GRP, BLK))
                part_left, part_right = weight * left[i], weight * right[i]
                total_left = part_left if total_left is None else total_left + part_left
                total_right = part_right if total_right is None else total_right + part_right
            matrix[later] = rows - total_left
            inverse[later] = inverse[later] - total_right


def fill_one(ids_ref, packs, work):
    leaf, column = ids_ref[0], ids_ref[1]
    half = leaf & 1
    order = work.shape[1]
    own, core, y, y_core, x, x_core = packs[:6]
    for apart, mine, peers in (
        (0, own, (x,)),
        (1, core, (x_core,)),
        (2, y, packs[6:8]),
        (3, y_core, packs[8:10]),
    ):
        base = (column ^ apart) * TILE
        height = TILE // len(peers)
        for part, peer in enumerate(peers):
            rows = pl.ds(pl.multiple_of(base + part * height, height), height)
            piece = slice(part * height, (part + 1) * height)
            work[rows, :] = mine[piece, 0:order].astype(jnp.float32) + peer[:, 0:order].astype(jnp.float32)
            for place, ref, span in ((half, mine, piece), (1 - half, peer, slice(None))):
                columns = pl.ds(pl.multiple_of(place * (order // 2), order // 2), order // 2)
                work[rows, columns] = work[rows, columns] + ref[span, order:].astype(jnp.float32)


def fill_two(ids_ref, packs, work):
    leaf, column = ids_ref[0], ids_ref[1]
    half, side = leaf & 1, (leaf >> 1) & 1
    own, core, y, y_core, x, x_core = packs[:6]
    for apart, mine, peers in (
        (0, own, (x,)),
        (1, core, (x_core,)),
        (2, y, packs[6:8]),
        (3, y_core, packs[8:10]),
    ):
        base = (column ^ apart) * TILE
        for refs, last in (((mine,), half), (peers, 1 - half)):
            height = TILE // len(refs)
            for part, ref in enumerate(refs):
                rows = pl.ds(pl.multiple_of(base + part * height, height), height)
                for position, place in ((0, 2 * side + last), (1, 2 * (1 - side) + last)):
                    columns = pl.ds(pl.multiple_of(place * TILE, TILE), TILE)
                    work[rows, columns] = ref[:, position * TILE : (position + 1) * TILE]


def cholesky_kernel(fill, ids_ref, *refs):
    packs = refs[:10]
    lower_ref, inverse_ref, work, done, block_inverse, entries, rows = refs[10:]
    order = work.shape[0]
    blocks = order // BLK
    fill(ids_ref, packs, work)
    lower_ref[...] = jnp.zeros_like(lower_ref)
    row_id = lax.broadcasted_iota(jnp.int32, (BLK, BLK), 0)
    lane_id = lax.broadcasted_iota(jnp.int32, (BLK, BLK), 1)

    def step(k, carry):
        start = pl.multiple_of(k * BLK, BLK)
        span = pl.ds(start, BLK)
        factor_diagonal(work[span, span], done, entries, rows)
        upper = jnp.where(lane_id >= row_id, done[:, 0:BLK], 0.0)
        lower_ref[span, span] = upper.T
        block_inverse[k] = done[:, BLK:]
        for fixed in range(blocks - 1):
            after = (fixed + 1) * BLK

            @pl.when(k == fixed)
            def _():
                strip = dot_rows(
                    left_parts(done[:, BLK:]), right_rows(work[after - BLK : after, after:])
                )
                column = strip.T
                lower_ref[after:, after - BLK : after] = column
                left = left_parts(column)
                right = right_rows(strip)
                width = order - after
                for top in range(0, width, TILE):
                    high = min(TILE, width - top)
                    work[after + top : after + top + high, after + top :] = work[
                        after + top : after + top + high, after + top :
                    ] - dot_rows(left[top : top + high], right[:, top:])

        return carry

    lax.fori_loop(0, blocks, step, 0)
    for tile in range(order // TILE):
        base = tile * TILE
        first, second = block_inverse[2 * tile], block_inverse[2 * tile + 1]
        corner = lower_ref[base + BLK : base + TILE, base : base + BLK]
        mixed = dot_rows(left_parts(corner), right_rows(first))
        mixed = -dot_rows(left_parts(second), right_rows(mixed))
        inverse_ref[tile, 0:BLK, 0:BLK] = first
        inverse_ref[tile, 0:BLK, BLK:] = jnp.zeros((BLK, BLK), jnp.float32)
        inverse_ref[tile, BLK:, 0:BLK] = mixed
        inverse_ref[tile, BLK:, BLK:] = second


def cholesky(ids, packs, fill, order):
    return pl.pallas_call(
        functools.partial(cholesky_kernel, fill),
        out_shape=(
            jax.ShapeDtypeStruct((order, order), jnp.float32),
            jax.ShapeDtypeStruct((order // TILE, TILE, TILE), jnp.float32),
        ),
        in_specs=[SMEM] + [VMEM] * len(packs),
        out_specs=(VMEM, VMEM),
        scratch_shapes=[
            pltpu.VMEM((order, order), jnp.float32),
            pltpu.VMEM((BLK, 2 * BLK), jnp.float32),
            pltpu.VMEM((order // BLK, BLK, BLK), jnp.float32),
            pltpu.VMEM((2, GRP, GRP, BLK), jnp.float32),
            pltpu.VMEM((2, GRP, 2 * BLK), jnp.float32),
        ],
        compiler_params=pltpu.CompilerParams(vmem_limit_bytes=32 * 2**20),
        cost_estimate=pl.CostEstimate(flops=4 * 10**10, bytes_accessed=10**8, transcendentals=0),
        name="cholesky",
    )(ids, *packs)


def swapped(value, axis, mask):
    pairs = [(source, source ^ mask) for source in range(lax.axis_size(axis))]
    return lax.ppermute(value, axis, pairs)


def find_tile(map_ref, owner, group, slot, count):
    found = jnp.int32(-1)
    for s in range(count):
        found = jnp.where(map_ref[owner, group, s] == slot, jnp.int32(s), found)
    return found


def column_targets(half, side):
    targets = []
    for part in (side, 1 - side):
        targets.append(2 * part + half)
        targets += [4 + 3 * (2 * part + half) + i for i in range(3)]
    return targets


def share_place(target, half):
    place = jnp.int32(0)
    for other in column_targets(half, 0):
        earlier = jnp.logical_and((other & 3) == (target & 3), other < target)
        place = place + earlier.astype(jnp.int32)
    return place


def move_tile(live, source, target, sem):
    @pl.when(live)
    def _():
        pltpu.make_async_copy(source, target, sem).start()

    @pl.when(jnp.logical_not(live))
    def _():
        target[...] = jnp.zeros(target.shape, target.dtype)

    def wait():
        @pl.when(live)
        def _():
            pltpu.make_async_copy(source, target, sem).wait()

    return wait


def move_separator(leaf, column, map_ref, child_ref, slots, target_of, sems):
    count = child_ref.shape[0]
    waits = []
    for slot in slots:
        row = find_tile(map_ref, leaf, column, slot, count)
        for group in range(GROUPS):
            place = find_tile(map_ref, leaf, group, 0, count)
            live = jnp.logical_and(row >= 0, place >= 0)
            span = pl.ds(pl.multiple_of((jnp.maximum(place, 0) * GROUPS + group) * TILE, TILE), TILE)
            source = child_ref.at[jnp.maximum(row, 0), :, span]
            target = target_of(slot).at[:, pl.ds(group * TILE, TILE)]
            waits.append(move_tile(live, source, target, sems.at[len(waits)]))
    return waits


def pick_pivot_kernel(ids_ref, map_ref, child_ref, entries_ref, pivot_ref, sems, entry_sem):
    width = GROUPS * TILE
    entries = pltpu.make_async_copy(entries_ref.at[0], pivot_ref.at[:, pl.ds(width, width // 2)], entry_sem.at[0])
    entries.start()
    waits = move_separator(ids_ref[0], ids_ref[1], map_ref, child_ref, (0,), lambda slot: pivot_ref, sems)
    for wait in waits:
        wait()
    entries.wait()


def pick_pivot(ids, child_map, child, entries):
    width = GROUPS * TILE + entries.shape[-1]
    return pl.pallas_call(
        pick_pivot_kernel,
        out_shape=jax.ShapeDtypeStruct((TILE, width), child.dtype),
        in_specs=[SMEM, SMEM, ANY, ANY],
        out_specs=VMEM,
        scratch_shapes=[pltpu.SemaphoreType.DMA((GROUPS,)), pltpu.SemaphoreType.DMA((1,))],
        compiler_params=pltpu.CompilerParams(vmem_limit_bytes=56 * 2**20),
        name="pick_pivot",
    )(ids, child_map, child, entries)


def pick_rest_kernel(ids_ref, map_ref, next_ref, child_ref, entries_ref, coupling_ref, *refs):
    outs, (first_sems, sems, entry_sem) = refs[:6], refs[6:]
    count = child_ref.shape[0]
    width = GROUPS * TILE
    leaf, column = ids_ref[0], ids_ref[1]
    pair = leaf >> 1
    entries = pltpu.make_async_copy(
        entries_ref.at[pl.ds(1, count)], coupling_ref.at[:, :, pl.ds(width, width // 2)], entry_sem.at[0]
    )
    entries.start()
    slots = range(1, count + 1)
    waits = move_separator(
        leaf, column, map_ref, child_ref, slots, lambda slot: coupling_ref.at[slot - 1], first_sems
    )
    rows = [find_tile(map_ref, leaf, column, slot, count) for slot in slots]
    used = 0
    for which, device in enumerate((leaf ^ 1, leaf)):
        for position, target in enumerate(column_targets(device & 1, (device >> 1) & 1)):
            group = target & 3
            update = find_tile(next_ref, pair, group, target >> 2, count)
            place = find_tile(map_ref, leaf, group, update + 1, count)
            column_live = jnp.logical_and(update >= 0, place >= 0)
            source_span = pl.ds(pl.multiple_of((jnp.maximum(place, 0) * GROUPS + group) * TILE, TILE), TILE)
            for slot, row in enumerate(rows):
                live = jnp.logical_and(column_live, row >= 0)
                source = child_ref.at[jnp.maximum(row, 0), :, source_span]
                if position % 4 == 0:
                    goal = outs[3 * which].at[slot, :, pl.ds(position // 4 * TILE, TILE)]
                else:
                    goal = outs[3 * which + 1 + position // 4].at[slot, :, pl.ds((position % 4 - 1) * TILE, TILE)]
                waits.append(move_tile(live, source, goal, sems.at[used]))
                used += 1
    for wait in waits:
        wait()
    entries.wait()


def pick_rest(ids, child_map, next_map, child, entries):
    count = child.shape[0]
    wide = GROUPS * TILE + entries.shape[-1]
    widths = (wide,) + (2 * TILE, 3 * TILE, 3 * TILE) * 2
    return pl.pallas_call(
        pick_rest_kernel,
        out_shape=tuple(jax.ShapeDtypeStruct((count, TILE, width), child.dtype) for width in widths),
        in_specs=[SMEM, SMEM, SMEM, ANY, ANY],
        out_specs=(VMEM,) * 7,
        scratch_shapes=[
            pltpu.SemaphoreType.DMA((GROUPS * count,)),
            pltpu.SemaphoreType.DMA((16 * count,)),
            pltpu.SemaphoreType.DMA((1,)),
        ],
        compiler_params=pltpu.CompilerParams(vmem_limit_bytes=56 * 2**20),
        cost_estimate=pl.CostEstimate(flops=0, bytes_accessed=2 * 10**7, transcendentals=0),
        name="pick_rest",
    )(ids, child_map, next_map, child, entries)


def solve_blocks(coupling_ref, lower_ref, inverse_ref, panel_ref):
    order = lower_ref.shape[0]
    solved = []
    for k in range(order // TILE):
        span = slice(k * TILE, (k + 1) * TILE)
        rest = coupling_ref[:, span]
        if k:
            left = jnp.concatenate([part[0] for part in solved], axis=1)
            low = jnp.concatenate([part[1] for part in solved], axis=1)
            high_lower, low_lower = halves(lower_ref[span, 0 : k * TILE])
            rest = rest - dot_lanes(
                jnp.concatenate([left, low, left], axis=1),
                jnp.concatenate([high_lower, high_lower, low_lower], axis=1),
            )
        block = dot_lanes(left_parts(rest), right_lanes(inverse_ref[k]))
        panel_ref[:, span] = block
        solved.append(halves(block))
    return jnp.concatenate([part[0] for part in solved], axis=1)


def write_factor(column, offset, lower_ref, panel, factor_ref):
    width = factor_ref.shape[-1]
    rows = pl.ds(pl.multiple_of(column * TILE, TILE), TILE)
    span = pl.ds(pl.multiple_of(offset * width, width), width)
    factor_ref[0] = lower_ref[rows, span]
    for s in range(factor_ref.shape[0] - 1):
        factor_ref[s + 1] = panel[s * TILE : (s + 1) * TILE, span]


def panel_one_kernel(
    ids_ref, mask_ref, next_ref, mine_ref, peer_ref, lower_ref, inverse_ref, factor_ref, round_ref, first_ref, second_ref, third_ref, coupling, panel
):
    leaf, column = ids_ref[0], ids_ref[1]
    half, pair = leaf & 1, leaf >> 1
    count = mine_ref.shape[0]
    order = lower_ref.shape[0]
    for s in range(count):
        for tile in range(order // TILE):
            span = slice(tile * TILE, (tile + 1) * TILE)
            where = order + (tile % 2) * TILE
            weight = mask_ref[((pair * count + s) * GROUPS + column) * GROUPS + tile].astype(jnp.float32)
            mine = mine_ref[s, :, where : where + TILE].astype(jnp.float32)
            peer = peer_ref[s, :, where : where + TILE].astype(jnp.float32)
            own_first = half == tile // 2
            entry = jnp.where(own_first, mine, peer)
            coupling[s * TILE : (s + 1) * TILE, span] = (
                mine_ref[s, :, span].astype(jnp.float32) + peer_ref[s, :, span].astype(jnp.float32) + entry * weight
            )
    rounded = solve_blocks(coupling, lower_ref, inverse_ref, panel)
    for s in range(count):
        round_ref[s] = rounded[s * TILE : (s + 1) * TILE]
    write_factor(column, half, lower_ref, panel, factor_ref)
    for a, share_ref in enumerate((first_ref, second_ref, third_ref)):
        slot = jnp.int32(0)
        for target in column_targets(half, 0):
            hit = jnp.logical_and((target & 3) == column, share_place(target, half) == a)
            slot = jnp.where(hit, target >> 2, slot)
        tile = find_tile(next_ref, pair, column, slot, count)
        share_ref[...] = round_ref[jnp.maximum(tile, 0)]


def panel_one(ids, mask, next_map, mine, peer, lower, inverse):
    count = mine.shape[0]
    order = lower.shape[0]
    return pl.pallas_call(
        panel_one_kernel,
        out_shape=(
            jax.ShapeDtypeStruct((count + 1, TILE, order // 2), jnp.float32),
            jax.ShapeDtypeStruct((count, TILE, order), jnp.bfloat16),
        )
        + (jax.ShapeDtypeStruct((TILE, order), jnp.bfloat16),) * 3,
        in_specs=[SMEM, SMEM, SMEM, VMEM, VMEM, VMEM, VMEM],
        out_specs=(VMEM,) * 5,
        scratch_shapes=[
            pltpu.VMEM((count * TILE, order), jnp.float32),
            pltpu.VMEM((count * TILE, order), jnp.float32),
        ],
        compiler_params=PARAMS,
        cost_estimate=pl.CostEstimate(flops=10**9, bytes_accessed=10**6, transcendentals=0),
        name="panel_one",
    )(ids, mask, next_map, mine, peer, lower, inverse)


def panel_two_kernel(ids_ref, own_ref, x_ref, z_ref, both_ref, lower_ref, inverse_ref, factor_ref, round_ref, share_ref, coupling, panel):
    leaf, column = ids_ref[0], ids_ref[1]
    half, side = leaf & 1, (leaf >> 1) & 1
    quarter = leaf & 3
    count = round_ref.shape[0]
    for place, ref in (
        (2 * side + half, own_ref),
        (2 * side + 1 - half, x_ref),
        (2 * (1 - side) + half, z_ref),
        (2 * (1 - side) + 1 - half, both_ref),
    ):
        coupling[:, pl.ds(pl.multiple_of(place * TILE, TILE), TILE)] = ref[...]
    rounded = solve_blocks(coupling, lower_ref, inverse_ref, panel)
    for s in range(count):
        round_ref[s] = rounded[s * TILE : (s + 1) * TILE]
    write_factor(column, quarter, lower_ref, panel, factor_ref)
    chosen = jnp.int32(0)
    for i in range(3):
        tile = 3 * quarter + i
        chosen = jnp.where((tile & 3) == column, tile >> 2, chosen)
    share_ref[...] = round_ref[chosen]


def panel_two(ids, parts, lower, inverse):
    rows = parts[0].shape[0]
    count = rows // TILE
    order = lower.shape[0]
    return pl.pallas_call(
        panel_two_kernel,
        out_shape=(
            jax.ShapeDtypeStruct((count + 1, TILE, order // 4), jnp.float32),
            jax.ShapeDtypeStruct((count, TILE, order), jnp.bfloat16),
            jax.ShapeDtypeStruct((TILE, order), jnp.bfloat16),
        ),
        in_specs=[SMEM] + [VMEM] * 6,
        out_specs=(VMEM, VMEM, VMEM),
        scratch_shapes=[pltpu.VMEM((rows, order), jnp.float32), pltpu.VMEM((rows, order), jnp.float32)],
        compiler_params=PARAMS,
        cost_estimate=pl.CostEstimate(flops=10**9, bytes_accessed=10**6, transcendentals=0),
        name="panel_two",
    )(ids, *parts, lower, inverse)


def take_tile(owner, column, refs, live, target, sem):
    for apart, ref in enumerate(refs):

        @pl.when(jnp.logical_and(live, (owner ^ column) == apart))
        def _():
            pltpu.make_async_copy(ref, target, sem).start()


def start_shared(ids_ref, positions, firsts, seconds, taken, sems):
    leaf, column = ids_ref[0], ids_ref[1]
    half, side = leaf & 1, (leaf >> 1) & 1
    targets = column_targets(half, side)
    copies = []
    for i, position in enumerate(positions):
        target = targets[position]
        group = target & 3
        place = share_place(target, half)
        take_tile(group, column, firsts, place == 0, taken.at[i], sems.at[i])
        if seconds:
            take_tile(jnp.where(place == 2, group ^ 1, group), column, seconds, place > 0, taken.at[i], sems.at[i])
        copies.append(pltpu.make_async_copy(firsts[0], taken.at[i], sems.at[i]))
    return copies


def update_columns(ids_ref, next_ref, positions, copies, keep_ref, peer_ref, round_ref, taken, tiles, write):
    leaf, column = ids_ref[0], ids_ref[1]
    half, side, pair = leaf & 1, (leaf >> 1) & 1, leaf >> 1
    count = keep_ref.shape[0]
    targets = column_targets(half, side)
    rows = [find_tile(next_ref, pair, column, slot, count) for slot in range(count + 1)]
    tiles[:, count] = jnp.zeros_like(tiles[:, count])
    for i, position in enumerate(positions):
        target = targets[position]
        live = find_tile(next_ref, pair, target & 3, target >> 2, count) >= 0
        span = slice(i * TILE, (i + 1) * TILE)
        copies[i].wait()
        for s in range(count):
            value = keep_ref[s, :, span].astype(jnp.float32) + peer_ref[s, :, span].astype(jnp.float32)
            value = value - dot_lanes(round_ref[s], taken[i])
            tiles[i, s] = jnp.where(live, value, 0.0).astype(jnp.bfloat16)
        for slot, row in enumerate(rows):
            write(i, slot, lambda row=row: tiles[i, jnp.where(row < 0, count, row)])


def update_separator_kernel(
    ids_ref, next_ref, keep_ref, peer_ref, round_ref, *refs
):
    firsts, (pivot_ref, near_ref, far_ref, taken, tiles, sems) = refs[:4], refs[4:]

    def write(i, slot, tile):
        if slot == 0:
            pivot_ref[:, i * TILE : (i + 1) * TILE] = tile()
        else:
            (near_ref, far_ref)[i][slot - 1] = tile()

    copies = start_shared(ids_ref, (0, 4), firsts, (), taken, sems)
    update_columns(ids_ref, next_ref, (0, 4), copies, keep_ref, peer_ref, round_ref, taken, tiles, write)


def update_separator(ids, next_map, keep, peer, rounded, firsts):
    count, _, order = rounded.shape
    tile = jax.ShapeDtypeStruct((count, TILE, TILE), jnp.bfloat16)
    return pl.pallas_call(
        update_separator_kernel,
        out_shape=(jax.ShapeDtypeStruct((TILE, 2 * TILE), jnp.bfloat16), tile, tile),
        in_specs=[SMEM, SMEM, VMEM, VMEM, VMEM] + [ANY] * 4,
        out_specs=(VMEM, VMEM, VMEM),
        scratch_shapes=[
            pltpu.VMEM((2, TILE, order), jnp.bfloat16),
            pltpu.VMEM((2, count + 1, TILE, TILE), jnp.bfloat16),
            pltpu.SemaphoreType.DMA((2,)),
        ],
        compiler_params=pltpu.CompilerParams(vmem_limit_bytes=56 * 2**20),
        cost_estimate=pl.CostEstimate(flops=3 * 10**9, bytes_accessed=10**7, transcendentals=0),
        name="update_separator",
    )(ids, next_map, keep, peer, rounded, *firsts)


def update_trailing_kernel(
    positions, ids_ref, next_ref, keep_ref, peer_ref, round_ref, *refs
):
    firsts, seconds, (out_ref, taken, tiles, sems) = refs[:4], refs[4:8], refs[8:]

    def write(i, slot, tile):
        if slot:
            out_ref[slot - 1, :, i * TILE : (i + 1) * TILE] = tile()

    copies = start_shared(ids_ref, positions, firsts, seconds, taken, sems)
    update_columns(ids_ref, next_ref, positions, copies, keep_ref, peer_ref, round_ref, taken, tiles, write)


def update_trailing(ids, next_map, keep, peer, rounded, firsts, seconds, positions):
    count, _, order = rounded.shape
    width = len(positions)
    return pl.pallas_call(
        functools.partial(update_trailing_kernel, positions),
        out_shape=jax.ShapeDtypeStruct((count, TILE, width * TILE), jnp.bfloat16),
        in_specs=[SMEM, SMEM, VMEM, VMEM, VMEM] + [ANY] * 8,
        out_specs=VMEM,
        scratch_shapes=[
            pltpu.VMEM((width, TILE, order), jnp.bfloat16),
            pltpu.VMEM((width, count + 1, TILE, TILE), jnp.bfloat16),
            pltpu.SemaphoreType.DMA((width,)),
        ],
        compiler_params=pltpu.CompilerParams(vmem_limit_bytes=56 * 2**20),
        cost_estimate=pl.CostEstimate(flops=4 * 10**9, bytes_accessed=12 * 10**6, transcendentals=0),
        name="update_trailing",
    )(ids, next_map, keep, peer, rounded, *firsts, *seconds)


def update_two_kernel(ids_ref, near_ref, far_ref, round_ref, *refs):
    firsts, (out_ref, taken, sems) = refs[:4], refs[4:]
    quarter, column = ids_ref[0] & 3, ids_ref[1]
    for i in range(3):
        take_tile((3 * quarter + i) & 3, column, firsts, True, taken.at[i], sems.at[i])
    for i in range(3):
        span = slice(i * TILE, (i + 1) * TILE)
        pltpu.make_async_copy(firsts[0], taken.at[i], sems.at[i]).wait()
        for s in range(near_ref.shape[0]):
            total = near_ref[s, :, span].astype(jnp.float32) + far_ref[s, :, span].astype(jnp.float32)
            out_ref[s, :, span] = (total - dot_lanes(round_ref[s], taken[i])).astype(jnp.bfloat16)


def update_two(ids, near, far, rounded, firsts):
    order = rounded.shape[-1]
    return pl.pallas_call(
        update_two_kernel,
        out_shape=jax.ShapeDtypeStruct(near.shape, jnp.bfloat16),
        in_specs=[SMEM, VMEM, VMEM, VMEM] + [ANY] * 4,
        out_specs=VMEM,
        scratch_shapes=[pltpu.VMEM((3, TILE, order), jnp.bfloat16), pltpu.SemaphoreType.DMA((3,))],
        compiler_params=pltpu.CompilerParams(vmem_limit_bytes=56 * 2**20),
        cost_estimate=pl.CostEstimate(flops=2 * 10**9, bytes_accessed=10**7, transcendentals=0),
        name="update_two",
    )(ids, near, far, rounded, *firsts)


def over_square(pack, beside):
    half = pack.shape[0] // 2
    x, y, core = swapped(pack, "leaf", 1), swapped(pack, "front", 2), swapped(pack, "front", 1)
    x, y = lax.optimization_barrier((x, y, beside))[:2]
    top = swapped(y[:half], "leaf", 1)
    low = swapped(x[half:], "front", 2)
    x_core, y_core = swapped(x, "front", 1), swapped(y, "front", 1)
    top_core, low_core = swapped(top, "front", 1), swapped(low, "front", 1)
    return (pack, core, y, y_core, x, x_core, top, low, top_core, low_core)


def over_front(tile, y, *earlier):
    return (tile, swapped(tile, "front", 1), y, swapped(after(y, *earlier), "front", 1))


def after(value, *earlier):
    return lax.optimization_barrier((value, *earlier))[0]


def body(child_update, sep_one, sep_two, map_one, map_two, mask_one, mask_two):
    column = lax.axis_index("front")
    leaf = lax.axis_index("leaf")
    quad, quarter = leaf >> 2, leaf & 3
    ids = jnp.stack([leaf, column]).astype(jnp.int32)
    child = child_update[0, 0, 0]
    entries_one = sep_one[0, 0, 0]
    entries_two = sep_two[0, 0, 0]
    count = child.shape[0]
    order = GROUPS * TILE
    maps_one = map_one[:, 0]
    maps_two = map_two[:, 0]

    pivot_mine = pick_pivot(ids, maps_one, child, entries_one)
    coupling_mine, sep_send, near_send, far_send, sep_keep, near_keep, far_keep = pick_rest(
        ids, maps_one, maps_two, child, entries_one
    )
    packs = over_square(pivot_mine, coupling_mine)
    coupling_peer = swapped(after(coupling_mine, packs[4]), "leaf", 1)
    sep_peer = swapped(after(sep_send, packs[6]), "leaf", 1)
    far_peer = swapped(after(far_send, packs[6]), "leaf", 1)
    entries_far = swapped(entries_two[0], "leaf", 2)

    lower, inverse = cholesky(ids, packs, fill_one, order)
    factor_one, rounded, first, second, third = panel_one(
        ids, mask_one.reshape(-1), maps_two, coupling_mine, coupling_peer, lower, inverse
    )
    first_y = swapped(first, "front", 2)
    firsts = over_front(first, first_y, sep_peer)
    pivot_own, near_coupling, far_coupling = update_separator(ids, maps_two, sep_keep, sep_peer, rounded, firsts)
    second = jnp.where((leaf & 1) == (column & 1), second, swapped(third, "front", 1))
    second_y = swapped(after(second, first_y), "front", 2)
    seconds = over_front(second, second_y)

    pivot_far = swapped(pivot_own, "leaf", 2)
    pivot_tile = (
        pivot_own.astype(jnp.float32)
        + jnp.concatenate([pivot_far[:, TILE:], pivot_far[:, :TILE]], axis=1).astype(jnp.float32)
        + jnp.concatenate([entries_two[0], entries_far], axis=1).astype(jnp.float32)
    )
    far_trailing = update_trailing(
        ids, maps_two, far_keep, far_peer, after(rounded, pivot_far), firsts, seconds, (5, 6, 7)
    )
    packs = over_square(after(pivot_tile, far_peer), far_trailing)
    coupling_far = swapped(after(far_coupling, pivot_far), "leaf", 2)
    mask_second = lax.dynamic_index_in_dim(mask_two, quad, 0, keepdims=False).reshape(count, GROUPS, -1)
    mask_second = lax.dynamic_index_in_dim(mask_second, column, 1, keepdims=False)
    mask_second = lax.dynamic_index_in_dim(mask_second, quarter, 1, keepdims=False)
    coupling = (
        near_coupling.astype(jnp.float32)
        + coupling_far.astype(jnp.float32)
        + entries_two[1:].astype(jnp.float32) * mask_second.astype(jnp.float32)[:, None, None]
    ).reshape(count * TILE, TILE)
    coupling = after(coupling, packs[4])
    coupling_x, coupling_z, coupling_xz = (swapped(coupling, "leaf", mask) for mask in (1, 2, 3))
    trailing_far = swapped(after(far_trailing, packs[4]), "leaf", 2)
    near_peer = swapped(after(near_send, packs[6]), "leaf", 1)
    lower, inverse = cholesky(ids, packs, fill_two, order)
    factor_two, rounded_two, share = panel_two(
        ids, (coupling, coupling_x, coupling_z, coupling_xz), lower, inverse
    )
    near_trailing = update_trailing(ids, maps_two, near_keep, near_peer, rounded, firsts, seconds, (1, 2, 3))
    shares = over_front(share, swapped(share, "front", 2), near_peer, trailing_far)
    update = update_two(ids, near_trailing, trailing_far, rounded_two, shares)
    return (factor_one[None, None, None], factor_two[None, None, None], update[None, None, None])


def solution(mesh):
    split = P("leaf", "front", None, None, None, None)
    return jax.shard_map(
        body,
        mesh=mesh,
        in_specs=(split, split, split, P(), P(), P(), P()),
        out_specs=(split, split, split),
        check_vma=False,
    )
```

```python
import functools

import jax
import jax.numpy as jnp
from jax import lax
from jax.experimental import pallas as pl
from jax.experimental.pallas import tpu as pltpu
from jax.sharding import PartitionSpec as P

VMEM = pl.BlockSpec(memory_space=pltpu.VMEM)
SMEM = pl.BlockSpec(memory_space=pltpu.SMEM)
ANY = pl.BlockSpec(memory_space=pl.ANY)
GROUPS = 4
PARAMS = pltpu.CompilerParams(vmem_limit_bytes=32 * 2**20)
BLK = 128
GRP = 8
TILE = 256
NT = (((1,), (1,)), ((), ()))


def halves(x):
    high = x.astype(jnp.bfloat16)
    low = (x - high.astype(jnp.float32)).astype(jnp.bfloat16)
    return high, low


def left_parts(x):
    high, low = halves(x)
    return jnp.concatenate([high, low, high], axis=1)


def right_rows(x):
    high, low = halves(x)
    return jnp.concatenate([high, high, low], axis=0)


def right_lanes(x):
    high, low = halves(x)
    return jnp.concatenate([high, high, low], axis=1)


def dot_rows(left, right):
    return jnp.dot(left, right, preferred_element_type=jnp.float32)


def dot_lanes(left, right):
    return lax.dot_general(left, right, NT, preferred_element_type=jnp.float32)


def spread_row(ref, index):
    return jnp.broadcast_to(ref[index], (GRP, BLK))


def tree_sum(parts):
    while len(parts) > 1:
        parts = [parts[k] + parts[k + 1] for k in range(0, len(parts), 2)]
    return parts[0]


def factor_diagonal(block, done_ref, pivot_ref, rows_ref):
    steps = BLK // GRP
    row_id = lax.broadcasted_iota(jnp.int32, (GRP, BLK), 0)
    lane_id = lax.broadcasted_iota(jnp.int32, (GRP, BLK), 1)
    matrix = [block[GRP * g : GRP * (g + 1), :] for g in range(steps)]
    inverse = [jnp.where(lane_id == row_id + GRP * g, 1.0, 0.0).astype(jnp.float32) for g in range(steps)]
    for g in range(steps):
        first = GRP * g
        slot = g % 2
        current = matrix[g]
        rows_ref[slot, :, 0:BLK] = current
        rows_ref[slot, :, BLK:] = inverse[g]
        for i in range(GRP):
            pivot_ref[slot, i] = jnp.broadcast_to(current[:, first + i : first + i + 1], (GRP, BLK))
        entry = {}
        for m in range(GRP):
            for i in range(m + 1):
                entry[m, i] = jnp.broadcast_to(pivot_ref[slot, i, m : m + 1, :], (GRP, BLK))
                entry[i, m] = entry[m, i]
        left = [jnp.broadcast_to(rows_ref[slot, m : m + 1, 0:BLK], (GRP, BLK)) for m in range(GRP)]
        right = [jnp.broadcast_to(rows_ref[slot, m : m + 1, BLK:], (GRP, BLK)) for m in range(GRP)]
        for i in range(0, GRP, 2):
            n = i + 1
            a, b, c = entry[i, i], entry[n, i], entry[n, n]
            root = lax.rsqrt(a)
            root_both = lax.rsqrt(a * c - b * b)
            scale = root_both * root_both
            second_root = root * root_both

            def solve(x, y):
                return c * x - b * y, a * y - b * x

            solved = {}
            for name, rows_now in (("left", left), ("right", right)):
                raw = solve(rows_now[i], rows_now[n])
                lanes = slice(0, BLK) if name == "left" else slice(BLK, 2 * BLK)
                done_ref[first + i : first + i + 1, lanes] = (rows_now[i] * root)[0:1]
                done_ref[first + n : first + n + 1, lanes] = (raw[1] * second_root)[0:1]
                rows_now[i], rows_now[n] = raw[0] * scale, raw[1] * scale
            for col in range(i + 2, GRP):
                raw = solve(entry[i, col], entry[n, col])
                solved[col] = (raw[0] * scale, raw[1] * scale)
            for m in range(GRP):
                if m in (i, n):
                    continue
                weight, other = entry[m, i], entry[m, n]
                for rows_now in (left, right):
                    rows_now[m] = rows_now[m] - (weight * rows_now[i] + other * rows_now[n])
                for col in range(i + 2, GRP):
                    if m > col:
                        continue
                    entry[m, col] = entry[m, col] - (weight * solved[col][0] + other * solved[col][1])
            for m in range(i + 2, GRP):
                for col in range(i + 2, m):
                    entry[m, col] = entry[col, m]
            for col in range(i + 2, GRP):
                entry[i, col], entry[n, col] = solved[col]
        for later in range(g + 1, steps):
            rows = matrix[later]
            parts_left, parts_right = [], []
            for i in range(GRP):
                weight = jnp.broadcast_to(rows[:, first + i : first + i + 1], (GRP, BLK))
                parts_left.append(weight * left[i])
                parts_right.append(weight * right[i])
            matrix[later] = rows - tree_sum(parts_left)
            inverse[later] = inverse[later] - tree_sum(parts_right)


def fill_one(ids_ref, packs, work):
    leaf, column = ids_ref[0], ids_ref[1]
    half = leaf & 1
    order = work.shape[1]
    own, core, y, y_core, x, x_core = packs[:6]
    for apart, mine, peers in (
        (0, own, (x,)),
        (1, core, (x_core,)),
        (2, y, packs[6:8]),
        (3, y_core, packs[8:10]),
    ):
        base = (column ^ apart) * TILE
        height = TILE // len(peers)
        for part, peer in enumerate(peers):
            rows = pl.ds(pl.multiple_of(base + part * height, height), height)
            piece = slice(part * height, (part + 1) * height)
            work[rows, :] = mine[piece, 0:order].astype(jnp.float32) + peer[:, 0:order].astype(jnp.float32)
            for place, ref, span in ((half, mine, piece), (1 - half, peer, slice(None))):
                columns = pl.ds(pl.multiple_of(place * (order // 2), order // 2), order // 2)
                work[rows, columns] = work[rows, columns] + ref[span, order:].astype(jnp.float32)


def fill_two(ids_ref, packs, work):
    leaf, column = ids_ref[0], ids_ref[1]
    half, side = leaf & 1, (leaf >> 1) & 1
    own, core, y, y_core, x, x_core = packs[:6]
    for apart, mine, peers in (
        (0, own, (x,)),
        (1, core, (x_core,)),
        (2, y, packs[6:8]),
        (3, y_core, packs[8:10]),
    ):
        base = (column ^ apart) * TILE
        for refs, last in (((mine,), half), (peers, 1 - half)):
            height = TILE // len(refs)
            for part, ref in enumerate(refs):
                rows = pl.ds(pl.multiple_of(base + part * height, height), height)
                for position, place in ((0, 2 * side + last), (1, 2 * (1 - side) + last)):
                    columns = pl.ds(pl.multiple_of(place * TILE, TILE), TILE)
                    work[rows, columns] = ref[:, position * TILE : (position + 1) * TILE]


def cholesky_kernel(fill, ids_ref, *refs):
    packs = refs[:10]
    lower_ref, inverse_ref, work, done, block_inverse, entries, rows = refs[10:]
    order = work.shape[0]
    blocks = order // BLK
    fill(ids_ref, packs, work)
    lower_ref[...] = jnp.zeros_like(lower_ref)
    row_id = lax.broadcasted_iota(jnp.int32, (BLK, BLK), 0)
    lane_id = lax.broadcasted_iota(jnp.int32, (BLK, BLK), 1)

    def step(k, carry):
        start = pl.multiple_of(k * BLK, BLK)
        span = pl.ds(start, BLK)
        factor_diagonal(work[span, span], done, entries, rows)
        upper = jnp.where(lane_id >= row_id, done[:, 0:BLK], 0.0)
        lower_ref[span, span] = upper.T
        block_inverse[k] = done[:, BLK:]
        for fixed in range(blocks - 1):
            after = (fixed + 1) * BLK

            @pl.when(k == fixed)
            def _():
                strip = dot_rows(
                    left_parts(done[:, BLK:]), right_rows(work[after - BLK : after, after:])
                )
                column = strip.T
                lower_ref[after:, after - BLK : after] = column
                left = left_parts(column)
                right = right_rows(strip)
                width = order - after
                for top in range(0, width, TILE):
                    high = min(TILE, width - top)
                    work[after + top : after + top + high, after + top :] = work[
                        after + top : after + top + high, after + top :
                    ] - dot_rows(left[top : top + high], right[:, top:])

        return carry

    lax.fori_loop(0, blocks, step, 0)
    for tile in range(order // TILE):
        base = tile * TILE
        first, second = block_inverse[2 * tile], block_inverse[2 * tile + 1]
        corner = lower_ref[base + BLK : base + TILE, base : base + BLK]
        mixed = dot_rows(left_parts(corner), right_rows(first))
        mixed = -dot_rows(left_parts(second), right_rows(mixed))
        inverse_ref[tile, 0:BLK, 0:BLK] = first
        inverse_ref[tile, 0:BLK, BLK:] = jnp.zeros((BLK, BLK), jnp.float32)
        inverse_ref[tile, BLK:, 0:BLK] = mixed
        inverse_ref[tile, BLK:, BLK:] = second


def cholesky(ids, packs, fill, order):
    return pl.pallas_call(
        functools.partial(cholesky_kernel, fill),
        out_shape=(
            jax.ShapeDtypeStruct((order, order), jnp.float32),
            jax.ShapeDtypeStruct((order // TILE, TILE, TILE), jnp.float32),
        ),
        in_specs=[SMEM] + [VMEM] * len(packs),
        out_specs=(VMEM, VMEM),
        scratch_shapes=[
            pltpu.VMEM((order, order), jnp.float32),
            pltpu.VMEM((BLK, 2 * BLK), jnp.float32),
            pltpu.VMEM((order // BLK, BLK, BLK), jnp.float32),
            pltpu.VMEM((2, GRP, GRP, BLK), jnp.float32),
            pltpu.VMEM((2, GRP, 2 * BLK), jnp.float32),
        ],
        compiler_params=pltpu.CompilerParams(vmem_limit_bytes=32 * 2**20),
        cost_estimate=pl.CostEstimate(flops=4 * 10**10, bytes_accessed=10**8, transcendentals=0),
        name="cholesky",
    )(ids, *packs)


def swapped(value, axis, mask):
    pairs = [(source, source ^ mask) for source in range(lax.axis_size(axis))]
    return lax.ppermute(value, axis, pairs)


def swapped_heavy(value, mask):
    groups = lax.axis_size("front")
    pairs = [
        (leaf * groups + column, leaf * groups + (column ^ mask))
        for leaf in range(lax.axis_size("leaf"))
        for column in range(groups)
        if (leaf & 1) == (column & 1)
    ]
    return lax.ppermute(value, ("leaf", "front"), pairs)


def find_tile(map_ref, owner, group, slot, count):
    found = jnp.int32(-1)
    for s in range(count):
        found = jnp.where(map_ref[owner, group, s] == slot, jnp.int32(s), found)
    return found


def column_targets(half, side):
    targets = []
    for part in (side, 1 - side):
        targets.append(2 * part + half)
        targets += [4 + 3 * (2 * part + half) + i for i in range(3)]
    return targets


def share_place(target, half):
    place = jnp.int32(0)
    for other in column_targets(half, 0):
        earlier = jnp.logical_and((other & 3) == (target & 3), other < target)
        place = place + earlier.astype(jnp.int32)
    return place


def move_tile(live, source, target, sem):
    @pl.when(live)
    def _():
        pltpu.make_async_copy(source, target, sem).start()

    @pl.when(jnp.logical_not(live))
    def _():
        target[...] = jnp.zeros(target.shape, target.dtype)

    def wait():
        @pl.when(live)
        def _():
            pltpu.make_async_copy(source, target, sem).wait()

    return wait


def move_separator(leaf, column, map_ref, child_ref, slots, target_of, sems):
    count = child_ref.shape[0]
    waits = []
    for slot in slots:
        row = find_tile(map_ref, leaf, column, slot, count)
        for group in range(GROUPS):
            place = find_tile(map_ref, leaf, group, 0, count)
            live = jnp.logical_and(row >= 0, place >= 0)
            span = pl.ds(pl.multiple_of((jnp.maximum(place, 0) * GROUPS + group) * TILE, TILE), TILE)
            source = child_ref.at[jnp.maximum(row, 0), :, span]
            target = target_of(slot).at[:, pl.ds(group * TILE, TILE)]
            waits.append(move_tile(live, source, target, sems.at[len(waits)]))
    return waits


def pick_pivot_kernel(ids_ref, map_ref, child_ref, entries_ref, pivot_ref, sems, entry_sem):
    width = GROUPS * TILE
    entries = pltpu.make_async_copy(entries_ref.at[0], pivot_ref.at[:, pl.ds(width, width // 2)], entry_sem.at[0])
    entries.start()
    waits = move_separator(ids_ref[0], ids_ref[1], map_ref, child_ref, (0,), lambda slot: pivot_ref, sems)
    for wait in waits:
        wait()
    entries.wait()


def pick_pivot(ids, child_map, child, entries):
    width = GROUPS * TILE + entries.shape[-1]
    return pl.pallas_call(
        pick_pivot_kernel,
        out_shape=jax.ShapeDtypeStruct((TILE, width), child.dtype),
        in_specs=[SMEM, SMEM, ANY, ANY],
        out_specs=VMEM,
        scratch_shapes=[pltpu.SemaphoreType.DMA((GROUPS,)), pltpu.SemaphoreType.DMA((1,))],
        compiler_params=pltpu.CompilerParams(vmem_limit_bytes=56 * 2**20),
        name="pick_pivot",
    )(ids, child_map, child, entries)


def pick_rest_kernel(ids_ref, map_ref, next_ref, child_ref, entries_ref, coupling_ref, *refs):
    outs, (first_sems, sems, entry_sem) = refs[:6], refs[6:]
    count = child_ref.shape[0]
    width = GROUPS * TILE
    leaf, column = ids_ref[0], ids_ref[1]
    pair = leaf >> 1
    entries = pltpu.make_async_copy(
        entries_ref.at[pl.ds(1, count)], coupling_ref.at[:, :, pl.ds(width, width // 2)], entry_sem.at[0]
    )
    entries.start()
    slots = range(1, count + 1)
    waits = move_separator(
        leaf, column, map_ref, child_ref, slots, lambda slot: coupling_ref.at[slot - 1], first_sems
    )
    rows = [find_tile(map_ref, leaf, column, slot, count) for slot in slots]
    used = 0
    for which, device in enumerate((leaf ^ 1, leaf)):
        for position, target in enumerate(column_targets(device & 1, (device >> 1) & 1)):
            group = target & 3
            update = find_tile(next_ref, pair, group, target >> 2, count)
            place = find_tile(map_ref, leaf, group, update + 1, count)
            column_live = jnp.logical_and(update >= 0, place >= 0)
            source_span = pl.ds(pl.multiple_of((jnp.maximum(place, 0) * GROUPS + group) * TILE, TILE), TILE)
            for slot, row in enumerate(rows):
                live = jnp.logical_and(column_live, row >= 0)
                source = child_ref.at[jnp.maximum(row, 0), :, source_span]
                if position % 4 == 0:
                    goal = outs[3 * which].at[slot, :, pl.ds(position // 4 * TILE, TILE)]
                else:
                    goal = outs[3 * which + 1 + position // 4].at[slot, :, pl.ds((position % 4 - 1) * TILE, TILE)]
                waits.append(move_tile(live, source, goal, sems.at[used]))
                used += 1
    for wait in waits:
        wait()
    entries.wait()


def pick_rest(ids, child_map, next_map, child, entries):
    count = child.shape[0]
    wide = GROUPS * TILE + entries.shape[-1]
    widths = (wide,) + (2 * TILE, 3 * TILE, 3 * TILE) * 2
    return pl.pallas_call(
        pick_rest_kernel,
        out_shape=tuple(jax.ShapeDtypeStruct((count, TILE, width), child.dtype) for width in widths),
        in_specs=[SMEM, SMEM, SMEM, ANY, ANY],
        out_specs=(VMEM,) * 7,
        scratch_shapes=[
            pltpu.SemaphoreType.DMA((GROUPS * count,)),
            pltpu.SemaphoreType.DMA((16 * count,)),
            pltpu.SemaphoreType.DMA((1,)),
        ],
        compiler_params=pltpu.CompilerParams(vmem_limit_bytes=56 * 2**20),
        cost_estimate=pl.CostEstimate(flops=0, bytes_accessed=2 * 10**7, transcendentals=0),
        name="pick_rest",
    )(ids, child_map, next_map, child, entries)


def solve_blocks(coupling_ref, lower_ref, inverse_ref, panel_ref):
    order = lower_ref.shape[0]
    solved = []
    for k in range(order // TILE):
        span = slice(k * TILE, (k + 1) * TILE)
        rest = coupling_ref[:, span]
        if k:
            left = jnp.concatenate([part[0] for part in solved], axis=1)
            low = jnp.concatenate([part[1] for part in solved], axis=1)
            high_lower, low_lower = halves(lower_ref[span, 0 : k * TILE])
            rest = rest - dot_lanes(
                jnp.concatenate([left, low, left], axis=1),
                jnp.concatenate([high_lower, high_lower, low_lower], axis=1),
            )
        block = dot_lanes(left_parts(rest), right_lanes(inverse_ref[k]))
        panel_ref[:, span] = block
        solved.append(halves(block))
    return jnp.concatenate([part[0] for part in solved], axis=1)


def write_factor(column, offset, lower_ref, panel, factor_ref):
    width = factor_ref.shape[-1]
    rows = pl.ds(pl.multiple_of(column * TILE, TILE), TILE)
    span = pl.ds(pl.multiple_of(offset * width, width), width)
    factor_ref[0] = lower_ref[rows, span]
    for s in range(factor_ref.shape[0] - 1):
        factor_ref[s + 1] = panel[s * TILE : (s + 1) * TILE, span]


def panel_one_kernel(
    ids_ref, mask_ref, next_ref, mine_ref, peer_ref, lower_ref, inverse_ref, factor_ref, round_ref, first_ref, second_ref, third_ref, coupling, panel
):
    leaf, column = ids_ref[0], ids_ref[1]
    half, pair = leaf & 1, leaf >> 1
    count = mine_ref.shape[0]
    order = lower_ref.shape[0]
    for s in range(count):
        for tile in range(order // TILE):
            span = slice(tile * TILE, (tile + 1) * TILE)
            where = order + (tile % 2) * TILE
            weight = mask_ref[((pair * count + s) * GROUPS + column) * GROUPS + tile].astype(jnp.float32)
            mine = mine_ref[s, :, where : where + TILE].astype(jnp.float32)
            peer = peer_ref[s, :, where : where + TILE].astype(jnp.float32)
            own_first = half == tile // 2
            entry = jnp.where(own_first, mine, peer)
            coupling[s * TILE : (s + 1) * TILE, span] = (
                mine_ref[s, :, span].astype(jnp.float32) + peer_ref[s, :, span].astype(jnp.float32) + entry * weight
            )
    rounded = solve_blocks(coupling, lower_ref, inverse_ref, panel)
    for s in range(count):
        round_ref[s] = rounded[s * TILE : (s + 1) * TILE]
    write_factor(column, half, lower_ref, panel, factor_ref)
    heavy = half == (column & 1)
    for a, share_ref in ((0, first_ref), (jnp.where(heavy, 1, 0), second_ref), (2, third_ref)):
        slot = jnp.int32(0)
        for target in column_targets(half, 0):
            hit = jnp.logical_and((target & 3) == column, share_place(target, half) == a)
            slot = jnp.where(hit, target >> 2, slot)
        tile = find_tile(next_ref, pair, column, slot, count)
        share_ref[...] = round_ref[jnp.maximum(tile, 0)]


def panel_one(ids, mask, next_map, mine, peer, lower, inverse):
    count = mine.shape[0]
    order = lower.shape[0]
    return pl.pallas_call(
        panel_one_kernel,
        out_shape=(
            jax.ShapeDtypeStruct((count + 1, TILE, order // 2), jnp.float32),
            jax.ShapeDtypeStruct((count, TILE, order), jnp.bfloat16),
        )
        + (jax.ShapeDtypeStruct((TILE, order), jnp.bfloat16),) * 3,
        in_specs=[SMEM, SMEM, SMEM, VMEM, VMEM, VMEM, VMEM],
        out_specs=(VMEM,) * 5,
        scratch_shapes=[
            pltpu.VMEM((count * TILE, order), jnp.float32),
            pltpu.VMEM((count * TILE, order), jnp.float32),
        ],
        compiler_params=PARAMS,
        cost_estimate=pl.CostEstimate(flops=10**9, bytes_accessed=10**6, transcendentals=0),
        name="panel_one",
    )(ids, mask, next_map, mine, peer, lower, inverse)


def panel_two_kernel(ids_ref, own_ref, x_ref, z_ref, both_ref, lower_ref, inverse_ref, factor_ref, round_ref, share_ref, coupling, panel):
    leaf, column = ids_ref[0], ids_ref[1]
    half, side = leaf & 1, (leaf >> 1) & 1
    quarter = leaf & 3
    count = round_ref.shape[0]
    for place, ref in (
        (2 * side + half, own_ref),
        (2 * side + 1 - half, x_ref),
        (2 * (1 - side) + half, z_ref),
        (2 * (1 - side) + 1 - half, both_ref),
    ):
        coupling[:, pl.ds(pl.multiple_of(place * TILE, TILE), TILE)] = ref[...]
    rounded = solve_blocks(coupling, lower_ref, inverse_ref, panel)
    for s in range(count):
        round_ref[s] = rounded[s * TILE : (s + 1) * TILE]
    write_factor(column, quarter, lower_ref, panel, factor_ref)
    chosen = jnp.int32(0)
    for i in range(3):
        tile = 3 * quarter + i
        chosen = jnp.where((tile & 3) == column, tile >> 2, chosen)
    share_ref[...] = round_ref[chosen]


def panel_two(ids, parts, lower, inverse):
    rows = parts[0].shape[0]
    count = rows // TILE
    order = lower.shape[0]
    return pl.pallas_call(
        panel_two_kernel,
        out_shape=(
            jax.ShapeDtypeStruct((count + 1, TILE, order // 4), jnp.float32),
            jax.ShapeDtypeStruct((count, TILE, order), jnp.bfloat16),
            jax.ShapeDtypeStruct((TILE, order), jnp.bfloat16),
        ),
        in_specs=[SMEM] + [VMEM] * 6,
        out_specs=(VMEM, VMEM, VMEM),
        scratch_shapes=[pltpu.VMEM((rows, order), jnp.float32), pltpu.VMEM((rows, order), jnp.float32)],
        compiler_params=PARAMS,
        cost_estimate=pl.CostEstimate(flops=10**9, bytes_accessed=10**6, transcendentals=0),
        name="panel_two",
    )(ids, *parts, lower, inverse)


def take_tile(owner, column, refs, live, target, sem):
    for apart, ref in enumerate(refs):

        @pl.when(jnp.logical_and(live, (owner ^ column) == apart))
        def _():
            pltpu.make_async_copy(ref, target, sem).start()


def start_shared(ids_ref, positions, firsts, thirds, taken, sems):
    leaf, column = ids_ref[0], ids_ref[1]
    half, side = leaf & 1, (leaf >> 1) & 1
    targets = column_targets(half, side)
    copies = []
    for i, position in enumerate(positions):
        target = targets[position]
        group = target & 3
        place = share_place(target, half)
        take_tile(group, column, firsts, place < 2, taken.at[i], sems.at[i])
        if thirds:
            take_tile(group, column, thirds, place == 2, taken.at[i], sems.at[i])
        copies.append(pltpu.make_async_copy(firsts[0], taken.at[i], sems.at[i]))
    return copies


def update_columns(ids_ref, next_ref, positions, copies, keep_ref, peer_ref, round_ref, taken, tiles, write):
    leaf, column = ids_ref[0], ids_ref[1]
    half, side, pair = leaf & 1, (leaf >> 1) & 1, leaf >> 1
    count = keep_ref.shape[0]
    targets = column_targets(half, side)
    rows = [find_tile(next_ref, pair, column, slot, count) for slot in range(count + 1)]
    tiles[:, count] = jnp.zeros_like(tiles[:, count])
    for i, position in enumerate(positions):
        target = targets[position]
        live = find_tile(next_ref, pair, target & 3, target >> 2, count) >= 0
        span = slice(i * TILE, (i + 1) * TILE)
        copies[i].wait()
        for s in range(count):
            value = keep_ref[s, :, span].astype(jnp.float32) + peer_ref[s, :, span].astype(jnp.float32)
            value = value - dot_lanes(round_ref[s], taken[i])
            tiles[i, s] = jnp.where(live, value, 0.0).astype(jnp.bfloat16)
        for slot, row in enumerate(rows):
            write(i, slot, lambda row=row: tiles[i, jnp.where(row < 0, count, row)])


def update_separator_kernel(
    ids_ref, next_ref, keep_ref, peer_ref, round_ref, *refs
):
    firsts, (pivot_ref, near_ref, far_ref, taken, tiles, sems) = refs[:4], refs[4:]

    def write(i, slot, tile):
        if slot == 0:
            pivot_ref[:, i * TILE : (i + 1) * TILE] = tile()
        else:
            (near_ref, far_ref)[i][slot - 1] = tile()

    copies = start_shared(ids_ref, (0, 4), firsts, (), taken, sems)
    update_columns(ids_ref, next_ref, (0, 4), copies, keep_ref, peer_ref, round_ref, taken, tiles, write)


def update_separator(ids, next_map, keep, peer, rounded, firsts):
    count, _, order = rounded.shape
    tile = jax.ShapeDtypeStruct((count, TILE, TILE), jnp.bfloat16)
    return pl.pallas_call(
        update_separator_kernel,
        out_shape=(jax.ShapeDtypeStruct((TILE, 2 * TILE), jnp.bfloat16), tile, tile),
        in_specs=[SMEM, SMEM, VMEM, VMEM, VMEM] + [ANY] * 4,
        out_specs=(VMEM, VMEM, VMEM),
        scratch_shapes=[
            pltpu.VMEM((2, TILE, order), jnp.bfloat16),
            pltpu.VMEM((2, count + 1, TILE, TILE), jnp.bfloat16),
            pltpu.SemaphoreType.DMA((2,)),
        ],
        compiler_params=pltpu.CompilerParams(vmem_limit_bytes=56 * 2**20),
        cost_estimate=pl.CostEstimate(flops=10**8, bytes_accessed=10**5, transcendentals=0),
        name="update_separator",
    )(ids, next_map, keep, peer, rounded, *firsts)


def update_trailing_kernel(
    positions, ids_ref, next_ref, keep_ref, peer_ref, round_ref, *refs
):
    seconds, thirds, (out_ref, taken, tiles, sems) = refs[:4], refs[4:8], refs[8:]

    def write(i, slot, tile):
        if slot:
            out_ref[slot - 1, :, i * TILE : (i + 1) * TILE] = tile()

    copies = start_shared(ids_ref, positions, seconds, thirds, taken, sems)
    update_columns(ids_ref, next_ref, positions, copies, keep_ref, peer_ref, round_ref, taken, tiles, write)


def update_trailing(ids, next_map, keep, peer, rounded, seconds, thirds, positions):
    count, _, order = rounded.shape
    width = len(positions)
    return pl.pallas_call(
        functools.partial(update_trailing_kernel, positions),
        out_shape=jax.ShapeDtypeStruct((count, TILE, width * TILE), jnp.bfloat16),
        in_specs=[SMEM, SMEM, VMEM, VMEM, VMEM] + [ANY] * 8,
        out_specs=VMEM,
        scratch_shapes=[
            pltpu.VMEM((width, TILE, order), jnp.bfloat16),
            pltpu.VMEM((width, count + 1, TILE, TILE), jnp.bfloat16),
            pltpu.SemaphoreType.DMA((width,)),
        ],
        compiler_params=pltpu.CompilerParams(vmem_limit_bytes=56 * 2**20),
        cost_estimate=pl.CostEstimate(flops=4 * 10**9, bytes_accessed=12 * 10**6, transcendentals=0),
        name="update_trailing",
    )(ids, next_map, keep, peer, rounded, *seconds, *thirds)


def update_two_kernel(ids_ref, near_ref, far_ref, round_ref, *refs):
    firsts, (out_ref, taken, sems) = refs[:4], refs[4:]
    quarter, column = ids_ref[0] & 3, ids_ref[1]
    for i in range(3):
        take_tile((3 * quarter + i) & 3, column, firsts, True, taken.at[i], sems.at[i])
    for i in range(3):
        span = slice(i * TILE, (i + 1) * TILE)
        pltpu.make_async_copy(firsts[0], taken.at[i], sems.at[i]).wait()
        for s in range(near_ref.shape[0]):
            total = near_ref[s, :, span].astype(jnp.float32) + far_ref[s, :, span].astype(jnp.float32)
            out_ref[s, :, span] = (total - dot_lanes(round_ref[s], taken[i])).astype(jnp.bfloat16)


def update_two(ids, near, far, rounded, firsts):
    order = rounded.shape[-1]
    return pl.pallas_call(
        update_two_kernel,
        out_shape=jax.ShapeDtypeStruct(near.shape, jnp.bfloat16),
        in_specs=[SMEM, VMEM, VMEM, VMEM] + [ANY] * 4,
        out_specs=VMEM,
        scratch_shapes=[pltpu.VMEM((3, TILE, order), jnp.bfloat16), pltpu.SemaphoreType.DMA((3,))],
        compiler_params=pltpu.CompilerParams(vmem_limit_bytes=56 * 2**20),
        cost_estimate=pl.CostEstimate(flops=2 * 10**9, bytes_accessed=10**7, transcendentals=0),
        name="update_two",
    )(ids, near, far, rounded, *firsts)


def over_square(pack, beside):
    half = pack.shape[0] // 2
    x, y, core = swapped(pack, "leaf", 1), swapped(pack, "front", 2), swapped(pack, "front", 1)
    x, y = lax.optimization_barrier((x, y, beside))[:2]
    top = swapped(y[:half], "leaf", 1)
    low = swapped(x[half:], "front", 2)
    x_core, y_core = swapped(x, "front", 1), swapped(y, "front", 1)
    top_core, low_core = swapped(top, "front", 1), swapped(low, "front", 1)
    return (pack, core, y, y_core, x, x_core, top, low, top_core, low_core)


def over_front(tile, y, *earlier):
    return (tile, swapped(tile, "front", 1), y, swapped(after(y, *earlier), "front", 1))


def over_heavy(tile, y, *earlier):
    return (tile, swapped_heavy(tile, 1), y, swapped_heavy(after(y, *earlier), 1))


def after(value, *earlier):
    return lax.optimization_barrier((value, *earlier))[0]


def body(child_update, sep_one, sep_two, map_one, map_two, mask_one, mask_two):
    column = lax.axis_index("front")
    leaf = lax.axis_index("leaf")
    quad, quarter = leaf >> 2, leaf & 3
    ids = jnp.stack([leaf, column]).astype(jnp.int32)
    child = child_update[0, 0, 0]
    entries_one = sep_one[0, 0, 0]
    entries_two = sep_two[0, 0, 0]
    count = child.shape[0]
    order = GROUPS * TILE
    maps_one = map_one[:, 0]
    maps_two = map_two[:, 0]

    pivot_mine = pick_pivot(ids, maps_one, child, entries_one)
    coupling_mine, sep_send, near_send, far_send, sep_keep, near_keep, far_keep = pick_rest(
        ids, maps_one, maps_two, child, entries_one
    )
    packs = over_square(pivot_mine, coupling_mine)
    coupling_peer = swapped(after(coupling_mine, packs[4]), "leaf", 1)
    sep_peer = swapped(after(sep_send, packs[6]), "leaf", 1)
    far_peer = swapped(after(far_send, packs[6]), "leaf", 1)
    entries_far = swapped(entries_two[0], "leaf", 2)

    lower, inverse = cholesky(ids, packs, fill_one, order)
    factor_one, rounded, first, second, third = panel_one(
        ids, mask_one.reshape(-1), maps_two, coupling_mine, coupling_peer, lower, inverse
    )
    first_y = swapped_heavy(first, 2)
    firsts = over_heavy(first, first_y, sep_peer)
    pivot_own, near_coupling, far_coupling = update_separator(ids, maps_two, sep_keep, sep_peer, rounded, firsts)
    second_y = swapped(after(second, first_y), "front", 2)
    seconds = over_front(second, second_y)
    thirds = over_heavy(third, swapped_heavy(after(third, first_y), 2))

    pivot_far = swapped(pivot_own, "leaf", 2)
    pivot_tile = (
        pivot_own.astype(jnp.float32)
        + jnp.concatenate([pivot_far[:, TILE:], pivot_far[:, :TILE]], axis=1).astype(jnp.float32)
        + jnp.concatenate([entries_two[0], entries_far], axis=1).astype(jnp.float32)
    )
    far_trailing = update_trailing(
        ids, maps_two, far_keep, far_peer, after(rounded, pivot_far), seconds, thirds, (5, 6, 7)
    )
    packs = over_square(after(pivot_tile, far_peer), far_trailing)
    coupling_far = swapped(after(far_coupling, pivot_far), "leaf", 2)
    mask_second = lax.dynamic_index_in_dim(mask_two, quad, 0, keepdims=False).reshape(count, GROUPS, -1)
    mask_second = lax.dynamic_index_in_dim(mask_second, column, 1, keepdims=False)
    mask_second = lax.dynamic_index_in_dim(mask_second, quarter, 1, keepdims=False)
    coupling = (
        near_coupling.astype(jnp.float32)
        + coupling_far.astype(jnp.float32)
        + entries_two[1:].astype(jnp.float32) * mask_second.astype(jnp.float32)[:, None, None]
    ).reshape(count * TILE, TILE)
    coupling = after(coupling, packs[4])
    coupling_x, coupling_z, coupling_xz = (swapped(coupling, "leaf", mask) for mask in (1, 2, 3))
    trailing_far = swapped(after(far_trailing, packs[4]), "leaf", 2)
    near_peer = swapped(after(near_send, packs[6]), "leaf", 1)
    lower, inverse = cholesky(ids, packs, fill_two, order)
    factor_two, rounded_two, share = panel_two(
        ids, (coupling, coupling_x, coupling_z, coupling_xz), lower, inverse
    )
    near_trailing = update_trailing(ids, maps_two, near_keep, near_peer, rounded, seconds, thirds, (1, 2, 3))
    shares = over_front(share, swapped(share, "front", 2), near_trailing, trailing_far)
    update = update_two(ids, near_trailing, trailing_far, rounded_two, shares)
    return (factor_one[None, None, None], factor_two[None, None, None], update[None, None, None])


def solution(mesh):
    split = P("leaf", "front", None, None, None, None)
    return jax.shard_map(
        body,
        mesh=mesh,
        in_specs=(split, split, split, P(), P(), P(), P()),
        out_specs=(split, split, split),
        check_vma=False,
    )
```

```python
import functools

import jax
import jax.numpy as jnp
from jax import lax
from jax.experimental import pallas as pl
from jax.experimental.pallas import tpu as pltpu
from jax.sharding import PartitionSpec as P

VMEM = pl.BlockSpec(memory_space=pltpu.VMEM)
SMEM = pl.BlockSpec(memory_space=pltpu.SMEM)
ANY = pl.BlockSpec(memory_space=pl.ANY)
GROUPS = 4
PARAMS = pltpu.CompilerParams(vmem_limit_bytes=32 * 2**20)
BLK = 128
GRP = 8
TILE = 256
NT = (((1,), (1,)), ((), ()))


def halves(x):
    high = x.astype(jnp.bfloat16)
    low = (x - high.astype(jnp.float32)).astype(jnp.bfloat16)
    return high, low


def left_parts(x):
    high, low = halves(x)
    return jnp.concatenate([high, low, high], axis=1)


def right_rows(x):
    high, low = halves(x)
    return jnp.concatenate([high, high, low], axis=0)


def right_lanes(x):
    high, low = halves(x)
    return jnp.concatenate([high, high, low], axis=1)


def dot_rows(left, right):
    return jnp.dot(left, right, preferred_element_type=jnp.float32)


def dot_lanes(left, right):
    return lax.dot_general(left, right, NT, preferred_element_type=jnp.float32)


def spread_row(ref, index):
    return jnp.broadcast_to(ref[index], (GRP, BLK))


def tree_sum(parts):
    while len(parts) > 1:
        parts = [parts[k] + parts[k + 1] for k in range(0, len(parts), 2)]
    return parts[0]


def factor_diagonal(block, done_ref, pivot_ref, rows_ref):
    steps = BLK // GRP
    row_id = lax.broadcasted_iota(jnp.int32, (GRP, BLK), 0)
    lane_id = lax.broadcasted_iota(jnp.int32, (GRP, BLK), 1)
    matrix = [block[GRP * g : GRP * (g + 1), :] for g in range(steps)]
    inverse = [jnp.where(lane_id == row_id + GRP * g, 1.0, 0.0).astype(jnp.float32) for g in range(steps)]
    for g in range(steps):
        first = GRP * g
        slot = g % 2
        current = matrix[g]
        rows_ref[slot, :, 0:BLK] = current
        rows_ref[slot, :, BLK:] = inverse[g]
        for i in range(GRP):
            pivot_ref[slot, i] = jnp.broadcast_to(current[:, first + i : first + i + 1], (GRP, BLK))
        entry = {}
        for m in range(GRP):
            for i in range(m + 1):
                entry[m, i] = jnp.broadcast_to(pivot_ref[slot, i, m : m + 1, :], (GRP, BLK))
                entry[i, m] = entry[m, i]
        left = [jnp.broadcast_to(rows_ref[slot, m : m + 1, 0:BLK], (GRP, BLK)) for m in range(GRP)]
        right = [jnp.broadcast_to(rows_ref[slot, m : m + 1, BLK:], (GRP, BLK)) for m in range(GRP)]
        for i in range(0, GRP, 2):
            n = i + 1
            a, b, c = entry[i, i], entry[n, i], entry[n, n]
            root = lax.rsqrt(a)
            root_both = lax.rsqrt(a * c - b * b)
            scale = root_both * root_both
            second_root = root * root_both

            def solve(x, y):
                return c * x - b * y, a * y - b * x

            solved = {}
            for name, rows_now in (("left", left), ("right", right)):
                raw = solve(rows_now[i], rows_now[n])
                lanes = slice(0, BLK) if name == "left" else slice(BLK, 2 * BLK)
                done_ref[first + i : first + i + 1, lanes] = (rows_now[i] * root)[0:1]
                done_ref[first + n : first + n + 1, lanes] = (raw[1] * second_root)[0:1]
                rows_now[i], rows_now[n] = raw[0] * scale, raw[1] * scale
            for col in range(i + 2, GRP):
                raw = solve(entry[i, col], entry[n, col])
                solved[col] = (raw[0] * scale, raw[1] * scale)
            for m in range(GRP):
                if m in (i, n):
                    continue
                weight, other = entry[m, i], entry[m, n]
                for rows_now in (left, right):
                    rows_now[m] = rows_now[m] - (weight * rows_now[i] + other * rows_now[n])
                for col in range(i + 2, GRP):
                    if m > col:
                        continue
                    entry[m, col] = entry[m, col] - (weight * solved[col][0] + other * solved[col][1])
            for m in range(i + 2, GRP):
                for col in range(i + 2, m):
                    entry[m, col] = entry[col, m]
            for col in range(i + 2, GRP):
                entry[i, col], entry[n, col] = solved[col]
        for later in range(g + 1, steps):
            rows = matrix[later]
            parts_left, parts_right = [], []
            for i in range(GRP):
                weight = jnp.broadcast_to(rows[:, first + i : first + i + 1], (GRP, BLK))
                parts_left.append(weight * left[i])
                parts_right.append(weight * right[i])
            matrix[later] = rows - tree_sum(parts_left)
            inverse[later] = inverse[later] - tree_sum(parts_right)


def fill_one(ids_ref, packs, work):
    leaf, column = ids_ref[0], ids_ref[1]
    half = leaf & 1
    order = work.shape[1]
    own, core, y, y_core, x, x_core = packs[:6]
    for apart, mine, peers in (
        (0, own, (x,)),
        (1, core, (x_core,)),
        (2, y, packs[6:8]),
        (3, y_core, packs[8:10]),
    ):
        base = (column ^ apart) * TILE
        height = TILE // len(peers)
        for part, peer in enumerate(peers):
            rows = pl.ds(pl.multiple_of(base + part * height, height), height)
            piece = slice(part * height, (part + 1) * height)
            work[rows, :] = mine[piece, 0:order].astype(jnp.float32) + peer[:, 0:order].astype(jnp.float32)
            for place, ref, span in ((half, mine, piece), (1 - half, peer, slice(None))):
                columns = pl.ds(pl.multiple_of(place * (order // 2), order // 2), order // 2)
                work[rows, columns] = work[rows, columns] + ref[span, order:].astype(jnp.float32)


def fill_two(ids_ref, packs, work):
    leaf, column = ids_ref[0], ids_ref[1]
    half, side = leaf & 1, (leaf >> 1) & 1
    own, core, y, y_core, x, x_core = packs[:6]
    for apart, mine, peers in (
        (0, own, (x,)),
        (1, core, (x_core,)),
        (2, y, packs[6:8]),
        (3, y_core, packs[8:10]),
    ):
        base = (column ^ apart) * TILE
        for refs, last in (((mine,), half), (peers, 1 - half)):
            height = TILE // len(refs)
            for part, ref in enumerate(refs):
                rows = pl.ds(pl.multiple_of(base + part * height, height), height)
                for position, place in ((0, 2 * side + last), (1, 2 * (1 - side) + last)):
                    columns = pl.ds(pl.multiple_of(place * TILE, TILE), TILE)
                    work[rows, columns] = ref[:, position * TILE : (position + 1) * TILE]


def eliminate(work, lower_ref, inverse_ref, done, block_inverse, entries, rows):
    order = work.shape[0]
    blocks = lower_ref.shape[1] // BLK
    lower_ref[...] = jnp.zeros_like(lower_ref)
    row_id = lax.broadcasted_iota(jnp.int32, (BLK, BLK), 0)
    lane_id = lax.broadcasted_iota(jnp.int32, (BLK, BLK), 1)

    def step(k, carry):
        start = pl.multiple_of(k * BLK, BLK)
        span = pl.ds(start, BLK)
        factor_diagonal(work[span, span], done, entries, rows)
        upper = jnp.where(lane_id >= row_id, done[:, 0:BLK], 0.0)
        lower_ref[span, span] = upper.T
        block_inverse[k] = done[:, BLK:]
        for fixed in range(blocks):
            after = (fixed + 1) * BLK
            if after == order:
                continue

            @pl.when(k == fixed)
            def _():
                strip = dot_rows(
                    left_parts(done[:, BLK:]), right_rows(work[after - BLK : after, after:])
                )
                column = strip.T
                lower_ref[after:, after - BLK : after] = column
                left = left_parts(column)
                right = right_rows(strip)
                width = order - after
                for top in range(0, width, TILE):
                    high = min(TILE, width - top)
                    work[after + top : after + top + high, after + top :] = work[
                        after + top : after + top + high, after + top :
                    ] - dot_rows(left[top : top + high], right[:, top:])

        return carry

    lax.fori_loop(0, blocks, step, 0)
    for tile in range(blocks * BLK // TILE):
        base = tile * TILE
        first, second = block_inverse[2 * tile], block_inverse[2 * tile + 1]
        corner = lower_ref[base + BLK : base + TILE, base : base + BLK]
        mixed = dot_rows(left_parts(corner), right_rows(first))
        mixed = -dot_rows(left_parts(second), right_rows(mixed))
        inverse_ref[tile, 0:BLK, 0:BLK] = first
        inverse_ref[tile, 0:BLK, BLK:] = jnp.zeros((BLK, BLK), jnp.float32)
        inverse_ref[tile, BLK:, 0:BLK] = mixed
        inverse_ref[tile, BLK:, BLK:] = second


def cholesky_first_kernel(fill, ids_ref, *refs):
    packs = refs[:10]
    lower_ref, inverse_ref, rest_ref, work, *scratch = refs[10:]
    fill(ids_ref, packs, work)
    eliminate(work, lower_ref, inverse_ref, *scratch)
    done = lower_ref.shape[1]
    rest_ref[...] = work[done:, done:]


def cholesky_second_kernel(rest_ref, lower_ref, inverse_ref, work, *scratch):
    work[...] = rest_ref[...]
    eliminate(work, lower_ref, inverse_ref, *scratch)


def elimination_scratch(order, blocks):
    return [
        pltpu.VMEM((order, order), jnp.float32),
        pltpu.VMEM((BLK, 2 * BLK), jnp.float32),
        pltpu.VMEM((blocks, BLK, BLK), jnp.float32),
        pltpu.VMEM((2, GRP, GRP, BLK), jnp.float32),
        pltpu.VMEM((2, GRP, 2 * BLK), jnp.float32),
    ]


def cholesky_first(ids, packs, fill, order):
    done = order // 2
    return pl.pallas_call(
        functools.partial(cholesky_first_kernel, fill),
        out_shape=(
            jax.ShapeDtypeStruct((order, done), jnp.float32),
            jax.ShapeDtypeStruct((done // TILE, TILE, TILE), jnp.float32),
            jax.ShapeDtypeStruct((order - done, order - done), jnp.float32),
        ),
        in_specs=[SMEM] + [VMEM] * len(packs),
        out_specs=(VMEM,) * 3,
        scratch_shapes=elimination_scratch(order, done // BLK),
        compiler_params=pltpu.CompilerParams(vmem_limit_bytes=32 * 2**20),
        cost_estimate=pl.CostEstimate(flops=2 * 10**10, bytes_accessed=5 * 10**7, transcendentals=0),
        name="cholesky_first",
    )(ids, *packs)


def cholesky_second(rest):
    order = rest.shape[0]
    return pl.pallas_call(
        cholesky_second_kernel,
        out_shape=(
            jax.ShapeDtypeStruct((order, order), jnp.float32),
            jax.ShapeDtypeStruct((order // TILE, TILE, TILE), jnp.float32),
        ),
        in_specs=[VMEM],
        out_specs=(VMEM,) * 2,
        scratch_shapes=elimination_scratch(order, order // BLK),
        compiler_params=pltpu.CompilerParams(vmem_limit_bytes=24 * 2**20),
        cost_estimate=pl.CostEstimate(flops=2 * 10**10, bytes_accessed=5 * 10**7, transcendentals=0),
        name="cholesky_second",
    )(rest)


def swapped(value, axis, mask):
    pairs = [(source, source ^ mask) for source in range(lax.axis_size(axis))]
    return lax.ppermute(value, axis, pairs)


def swapped_heavy(value, mask):
    groups = lax.axis_size("front")
    pairs = [
        (leaf * groups + column, leaf * groups + (column ^ mask))
        for leaf in range(lax.axis_size("leaf"))
        for column in range(groups)
        if (leaf & 1) == (column & 1)
    ]
    return lax.ppermute(value, ("leaf", "front"), pairs)


def find_tile(map_ref, owner, group, slot, count):
    found = jnp.int32(-1)
    for s in range(count):
        found = jnp.where(map_ref[owner, group, s] == slot, jnp.int32(s), found)
    return found


def column_targets(half, side):
    targets = []
    for part in (side, 1 - side):
        targets.append(2 * part + half)
        targets += [4 + 3 * (2 * part + half) + i for i in range(3)]
    return targets


def share_place(target, half):
    place = jnp.int32(0)
    for other in column_targets(half, 0):
        earlier = jnp.logical_and((other & 3) == (target & 3), other < target)
        place = place + earlier.astype(jnp.int32)
    return place


def move_tile(live, source, target, sem):
    @pl.when(live)
    def _():
        pltpu.make_async_copy(source, target, sem).start()

    @pl.when(jnp.logical_not(live))
    def _():
        target[...] = jnp.zeros(target.shape, target.dtype)

    def wait():
        @pl.when(live)
        def _():
            pltpu.make_async_copy(source, target, sem).wait()

    return wait


def move_separator(leaf, column, map_ref, child_ref, slots, groups, target_of, sems):
    count = child_ref.shape[0]
    waits = []
    for slot in slots:
        row = find_tile(map_ref, leaf, column, slot, count)
        for position, group in enumerate(groups):
            place = find_tile(map_ref, leaf, group, 0, count)
            live = jnp.logical_and(row >= 0, place >= 0)
            span = pl.ds(pl.multiple_of((jnp.maximum(place, 0) * GROUPS + group) * TILE, TILE), TILE)
            source = child_ref.at[jnp.maximum(row, 0), :, span]
            target = target_of(slot, position)
            waits.append(move_tile(live, source, target, sems.at[len(waits)]))
    return waits


def pick_pivot_kernel(ids_ref, map_ref, child_ref, entries_ref, pivot_ref, sems, entry_sem):
    width = GROUPS * TILE
    entries = pltpu.make_async_copy(entries_ref.at[0], pivot_ref.at[:, pl.ds(width, width // 2)], entry_sem.at[0])
    entries.start()
    waits = move_separator(
        ids_ref[0], ids_ref[1], map_ref, child_ref, (0,), range(GROUPS),
        lambda slot, position: pivot_ref.at[:, pl.ds(position * TILE, TILE)], sems,
    )
    for wait in waits:
        wait()
    entries.wait()


def pick_pivot(ids, child_map, child, entries):
    width = GROUPS * TILE + entries.shape[-1]
    return pl.pallas_call(
        pick_pivot_kernel,
        out_shape=jax.ShapeDtypeStruct((TILE, width), child.dtype),
        in_specs=[SMEM, SMEM, ANY, ANY],
        out_specs=VMEM,
        scratch_shapes=[pltpu.SemaphoreType.DMA((GROUPS,)), pltpu.SemaphoreType.DMA((1,))],
        compiler_params=pltpu.CompilerParams(vmem_limit_bytes=56 * 2**20),
        name="pick_pivot",
    )(ids, child_map, child, entries)


def pick_rest_kernel(ids_ref, map_ref, next_ref, child_ref, *refs):
    halves_out, outs, (first_sems, sems) = refs[:2], refs[2:8], refs[8:]
    count = child_ref.shape[0]
    leaf, column = ids_ref[0], ids_ref[1]
    half, pair = leaf & 1, leaf >> 1
    slots = range(1, count + 1)
    groups = (2 * (1 - half), 2 * (1 - half) + 1, 2 * half, 2 * half + 1)
    waits = move_separator(
        leaf, column, map_ref, child_ref, slots, groups,
        lambda slot, position: halves_out[position // 2].at[slot - 1, :, pl.ds(position % 2 * TILE, TILE)],
        first_sems,
    )
    rows = [find_tile(map_ref, leaf, column, slot, count) for slot in slots]
    used = 0
    for which, device in enumerate((leaf ^ 1, leaf)):
        for position, target in enumerate(column_targets(device & 1, (device >> 1) & 1)):
            group = target & 3
            update = find_tile(next_ref, pair, group, target >> 2, count)
            place = find_tile(map_ref, leaf, group, update + 1, count)
            column_live = jnp.logical_and(update >= 0, place >= 0)
            source_span = pl.ds(pl.multiple_of((jnp.maximum(place, 0) * GROUPS + group) * TILE, TILE), TILE)
            for slot, row in enumerate(rows):
                live = jnp.logical_and(column_live, row >= 0)
                source = child_ref.at[jnp.maximum(row, 0), :, source_span]
                if position % 4 == 0:
                    goal = outs[3 * which].at[slot, :, pl.ds(position // 4 * TILE, TILE)]
                else:
                    goal = outs[3 * which + 1 + position // 4].at[slot, :, pl.ds((position % 4 - 1) * TILE, TILE)]
                waits.append(move_tile(live, source, goal, sems.at[used]))
                used += 1
    for wait in waits:
        wait()


def pick_rest(ids, child_map, next_map, child):
    count = child.shape[0]
    widths = (2 * TILE, 2 * TILE) + (2 * TILE, 3 * TILE, 3 * TILE) * 2
    return pl.pallas_call(
        pick_rest_kernel,
        out_shape=tuple(jax.ShapeDtypeStruct((count, TILE, width), child.dtype) for width in widths),
        in_specs=[SMEM, SMEM, SMEM, ANY],
        out_specs=(VMEM,) * 8,
        scratch_shapes=[pltpu.SemaphoreType.DMA((GROUPS * count,)), pltpu.SemaphoreType.DMA((16 * count,))],
        compiler_params=pltpu.CompilerParams(vmem_limit_bytes=56 * 2**20),
        cost_estimate=pl.CostEstimate(flops=0, bytes_accessed=2 * 10**7, transcendentals=0),
        name="pick_rest",
    )(ids, child_map, next_map, child)


def solve_blocks(coupling_ref, lowers, inverses, panel_ref):
    split = lowers[0].shape[1]
    solved = []
    for k in range(panel_ref.shape[1] // TILE):
        span = slice(k * TILE, (k + 1) * TILE)
        rest = coupling_ref[:, span]
        if k:
            left = jnp.concatenate([part[0] for part in solved], axis=1)
            low = jnp.concatenate([part[1] for part in solved], axis=1)
            strip = lowers[0][span, 0 : min(k * TILE, split)]
            if k * TILE > split:
                inner = slice(k * TILE - split, (k + 1) * TILE - split)
                strip = jnp.concatenate([strip, lowers[1][inner, 0 : k * TILE - split]], axis=1)
            high_lower, low_lower = halves(strip)
            rest = rest - dot_lanes(
                jnp.concatenate([left, low, left], axis=1),
                jnp.concatenate([high_lower, high_lower, low_lower], axis=1),
            )
        tiles = split // TILE
        inverse = inverses[0][k] if k < tiles else inverses[1][k - tiles]
        block = dot_lanes(left_parts(rest), right_lanes(inverse))
        panel_ref[:, span] = block
        solved.append(halves(block))
    return jnp.concatenate([part[0] for part in solved], axis=1)


def write_factor(column, offset, lowers, panel, factor_ref):
    width = factor_ref.shape[-1]
    split = lowers[0].shape[1]
    per = split // width
    tiles = split // TILE
    span = pl.ds(pl.multiple_of(offset * width, width), width)
    factor_ref[0] = jnp.zeros(factor_ref.shape[1:], factor_ref.dtype)

    @pl.when(offset < per)
    def _():
        inner = pl.ds(pl.multiple_of(jnp.minimum(offset, per - 1) * width, width), width)
        factor_ref[0] = lowers[0][pl.ds(pl.multiple_of(column * TILE, TILE), TILE), inner]

    @pl.when(jnp.logical_and(offset >= per, column >= tiles))
    def _():
        inner = pl.ds(pl.multiple_of(jnp.maximum(offset - per, 0) * width, width), width)
        rows = pl.ds(pl.multiple_of(jnp.maximum(column - tiles, 0) * TILE, TILE), TILE)
        factor_ref[0] = lowers[1][rows, inner]

    for s in range(factor_ref.shape[0] - 1):
        factor_ref[s + 1] = panel[s * TILE : (s + 1) * TILE, span]


def panel_one_kernel(ids_ref, next_ref, mine_ref, peer_ref, *refs):
    lowers, inverses = refs[:2], refs[2:4]
    factor_ref, round_ref, first_ref, second_ref, third_ref, coupling, panel = refs[4:]
    leaf, column = ids_ref[0], ids_ref[1]
    half, pair = leaf & 1, leaf >> 1
    count, _, width = mine_ref.shape
    for ref, place in ((mine_ref, half), (peer_ref, 1 - half)):
        span = pl.ds(pl.multiple_of(place * width, width), width)
        for s in range(count):
            coupling[s * TILE : (s + 1) * TILE, span] = ref[s].astype(jnp.float32)
    rounded = solve_blocks(coupling, lowers, inverses, panel)
    for s in range(count):
        round_ref[s] = rounded[s * TILE : (s + 1) * TILE]
    write_factor(column, half, lowers, panel, factor_ref)
    heavy = half == (column & 1)
    for a, share_ref in ((0, first_ref), (jnp.where(heavy, 1, 0), second_ref), (2, third_ref)):
        slot = jnp.int32(0)
        for target in column_targets(half, 0):
            hit = jnp.logical_and((target & 3) == column, share_place(target, half) == a)
            slot = jnp.where(hit, target >> 2, slot)
        tile = find_tile(next_ref, pair, column, slot, count)
        share_ref[...] = round_ref[jnp.maximum(tile, 0)]


def panel_one(ids, next_map, mine, peer, lowers, inverses):
    count = mine.shape[0]
    order = lowers[0].shape[0]
    return pl.pallas_call(
        panel_one_kernel,
        out_shape=(
            jax.ShapeDtypeStruct((count + 1, TILE, order // 2), jnp.float32),
            jax.ShapeDtypeStruct((count, TILE, order), jnp.bfloat16),
        )
        + (jax.ShapeDtypeStruct((TILE, order), jnp.bfloat16),) * 3,
        in_specs=[SMEM, SMEM] + [VMEM] * 6,
        out_specs=(VMEM,) * 5,
        scratch_shapes=[
            pltpu.VMEM((count * TILE, order), jnp.float32),
            pltpu.VMEM((count * TILE, order), jnp.float32),
        ],
        compiler_params=PARAMS,
        cost_estimate=pl.CostEstimate(flops=10**9, bytes_accessed=10**6, transcendentals=0),
        name="panel_one",
    )(ids, next_map, mine, peer, *lowers, *inverses)


def panel_two_kernel(ids_ref, own_ref, x_ref, z_ref, both_ref, *refs):
    lowers, inverses = refs[:2], refs[2:4]
    factor_ref, round_ref, share_ref, coupling, panel = refs[4:]
    leaf, column = ids_ref[0], ids_ref[1]
    half, side = leaf & 1, (leaf >> 1) & 1
    quarter = leaf & 3
    count = round_ref.shape[0]
    for place, ref in (
        (2 * side + half, own_ref),
        (2 * side + 1 - half, x_ref),
        (2 * (1 - side) + half, z_ref),
        (2 * (1 - side) + 1 - half, both_ref),
    ):
        coupling[:, pl.ds(pl.multiple_of(place * TILE, TILE), TILE)] = ref[...].astype(jnp.float32)
    rounded = solve_blocks(coupling, lowers, inverses, panel)
    for s in range(count):
        round_ref[s] = rounded[s * TILE : (s + 1) * TILE]
    write_factor(column, quarter, lowers, panel, factor_ref)
    chosen = jnp.int32(0)
    for i in range(3):
        tile = 3 * quarter + i
        chosen = jnp.where((tile & 3) == column, tile >> 2, chosen)
    share_ref[...] = round_ref[chosen]


def panel_two(ids, parts, lowers, inverses):
    rows = parts[0].shape[0]
    count = rows // TILE
    order = lowers[0].shape[0]
    return pl.pallas_call(
        panel_two_kernel,
        out_shape=(
            jax.ShapeDtypeStruct((count + 1, TILE, order // 4), jnp.float32),
            jax.ShapeDtypeStruct((count, TILE, order), jnp.bfloat16),
            jax.ShapeDtypeStruct((TILE, order), jnp.bfloat16),
        ),
        in_specs=[SMEM] + [VMEM] * 8,
        out_specs=(VMEM, VMEM, VMEM),
        scratch_shapes=[pltpu.VMEM((rows, order), jnp.float32), pltpu.VMEM((rows, order), jnp.float32)],
        compiler_params=PARAMS,
        cost_estimate=pl.CostEstimate(flops=10**9, bytes_accessed=10**6, transcendentals=0),
        name="panel_two",
    )(ids, *parts, *lowers, *inverses)


def take_tile(owner, column, refs, live, target, sem):
    for apart, ref in enumerate(refs):

        @pl.when(jnp.logical_and(live, (owner ^ column) == apart))
        def _():
            pltpu.make_async_copy(ref, target, sem).start()


def start_shared(ids_ref, positions, firsts, thirds, taken, sems):
    leaf, column = ids_ref[0], ids_ref[1]
    half, side = leaf & 1, (leaf >> 1) & 1
    targets = column_targets(half, side)
    copies = []
    for i, position in enumerate(positions):
        target = targets[position]
        group = target & 3
        place = share_place(target, half)
        take_tile(group, column, firsts, place < 2, taken.at[i], sems.at[i])
        if thirds:
            take_tile(group, column, thirds, place == 2, taken.at[i], sems.at[i])
        copies.append(pltpu.make_async_copy(firsts[0], taken.at[i], sems.at[i]))
    return copies


def update_columns(ids_ref, next_ref, positions, copies, keep_ref, peer_ref, round_ref, taken, tiles, write):
    leaf, column = ids_ref[0], ids_ref[1]
    half, side, pair = leaf & 1, (leaf >> 1) & 1, leaf >> 1
    count = keep_ref.shape[0]
    targets = column_targets(half, side)
    rows = [find_tile(next_ref, pair, column, slot, count) for slot in range(count + 1)]
    tiles[:, count] = jnp.zeros_like(tiles[:, count])
    for i, position in enumerate(positions):
        target = targets[position]
        live = find_tile(next_ref, pair, target & 3, target >> 2, count) >= 0
        span = slice(i * TILE, (i + 1) * TILE)
        copies[i].wait()
        for s in range(count):
            value = keep_ref[s, :, span].astype(jnp.float32) + peer_ref[s, :, span].astype(jnp.float32)
            value = value - dot_lanes(round_ref[s], taken[i])
            tiles[i, s] = jnp.where(live, value, 0.0).astype(jnp.bfloat16)
        for slot, row in enumerate(rows):
            write(i, slot, lambda row=row: tiles[i, jnp.where(row < 0, count, row)])


def update_separator_kernel(
    ids_ref, next_ref, keep_ref, peer_ref, round_ref, *refs
):
    firsts, (pivot_ref, near_ref, far_ref, taken, tiles, sems) = refs[:4], refs[4:]

    def write(i, slot, tile):
        if slot == 0:
            pivot_ref[:, i * TILE : (i + 1) * TILE] = tile()
        else:
            (near_ref, far_ref)[i][slot - 1] = tile()

    copies = start_shared(ids_ref, (0, 4), firsts, (), taken, sems)
    update_columns(ids_ref, next_ref, (0, 4), copies, keep_ref, peer_ref, round_ref, taken, tiles, write)


def update_separator(ids, next_map, keep, peer, rounded, firsts):
    count, _, order = rounded.shape
    tile = jax.ShapeDtypeStruct((count, TILE, TILE), jnp.bfloat16)
    return pl.pallas_call(
        update_separator_kernel,
        out_shape=(jax.ShapeDtypeStruct((TILE, 2 * TILE), jnp.bfloat16), tile, tile),
        in_specs=[SMEM, SMEM, VMEM, VMEM, VMEM] + [ANY] * 4,
        out_specs=(VMEM, VMEM, VMEM),
        scratch_shapes=[
            pltpu.VMEM((2, TILE, order), jnp.bfloat16),
            pltpu.VMEM((2, count + 1, TILE, TILE), jnp.bfloat16),
            pltpu.SemaphoreType.DMA((2,)),
        ],
        compiler_params=pltpu.CompilerParams(vmem_limit_bytes=56 * 2**20),
        cost_estimate=pl.CostEstimate(flops=10**8, bytes_accessed=10**5, transcendentals=0),
        name="update_separator",
    )(ids, next_map, keep, peer, rounded, *firsts)


def update_trailing_kernel(
    positions, ids_ref, next_ref, keep_ref, peer_ref, round_ref, *refs
):
    seconds, thirds, (out_ref, taken, tiles, sems) = refs[:4], refs[4:8], refs[8:]

    def write(i, slot, tile):
        if slot:
            out_ref[slot - 1, :, i * TILE : (i + 1) * TILE] = tile()

    copies = start_shared(ids_ref, positions, seconds, thirds, taken, sems)
    update_columns(ids_ref, next_ref, positions, copies, keep_ref, peer_ref, round_ref, taken, tiles, write)


def update_trailing(ids, next_map, keep, peer, rounded, seconds, thirds, positions):
    count, _, order = rounded.shape
    width = len(positions)
    return pl.pallas_call(
        functools.partial(update_trailing_kernel, positions),
        out_shape=jax.ShapeDtypeStruct((count, TILE, width * TILE), jnp.bfloat16),
        in_specs=[SMEM, SMEM, VMEM, VMEM, VMEM] + [ANY] * 8,
        out_specs=VMEM,
        scratch_shapes=[
            pltpu.VMEM((width, TILE, order), jnp.bfloat16),
            pltpu.VMEM((width, count + 1, TILE, TILE), jnp.bfloat16),
            pltpu.SemaphoreType.DMA((width,)),
        ],
        compiler_params=pltpu.CompilerParams(vmem_limit_bytes=56 * 2**20),
        cost_estimate=pl.CostEstimate(flops=4 * 10**9, bytes_accessed=12 * 10**6, transcendentals=0),
        name="update_trailing",
    )(ids, next_map, keep, peer, rounded, *seconds, *thirds)


def update_two_kernel(ids_ref, near_ref, far_ref, round_ref, *refs):
    firsts, (out_ref, taken, sems) = refs[:4], refs[4:]
    quarter, column = ids_ref[0] & 3, ids_ref[1]
    for i in range(3):
        take_tile((3 * quarter + i) & 3, column, firsts, True, taken.at[i], sems.at[i])
    for i in range(3):
        span = slice(i * TILE, (i + 1) * TILE)
        pltpu.make_async_copy(firsts[0], taken.at[i], sems.at[i]).wait()
        for s in range(near_ref.shape[0]):
            total = near_ref[s, :, span].astype(jnp.float32) + far_ref[s, :, span].astype(jnp.float32)
            out_ref[s, :, span] = (total - dot_lanes(round_ref[s], taken[i])).astype(jnp.bfloat16)


def update_two(ids, near, far, rounded, firsts):
    order = rounded.shape[-1]
    return pl.pallas_call(
        update_two_kernel,
        out_shape=jax.ShapeDtypeStruct(near.shape, jnp.bfloat16),
        in_specs=[SMEM, VMEM, VMEM, VMEM] + [ANY] * 4,
        out_specs=VMEM,
        scratch_shapes=[pltpu.VMEM((3, TILE, order), jnp.bfloat16), pltpu.SemaphoreType.DMA((3,))],
        compiler_params=pltpu.CompilerParams(vmem_limit_bytes=56 * 2**20),
        cost_estimate=pl.CostEstimate(flops=2 * 10**9, bytes_accessed=10**7, transcendentals=0),
        name="update_two",
    )(ids, near, far, rounded, *firsts)


def over_square(pack, beside):
    half = pack.shape[0] // 2
    x, y, core = swapped(pack, "leaf", 1), swapped(pack, "front", 2), swapped(pack, "front", 1)
    x, y = lax.optimization_barrier((x, y, beside))[:2]
    top = swapped(y[:half], "leaf", 1)
    low = swapped(x[half:], "front", 2)
    x_core, y_core = swapped(x, "front", 1), swapped(y, "front", 1)
    top_core, low_core = swapped(top, "front", 1), swapped(low, "front", 1)
    return (pack, core, y, y_core, x, x_core, top, low, top_core, low_core)


def over_front(tile, y, *earlier):
    return (tile, swapped(tile, "front", 1), y, swapped(after(y, *earlier), "front", 1))


def over_heavy(tile, y, *earlier):
    return (tile, swapped_heavy(tile, 1), y, swapped_heavy(after(y, *earlier), 1))


def after(value, *earlier):
    return lax.optimization_barrier((value, *earlier))[0]


def own_mask(mask, front, column, count):
    rows = lax.dynamic_index_in_dim(mask, front, 0, keepdims=False).reshape(count, GROUPS, -1)
    return lax.dynamic_index_in_dim(rows, column, 1, keepdims=False).astype(jnp.float32)


def body(child_update, sep_one, sep_two, map_one, map_two, mask_one, mask_two):
    column = lax.axis_index("front")
    leaf = lax.axis_index("leaf")
    quad, quarter = leaf >> 2, leaf & 3
    ids = jnp.stack([leaf, column]).astype(jnp.int32)
    child = child_update[0, 0, 0]
    entries_one = sep_one[0, 0, 0]
    entries_two = sep_two[0, 0, 0]
    count = child.shape[0]
    order = GROUPS * TILE
    maps_one = map_one[:, 0]
    maps_two = map_two[:, 0]

    pivot_mine = pick_pivot(ids, maps_one, child, entries_one)
    coupling_send, coupling_keep, sep_send, near_send, far_send, sep_keep, near_keep, far_keep = pick_rest(
        ids, maps_one, maps_two, child
    )
    packs = over_square(pivot_mine, coupling_send)
    coupling_got = swapped(after(coupling_send, packs[4]), "leaf", 1)
    entries_far = swapped(entries_two[0], "leaf", 2)
    mask_first = own_mask(mask_one, leaf >> 1, column, count)
    mask_first = lax.dynamic_slice_in_dim(mask_first, 2 * (leaf & 1), 2, 1)
    mask_first = jnp.repeat(mask_first, TILE, axis=1)[:, None, :]

    lower, inverse, rest = cholesky_first(ids, packs, fill_one, order)
    coupling = (
        coupling_keep.astype(jnp.float32)
        + after(coupling_got, rest).astype(jnp.float32)
        + entries_one[1:].astype(jnp.float32) * mask_first
    )
    coupling_peer = swapped(coupling.astype(jnp.bfloat16), "leaf", 1)
    lower_rest, inverse_rest = cholesky_second(rest)
    sep_peer = swapped(after(sep_send, lower_rest), "leaf", 1)
    far_peer = swapped(after(far_send, lower_rest), "leaf", 1)
    factor_one, rounded, first, second, third = panel_one(
        ids, maps_two, coupling, coupling_peer, (lower, lower_rest), (inverse, inverse_rest)
    )
    first_y = swapped_heavy(first, 2)
    firsts = over_heavy(first, first_y, sep_peer)
    pivot_own, near_coupling, far_coupling = update_separator(ids, maps_two, sep_keep, sep_peer, rounded, firsts)
    second_y = swapped(after(second, first_y), "front", 2)
    seconds = over_front(second, second_y)
    thirds = over_heavy(third, swapped_heavy(after(third, first_y), 2))

    pivot_far = swapped(pivot_own, "leaf", 2)
    pivot_tile = (
        pivot_own.astype(jnp.float32)
        + jnp.concatenate([pivot_far[:, TILE:], pivot_far[:, :TILE]], axis=1).astype(jnp.float32)
        + jnp.concatenate([entries_two[0], entries_far], axis=1).astype(jnp.float32)
    )
    far_trailing = update_trailing(
        ids, maps_two, far_keep, far_peer, after(rounded, pivot_far), seconds, thirds, (5, 6, 7)
    )
    packs = over_square(after(pivot_tile, far_peer), far_trailing)
    coupling_far = swapped(after(far_coupling, pivot_far), "leaf", 2)
    mask_second = lax.dynamic_index_in_dim(own_mask(mask_two, quad, column, count), quarter, 1, keepdims=False)
    coupling = (
        near_coupling.astype(jnp.float32)
        + coupling_far.astype(jnp.float32)
        + entries_two[1:].astype(jnp.float32) * mask_second[:, None, None]
    ).reshape(count * TILE, TILE)
    coupling_sent = after(coupling.astype(jnp.bfloat16), packs[4])
    coupling_x, coupling_z, coupling_xz = (swapped(coupling_sent, "leaf", mask) for mask in (1, 2, 3))
    trailing_far = swapped(after(far_trailing, packs[4]), "leaf", 2)
    near_peer = swapped(after(near_send, packs[6]), "leaf", 1)
    lower, inverse, rest = cholesky_first(ids, packs, fill_two, order)
    lower_rest, inverse_rest = cholesky_second(rest)
    factor_two, rounded_two, share = panel_two(
        ids, (coupling, coupling_x, coupling_z, coupling_xz), (lower, lower_rest), (inverse, inverse_rest)
    )
    near_trailing = update_trailing(ids, maps_two, near_keep, near_peer, rounded, seconds, thirds, (1, 2, 3))
    shares = over_front(share, swapped(share, "front", 2), near_trailing, trailing_far)
    update = update_two(ids, near_trailing, trailing_far, rounded_two, shares)
    return (factor_one[None, None, None], factor_two[None, None, None], update[None, None, None])


def solution(mesh):
    split = P("leaf", "front", None, None, None, None)
    return jax.shard_map(
        body,
        mesh=mesh,
        in_specs=(split, split, split, P(), P(), P(), P()),
        out_specs=(split, split, split),
        check_vma=False,
    )
```

```python
import functools

import jax
import jax.numpy as jnp
from jax import lax
from jax.experimental import pallas as pl
from jax.experimental.pallas import tpu as pltpu
from jax.sharding import PartitionSpec as P

VMEM = pl.BlockSpec(memory_space=pltpu.VMEM)
SMEM = pl.BlockSpec(memory_space=pltpu.SMEM)
ANY = pl.BlockSpec(memory_space=pl.ANY)
GROUPS = 4
PARAMS = pltpu.CompilerParams(vmem_limit_bytes=32 * 2**20)
BLK = 128
GRP = 8
TILE = 256
NT = (((1,), (1,)), ((), ()))


def halves(x):
    high = x.astype(jnp.bfloat16)
    low = (x - high.astype(jnp.float32)).astype(jnp.bfloat16)
    return high, low


def left_parts(x):
    high, low = halves(x)
    return jnp.concatenate([high, low, high], axis=1)


def right_rows(x):
    high, low = halves(x)
    return jnp.concatenate([high, high, low], axis=0)


def right_lanes(x):
    high, low = halves(x)
    return jnp.concatenate([high, high, low], axis=1)


def dot_rows(left, right):
    return jnp.dot(left, right, preferred_element_type=jnp.float32)


def dot_lanes(left, right):
    return lax.dot_general(left, right, NT, preferred_element_type=jnp.float32)


def spread_row(ref, index):
    return jnp.broadcast_to(ref[index], (GRP, BLK))


def tree_sum(parts):
    while len(parts) > 1:
        parts = [parts[k] + parts[k + 1] for k in range(0, len(parts), 2)]
    return parts[0]


def factor_diagonal(block, done_ref, pivot_ref, rows_ref):
    steps = BLK // GRP
    row_id = lax.broadcasted_iota(jnp.int32, (GRP, BLK), 0)
    lane_id = lax.broadcasted_iota(jnp.int32, (GRP, BLK), 1)
    matrix = [block[GRP * g : GRP * (g + 1), :] for g in range(steps)]
    inverse = [jnp.where(lane_id == row_id + GRP * g, 1.0, 0.0).astype(jnp.float32) for g in range(steps)]
    for g in range(steps):
        first = GRP * g
        slot = g % 2
        current = matrix[g]
        rows_ref[slot, :, 0:BLK] = current
        rows_ref[slot, :, BLK:] = inverse[g]
        for i in range(GRP):
            pivot_ref[slot, i] = jnp.broadcast_to(current[:, first + i : first + i + 1], (GRP, BLK))
        entry = {}
        for m in range(GRP):
            for i in range(m + 1):
                entry[m, i] = jnp.broadcast_to(pivot_ref[slot, i, m : m + 1, :], (GRP, BLK))
                entry[i, m] = entry[m, i]
        left = [jnp.broadcast_to(rows_ref[slot, m : m + 1, 0:BLK], (GRP, BLK)) for m in range(GRP)]
        right = [jnp.broadcast_to(rows_ref[slot, m : m + 1, BLK:], (GRP, BLK)) for m in range(GRP)]
        for i in range(0, GRP, 2):
            n = i + 1
            a, b, c = entry[i, i], entry[n, i], entry[n, n]
            root = lax.rsqrt(a)
            root_both = lax.rsqrt(a * c - b * b)
            scale = root_both * root_both
            second_root = root * root_both

            def solve(x, y):
                return c * x - b * y, a * y - b * x

            solved = {}
            for name, rows_now in (("left", left), ("right", right)):
                raw = solve(rows_now[i], rows_now[n])
                lanes = slice(0, BLK) if name == "left" else slice(BLK, 2 * BLK)
                done_ref[first + i : first + i + 1, lanes] = (rows_now[i] * root)[0:1]
                done_ref[first + n : first + n + 1, lanes] = (raw[1] * second_root)[0:1]
                rows_now[i], rows_now[n] = raw[0] * scale, raw[1] * scale
            for col in range(i + 2, GRP):
                raw = solve(entry[i, col], entry[n, col])
                solved[col] = (raw[0] * scale, raw[1] * scale)
            for m in range(GRP):
                if m in (i, n):
                    continue
                weight, other = entry[m, i], entry[m, n]
                for rows_now in (left, right):
                    rows_now[m] = rows_now[m] - (weight * rows_now[i] + other * rows_now[n])
                for col in range(i + 2, GRP):
                    if m > col:
                        continue
                    entry[m, col] = entry[m, col] - (weight * solved[col][0] + other * solved[col][1])
            for m in range(i + 2, GRP):
                for col in range(i + 2, m):
                    entry[m, col] = entry[col, m]
            for col in range(i + 2, GRP):
                entry[i, col], entry[n, col] = solved[col]
        for later in range(g + 1, steps):
            rows = matrix[later]
            parts_left, parts_right = [], []
            for i in range(GRP):
                weight = jnp.broadcast_to(rows[:, first + i : first + i + 1], (GRP, BLK))
                parts_left.append(weight * left[i])
                parts_right.append(weight * right[i])
            matrix[later] = rows - tree_sum(parts_left)
            inverse[later] = inverse[later] - tree_sum(parts_right)


def tile_span(index):
    return pl.ds(pl.multiple_of(index * TILE, TILE), TILE)


def block_span(index, block):
    return pl.ds(pl.multiple_of(index * TILE + block * BLK, BLK), BLK)


def put_next(work, j, tile):
    last = work.shape[0] // TILE - 1

    @pl.when(j < last)
    def _():
        work[tile_span(j), tile_span(jnp.minimum(j + 1, last))] = tile()

    @pl.when(j == last)
    def _():
        work[0:TILE, last * TILE :] = tile().T


def put_half(work, j, block):
    for b in range(2):

        @pl.when(j < 2)
        def _():
            work[block_span(j, b), block_span(jnp.minimum(j, 1) + 2, 0)] = block(b)

        @pl.when(j >= 2)
        def _():
            work[block_span(jnp.maximum(j, 2) - 2, b), block_span(j, 1)] = block(b).T


def each_pack(packs):
    own, core, y, y_core, x, x_core, top, low, top_core, low_core = packs
    return (0, own, (x,)), (1, core, (x_core,)), (2, y, (top, low)), (3, y_core, (top_core, low_core))


def rows_of(refs, b, lanes):
    if len(refs) == 2:
        return refs[b][:, lanes].astype(jnp.float32)
    return refs[0][b * BLK : (b + 1) * BLK, lanes].astype(jnp.float32)


def fill_one(ids_ref, packs, work, mixed):
    leaf, column = ids_ref[0], ids_ref[1]
    half = leaf & 1
    width = mixed.shape[1]
    for apart, mine, peers in each_pack(packs):
        j = column ^ apart
        for b in range(2):
            rows = slice(b * BLK, (b + 1) * BLK)
            mixed[rows, :] = rows_of((mine,), b, slice(0, width)) + rows_of(peers, b, slice(0, width))
        for refs, side in (((mine,), half), (peers, 1 - half)):
            for q in range(2):
                apart_columns = (2 * side + q - j) & 3
                start = width + q * TILE
                for whole in range(2):

                    @pl.when(apart_columns == whole)
                    def _():
                        for b in range(2):
                            rows = slice(b * BLK, (b + 1) * BLK)
                            lanes = slice(whole * TILE, (whole + 1) * TILE)
                            mixed[rows, lanes] = mixed[rows, lanes] + rows_of(refs, b, slice(start, start + TILE))

                for b in range(2):
                    rows = slice(b * BLK, (b + 1) * BLK)

                    @pl.when(jnp.logical_and(apart_columns == 2, j < 2))
                    def _():
                        mixed[rows, 2 * TILE :] = mixed[rows, 2 * TILE :] + rows_of(refs, b, slice(start, start + BLK))

                    @pl.when(jnp.logical_and(apart_columns == 2, j >= 2))
                    def _():
                        lanes = slice(start + b * BLK, start + (b + 1) * BLK)
                        mixed[rows, 2 * TILE :] = mixed[rows, 2 * TILE :] + rows_of(refs, 1, lanes)

        work[tile_span(j), tile_span(j)] = mixed[:, 0:TILE]
        put_next(work, j, lambda: mixed[:, TILE : 2 * TILE])
        put_half(work, j, lambda b: mixed[b * BLK : (b + 1) * BLK, 2 * TILE :])


def fill_two(ids_ref, packs, work, mixed):
    leaf, column = ids_ref[0], ids_ref[1]
    half = leaf & 1
    for apart, mine, peers in each_pack(packs):
        j = column ^ apart
        for refs, side in (((mine,), half), (peers, 1 - half)):
            for b in range(2):
                mixed[b * BLK : (b + 1) * BLK, 0 : TILE + BLK] = rows_of(refs, b, slice(0, TILE + BLK))

            @pl.when(side == (j & 1))
            def _():
                work[tile_span(j), tile_span(j)] = mixed[:, 0:TILE]
                put_half(work, j, lambda b: mixed[b * BLK : (b + 1) * BLK, TILE : TILE + BLK])

            @pl.when(side != (j & 1))
            def _():
                put_next(work, j, lambda: mixed[:, 0:TILE])


def pack_two_kernel(ids_ref, own_ref, far_ref, near_entries_ref, far_entries_ref, pack_ref, both):
    leaf, column = ids_ref[0], ids_ref[1]
    half, side = leaf & 1, (leaf >> 1) & 1
    for place, other, entries_ref in ((0, 1, near_entries_ref), (1, 0, far_entries_ref)):
        both[place] = (
            own_ref[:, place * TILE : (place + 1) * TILE].astype(jnp.float32)
            + far_ref[:, other * TILE : (other + 1) * TILE].astype(jnp.float32)
            + entries_ref[...].astype(jnp.float32)
        )
    whole = jnp.where(half == (column & 1), column, (column + 1) & 3)
    place = jnp.where((whole >> 1) == side, 0, 1)
    pack_ref[:, 0:TILE] = both[place]
    for b in range(2):
        rows = slice(b * BLK, (b + 1) * BLK)

        @pl.when(column < 2)
        def _():
            pack_ref[rows, TILE:] = both[1 - place, rows, 0:BLK]

        @pl.when(column >= 2)
        def _():
            pack_ref[rows, TILE:] = both[1 - place, BLK:, rows]


def pack_two(ids, own, far, near_entries, far_entries):
    return pl.pallas_call(
        pack_two_kernel,
        out_shape=jax.ShapeDtypeStruct((TILE, TILE + BLK), jnp.float32),
        in_specs=[SMEM] + [VMEM] * 4,
        out_specs=VMEM,
        scratch_shapes=[pltpu.VMEM((2, TILE, TILE), jnp.float32)],
        compiler_params=pltpu.CompilerParams(vmem_limit_bytes=16 * 2**20),
        name="pack_two",
    )(ids, own, far, near_entries, far_entries)


def eliminate(work, lower_ref, inverse_ref, done, block_inverse, entries, rows):
    order = work.shape[0]
    blocks = lower_ref.shape[1] // BLK
    lower_ref[...] = jnp.zeros_like(lower_ref)
    row_id = lax.broadcasted_iota(jnp.int32, (BLK, BLK), 0)
    lane_id = lax.broadcasted_iota(jnp.int32, (BLK, BLK), 1)

    def step(k, carry):
        start = pl.multiple_of(k * BLK, BLK)
        span = pl.ds(start, BLK)
        factor_diagonal(work[span, span], done, entries, rows)
        upper = jnp.where(lane_id >= row_id, done[:, 0:BLK], 0.0)
        lower_ref[span, span] = upper.T
        block_inverse[k] = done[:, BLK:]
        for fixed in range(blocks):
            after = (fixed + 1) * BLK
            if after == order:
                continue

            @pl.when(k == fixed)
            def _():
                strip = dot_rows(
                    left_parts(done[:, BLK:]), right_rows(work[after - BLK : after, after:])
                )
                column = strip.T
                lower_ref[after:, after - BLK : after] = column
                left = left_parts(column)
                right = right_rows(strip)
                width = order - after
                for top in range(0, width, TILE):
                    high = min(TILE, width - top)
                    work[after + top : after + top + high, after + top :] = work[
                        after + top : after + top + high, after + top :
                    ] - dot_rows(left[top : top + high], right[:, top:])

        return carry

    lax.fori_loop(0, blocks, step, 0)
    for tile in range(blocks * BLK // TILE):
        base = tile * TILE
        first, second = block_inverse[2 * tile], block_inverse[2 * tile + 1]
        corner = lower_ref[base + BLK : base + TILE, base : base + BLK]
        mixed = dot_rows(left_parts(corner), right_rows(first))
        mixed = -dot_rows(left_parts(second), right_rows(mixed))
        inverse_ref[tile, 0:BLK, 0:BLK] = first
        inverse_ref[tile, 0:BLK, BLK:] = jnp.zeros((BLK, BLK), jnp.float32)
        inverse_ref[tile, BLK:, 0:BLK] = mixed
        inverse_ref[tile, BLK:, BLK:] = second


def cholesky_first_kernel(fill, ids_ref, *refs):
    packs = refs[:10]
    lower_ref, inverse_ref, rest_ref, mixed, work, *scratch = refs[10:]
    fill(ids_ref, packs, work, mixed)
    eliminate(work, lower_ref, inverse_ref, *scratch)
    done = lower_ref.shape[1]
    rest_ref[...] = work[done:, done:]


def cholesky_second_kernel(rest_ref, lower_ref, inverse_ref, work, *scratch):
    work[...] = rest_ref[...]
    eliminate(work, lower_ref, inverse_ref, *scratch)


def elimination_scratch(order, blocks):
    return [
        pltpu.VMEM((order, order), jnp.float32),
        pltpu.VMEM((BLK, 2 * BLK), jnp.float32),
        pltpu.VMEM((blocks, BLK, BLK), jnp.float32),
        pltpu.VMEM((2, GRP, GRP, BLK), jnp.float32),
        pltpu.VMEM((2, GRP, 2 * BLK), jnp.float32),
    ]


def cholesky_first(ids, packs, fill, order):
    done = order // 2
    return pl.pallas_call(
        functools.partial(cholesky_first_kernel, fill),
        out_shape=(
            jax.ShapeDtypeStruct((order, done), jnp.float32),
            jax.ShapeDtypeStruct((done // TILE, TILE, TILE), jnp.float32),
            jax.ShapeDtypeStruct((order - done, order - done), jnp.float32),
        ),
        in_specs=[SMEM] + [VMEM] * len(packs),
        out_specs=(VMEM,) * 3,
        scratch_shapes=[pltpu.VMEM((TILE, 2 * TILE + BLK), jnp.float32)] + elimination_scratch(order, done // BLK),
        compiler_params=pltpu.CompilerParams(vmem_limit_bytes=32 * 2**20),
        cost_estimate=pl.CostEstimate(flops=2 * 10**10, bytes_accessed=5 * 10**7, transcendentals=0),
        name="cholesky_first",
    )(ids, *packs)


def cholesky_second(rest):
    order = rest.shape[0]
    return pl.pallas_call(
        cholesky_second_kernel,
        out_shape=(
            jax.ShapeDtypeStruct((order, order), jnp.float32),
            jax.ShapeDtypeStruct((order // TILE, TILE, TILE), jnp.float32),
        ),
        in_specs=[VMEM],
        out_specs=(VMEM,) * 2,
        scratch_shapes=elimination_scratch(order, order // BLK),
        compiler_params=pltpu.CompilerParams(vmem_limit_bytes=24 * 2**20),
        cost_estimate=pl.CostEstimate(flops=2 * 10**10, bytes_accessed=5 * 10**7, transcendentals=0),
        name="cholesky_second",
    )(rest)


def swapped(value, axis, mask):
    pairs = [(source, source ^ mask) for source in range(lax.axis_size(axis))]
    return lax.ppermute(value, axis, pairs)


def swapped_heavy(value, mask):
    groups = lax.axis_size("front")
    pairs = [
        (leaf * groups + column, leaf * groups + (column ^ mask))
        for leaf in range(lax.axis_size("leaf"))
        for column in range(groups)
        if (leaf & 1) == (column & 1)
    ]
    return lax.ppermute(value, ("leaf", "front"), pairs)


def find_tile(map_ref, owner, group, slot, count):
    found = jnp.int32(-1)
    for s in range(count):
        found = jnp.where(map_ref[owner, group, s] == slot, jnp.int32(s), found)
    return found


def column_targets(half, side):
    targets = []
    for part in (side, 1 - side):
        targets.append(2 * part + half)
        targets += [4 + 3 * (2 * part + half) + i for i in range(3)]
    return targets


def share_place(target, half):
    place = jnp.int32(0)
    for other in column_targets(half, 0):
        earlier = jnp.logical_and((other & 3) == (target & 3), other < target)
        place = place + earlier.astype(jnp.int32)
    return place


def move_tile(live, source, target, sem):
    @pl.when(live)
    def _():
        pltpu.make_async_copy(source, target, sem).start()

    @pl.when(jnp.logical_not(live))
    def _():
        target[...] = jnp.zeros(target.shape, target.dtype)

    def wait():
        @pl.when(live)
        def _():
            pltpu.make_async_copy(source, target, sem).wait()

    return wait


def move_separator(leaf, column, map_ref, child_ref, slots, groups, target_of, sems):
    count = child_ref.shape[0]
    waits = []
    for slot in slots:
        row = find_tile(map_ref, leaf, column, slot, count)
        for position, group in enumerate(groups):
            place = find_tile(map_ref, leaf, group, 0, count)
            live = jnp.logical_and(row >= 0, place >= 0)
            span = pl.ds(pl.multiple_of((jnp.maximum(place, 0) * GROUPS + group) * TILE, TILE), TILE)
            source = child_ref.at[jnp.maximum(row, 0), :, span]
            target = target_of(slot, position)
            waits.append(move_tile(live, source, target, sems.at[len(waits)]))
    return waits


def pick_pivot_kernel(ids_ref, map_ref, child_ref, entries_ref, pivot_ref, sems, entry_sem):
    leaf, column = ids_ref[0], ids_ref[1]
    count = child_ref.shape[0]
    width = 2 * TILE + BLK
    entries = pltpu.make_async_copy(
        entries_ref.at[0], pivot_ref.at[:, pl.ds(width, entries_ref.shape[-1])], entry_sem.at[0]
    )
    entries.start()
    row = find_tile(map_ref, leaf, column, 0, count)
    waits = []
    for apart in range(3):
        group = (column + apart) & 3
        place = find_tile(map_ref, leaf, group, 0, count)
        live = jnp.logical_and(row >= 0, place >= 0)
        tile = jnp.maximum(place, 0) * GROUPS + group
        source_row = child_ref.at[jnp.maximum(row, 0)]
        if apart < 2:
            moves = [(source_row.at[:, tile_span(tile)], pivot_ref.at[:, pl.ds(apart * TILE, TILE)])]
        else:
            moves = []
            for b in range(2):
                top = pl.multiple_of(jnp.where(column < 2, b * BLK, BLK), BLK)
                lanes = pl.ds(pl.multiple_of(tile * TILE + jnp.where(column < 2, 0, b * BLK), BLK), BLK)
                target = pivot_ref.at[pl.ds(b * BLK, BLK), pl.ds(2 * TILE, BLK)]
                moves.append((source_row.at[pl.ds(top, BLK), lanes], target))
        for source, target in moves:
            waits.append(move_tile(live, source, target, sems.at[len(waits)]))
    for wait in waits:
        wait()
    entries.wait()


def pick_pivot(ids, child_map, child, entries):
    width = 2 * TILE + BLK + entries.shape[-1]
    return pl.pallas_call(
        pick_pivot_kernel,
        out_shape=jax.ShapeDtypeStruct((TILE, width), child.dtype),
        in_specs=[SMEM, SMEM, ANY, ANY],
        out_specs=VMEM,
        scratch_shapes=[pltpu.SemaphoreType.DMA((GROUPS,)), pltpu.SemaphoreType.DMA((1,))],
        compiler_params=pltpu.CompilerParams(vmem_limit_bytes=56 * 2**20),
        name="pick_pivot",
    )(ids, child_map, child, entries)


def pick_rest_kernel(ids_ref, map_ref, next_ref, child_ref, *refs):
    halves_out, outs, (first_sems, sems) = refs[:2], refs[2:8], refs[8:]
    count = child_ref.shape[0]
    leaf, column = ids_ref[0], ids_ref[1]
    half, pair = leaf & 1, leaf >> 1
    slots = range(1, count + 1)
    groups = (2 * (1 - half), 2 * (1 - half) + 1, 2 * half, 2 * half + 1)
    waits = move_separator(
        leaf, column, map_ref, child_ref, slots, groups,
        lambda slot, position: halves_out[position // 2].at[slot - 1, :, pl.ds(position % 2 * TILE, TILE)],
        first_sems,
    )
    rows = [find_tile(map_ref, leaf, column, slot, count) for slot in slots]
    used = 0
    for which, device in enumerate((leaf ^ 1, leaf)):
        for position, target in enumerate(column_targets(device & 1, (device >> 1) & 1)):
            group = target & 3
            update = find_tile(next_ref, pair, group, target >> 2, count)
            place = find_tile(map_ref, leaf, group, update + 1, count)
            column_live = jnp.logical_and(update >= 0, place >= 0)
            source_span = pl.ds(pl.multiple_of((jnp.maximum(place, 0) * GROUPS + group) * TILE, TILE), TILE)
            for slot, row in enumerate(rows):
                live = jnp.logical_and(column_live, row >= 0)
                source = child_ref.at[jnp.maximum(row, 0), :, source_span]
                if position % 4 == 0:
                    goal = outs[3 * which].at[slot, :, pl.ds(position // 4 * TILE, TILE)]
                else:
                    goal = outs[3 * which + 1 + position // 4].at[slot, :, pl.ds((position % 4 - 1) * TILE, TILE)]
                waits.append(move_tile(live, source, goal, sems.at[used]))
                used += 1
    for wait in waits:
        wait()


def pick_rest(ids, child_map, next_map, child):
    count = child.shape[0]
    widths = (2 * TILE, 2 * TILE) + (2 * TILE, 3 * TILE, 3 * TILE) * 2
    return pl.pallas_call(
        pick_rest_kernel,
        out_shape=tuple(jax.ShapeDtypeStruct((count, TILE, width), child.dtype) for width in widths),
        in_specs=[SMEM, SMEM, SMEM, ANY],
        out_specs=(VMEM,) * 8,
        scratch_shapes=[pltpu.SemaphoreType.DMA((GROUPS * count,)), pltpu.SemaphoreType.DMA((16 * count,))],
        compiler_params=pltpu.CompilerParams(vmem_limit_bytes=56 * 2**20),
        cost_estimate=pl.CostEstimate(flops=0, bytes_accessed=2 * 10**7, transcendentals=0),
        name="pick_rest",
    )(ids, child_map, next_map, child)


def solve_blocks(coupling_ref, lowers, inverses, panel_ref):
    split = lowers[0].shape[1]
    solved = []
    for k in range(panel_ref.shape[1] // TILE):
        span = slice(k * TILE, (k + 1) * TILE)
        rest = coupling_ref[:, span]
        if k:
            left = jnp.concatenate([part[0] for part in solved], axis=1)
            low = jnp.concatenate([part[1] for part in solved], axis=1)
            strip = lowers[0][span, 0 : min(k * TILE, split)]
            if k * TILE > split:
                inner = slice(k * TILE - split, (k + 1) * TILE - split)
                strip = jnp.concatenate([strip, lowers[1][inner, 0 : k * TILE - split]], axis=1)
            high_lower, low_lower = halves(strip)
            rest = rest - dot_lanes(
                jnp.concatenate([left, low, left], axis=1),
                jnp.concatenate([high_lower, high_lower, low_lower], axis=1),
            )
        tiles = split // TILE
        inverse = inverses[0][k] if k < tiles else inverses[1][k - tiles]
        block = dot_lanes(left_parts(rest), right_lanes(inverse))
        panel_ref[:, span] = block
        solved.append(halves(block))
    return jnp.concatenate([part[0] for part in solved], axis=1)


def write_factor(column, offset, lowers, panel, factor_ref):
    width = factor_ref.shape[-1]
    split = lowers[0].shape[1]
    per = split // width
    tiles = split // TILE
    span = pl.ds(pl.multiple_of(offset * width, width), width)
    factor_ref[0] = jnp.zeros(factor_ref.shape[1:], factor_ref.dtype)

    @pl.when(offset < per)
    def _():
        inner = pl.ds(pl.multiple_of(jnp.minimum(offset, per - 1) * width, width), width)
        factor_ref[0] = lowers[0][pl.ds(pl.multiple_of(column * TILE, TILE), TILE), inner]

    @pl.when(jnp.logical_and(offset >= per, column >= tiles))
    def _():
        inner = pl.ds(pl.multiple_of(jnp.maximum(offset - per, 0) * width, width), width)
        rows = pl.ds(pl.multiple_of(jnp.maximum(column - tiles, 0) * TILE, TILE), TILE)
        factor_ref[0] = lowers[1][rows, inner]

    for s in range(factor_ref.shape[0] - 1):
        factor_ref[s + 1] = panel[s * TILE : (s + 1) * TILE, span]


def panel_one_kernel(ids_ref, next_ref, mine_ref, peer_ref, *refs):
    lowers, inverses = refs[:2], refs[2:4]
    factor_ref, round_ref, first_ref, second_ref, third_ref, coupling, panel = refs[4:]
    leaf, column = ids_ref[0], ids_ref[1]
    half, pair = leaf & 1, leaf >> 1
    count, _, width = mine_ref.shape
    for ref, place in ((mine_ref, half), (peer_ref, 1 - half)):
        span = pl.ds(pl.multiple_of(place * width, width), width)
        for s in range(count):
            coupling[s * TILE : (s + 1) * TILE, span] = ref[s].astype(jnp.float32)
    rounded = solve_blocks(coupling, lowers, inverses, panel)
    for s in range(count):
        round_ref[s] = rounded[s * TILE : (s + 1) * TILE]
    write_factor(column, half, lowers, panel, factor_ref)
    heavy = half == (column & 1)
    for a, share_ref in ((0, first_ref), (jnp.where(heavy, 1, 0), second_ref), (2, third_ref)):
        slot = jnp.int32(0)
        for target in column_targets(half, 0):
            hit = jnp.logical_and((target & 3) == column, share_place(target, half) == a)
            slot = jnp.where(hit, target >> 2, slot)
        tile = find_tile(next_ref, pair, column, slot, count)
        share_ref[...] = round_ref[jnp.maximum(tile, 0)]


def panel_one(ids, next_map, mine, peer, lowers, inverses):
    count = mine.shape[0]
    order = lowers[0].shape[0]
    return pl.pallas_call(
        panel_one_kernel,
        out_shape=(
            jax.ShapeDtypeStruct((count + 1, TILE, order // 2), jnp.float32),
            jax.ShapeDtypeStruct((count, TILE, order), jnp.bfloat16),
        )
        + (jax.ShapeDtypeStruct((TILE, order), jnp.bfloat16),) * 3,
        in_specs=[SMEM, SMEM] + [VMEM] * 6,
        out_specs=(VMEM,) * 5,
        scratch_shapes=[
            pltpu.VMEM((count * TILE, order), jnp.float32),
            pltpu.VMEM((count * TILE, order), jnp.float32),
        ],
        compiler_params=PARAMS,
        cost_estimate=pl.CostEstimate(flops=10**9, bytes_accessed=10**6, transcendentals=0),
        name="panel_one",
    )(ids, next_map, mine, peer, *lowers, *inverses)


def panel_two_kernel(ids_ref, own_ref, x_ref, z_ref, both_ref, *refs):
    lowers, inverses = refs[:2], refs[2:4]
    factor_ref, round_ref, share_ref, coupling, panel = refs[4:]
    leaf, column = ids_ref[0], ids_ref[1]
    half, side = leaf & 1, (leaf >> 1) & 1
    quarter = leaf & 3
    count = round_ref.shape[0]
    for place, ref in (
        (2 * side + half, own_ref),
        (2 * side + 1 - half, x_ref),
        (2 * (1 - side) + half, z_ref),
        (2 * (1 - side) + 1 - half, both_ref),
    ):
        coupling[:, pl.ds(pl.multiple_of(place * TILE, TILE), TILE)] = ref[...].astype(jnp.float32)
    rounded = solve_blocks(coupling, lowers, inverses, panel)
    for s in range(count):
        round_ref[s] = rounded[s * TILE : (s + 1) * TILE]
    write_factor(column, quarter, lowers, panel, factor_ref)
    chosen = jnp.int32(0)
    for i in range(3):
        tile = 3 * quarter + i
        chosen = jnp.where((tile & 3) == column, tile >> 2, chosen)
    share_ref[...] = round_ref[chosen]


def panel_two(ids, parts, lowers, inverses):
    rows = parts[0].shape[0]
    count = rows // TILE
    order = lowers[0].shape[0]
    return pl.pallas_call(
        panel_two_kernel,
        out_shape=(
            jax.ShapeDtypeStruct((count + 1, TILE, order // 4), jnp.float32),
            jax.ShapeDtypeStruct((count, TILE, order), jnp.bfloat16),
            jax.ShapeDtypeStruct((TILE, order), jnp.bfloat16),
        ),
        in_specs=[SMEM] + [VMEM] * 8,
        out_specs=(VMEM, VMEM, VMEM),
        scratch_shapes=[pltpu.VMEM((rows, order), jnp.float32), pltpu.VMEM((rows, order), jnp.float32)],
        compiler_params=PARAMS,
        cost_estimate=pl.CostEstimate(flops=10**9, bytes_accessed=10**6, transcendentals=0),
        name="panel_two",
    )(ids, *parts, *lowers, *inverses)


def take_tile(owner, column, refs, live, target, sem):
    for apart, ref in enumerate(refs):

        @pl.when(jnp.logical_and(live, (owner ^ column) == apart))
        def _():
            pltpu.make_async_copy(ref, target, sem).start()


def start_shared(ids_ref, positions, firsts, thirds, taken, sems):
    leaf, column = ids_ref[0], ids_ref[1]
    half, side = leaf & 1, (leaf >> 1) & 1
    targets = column_targets(half, side)
    copies = []
    for i, position in enumerate(positions):
        target = targets[position]
        group = target & 3
        place = share_place(target, half)
        take_tile(group, column, firsts, place < 2, taken.at[i], sems.at[i])
        if thirds:
            take_tile(group, column, thirds, place == 2, taken.at[i], sems.at[i])
        copies.append(pltpu.make_async_copy(firsts[0], taken.at[i], sems.at[i]))
    return copies


def update_columns(ids_ref, next_ref, positions, copies, keep_ref, peer_ref, round_ref, taken, tiles, write):
    leaf, column = ids_ref[0], ids_ref[1]
    half, side, pair = leaf & 1, (leaf >> 1) & 1, leaf >> 1
    count = keep_ref.shape[0]
    targets = column_targets(half, side)
    rows = [find_tile(next_ref, pair, column, slot, count) for slot in range(count + 1)]
    tiles[:, count] = jnp.zeros_like(tiles[:, count])
    for i, position in enumerate(positions):
        target = targets[position]
        live = find_tile(next_ref, pair, target & 3, target >> 2, count) >= 0
        span = slice(i * TILE, (i + 1) * TILE)
        copies[i].wait()
        product = dot_lanes(round_ref[...].reshape(count * TILE, -1), taken[i])
        for s in range(count):
            value = keep_ref[s, :, span].astype(jnp.float32) + peer_ref[s, :, span].astype(jnp.float32)
            value = value - product[s * TILE : (s + 1) * TILE]
            tiles[i, s] = jnp.where(live, value, 0.0).astype(jnp.bfloat16)
        for slot, row in enumerate(rows):
            write(i, slot, lambda row=row: tiles[i, jnp.where(row < 0, count, row)])


def update_separator_kernel(
    ids_ref, next_ref, keep_ref, peer_ref, round_ref, *refs
):
    firsts, (pivot_ref, near_ref, far_ref, taken, tiles, sems) = refs[:4], refs[4:]

    def write(i, slot, tile):
        if slot == 0:
            pivot_ref[:, i * TILE : (i + 1) * TILE] = tile()
        else:
            (near_ref, far_ref)[i][slot - 1] = tile()

    copies = start_shared(ids_ref, (0, 4), firsts, (), taken, sems)
    update_columns(ids_ref, next_ref, (0, 4), copies, keep_ref, peer_ref, round_ref, taken, tiles, write)


def update_separator(ids, next_map, keep, peer, rounded, firsts):
    count, _, order = rounded.shape
    tile = jax.ShapeDtypeStruct((count, TILE, TILE), jnp.bfloat16)
    return pl.pallas_call(
        update_separator_kernel,
        out_shape=(jax.ShapeDtypeStruct((TILE, 2 * TILE), jnp.bfloat16), tile, tile),
        in_specs=[SMEM, SMEM, VMEM, VMEM, VMEM] + [ANY] * 4,
        out_specs=(VMEM, VMEM, VMEM),
        scratch_shapes=[
            pltpu.VMEM((2, TILE, order), jnp.bfloat16),
            pltpu.VMEM((2, count + 1, TILE, TILE), jnp.bfloat16),
            pltpu.SemaphoreType.DMA((2,)),
        ],
        compiler_params=pltpu.CompilerParams(vmem_limit_bytes=56 * 2**20),
        cost_estimate=pl.CostEstimate(flops=10**8, bytes_accessed=10**5, transcendentals=0),
        name="update_separator",
    )(ids, next_map, keep, peer, rounded, *firsts)


def update_trailing_kernel(
    positions, ids_ref, next_ref, keep_ref, peer_ref, round_ref, *refs
):
    seconds, thirds, (out_ref, taken, tiles, sems) = refs[:4], refs[4:8], refs[8:]

    def write(i, slot, tile):
        if slot:
            out_ref[slot - 1, :, i * TILE : (i + 1) * TILE] = tile()

    copies = start_shared(ids_ref, positions, seconds, thirds, taken, sems)
    update_columns(ids_ref, next_ref, positions, copies, keep_ref, peer_ref, round_ref, taken, tiles, write)


def update_trailing(ids, next_map, keep, peer, rounded, seconds, thirds, positions):
    count, _, order = rounded.shape
    width = len(positions)
    return pl.pallas_call(
        functools.partial(update_trailing_kernel, positions),
        out_shape=jax.ShapeDtypeStruct((count, TILE, width * TILE), jnp.bfloat16),
        in_specs=[SMEM, SMEM, VMEM, VMEM, VMEM] + [ANY] * 8,
        out_specs=VMEM,
        scratch_shapes=[
            pltpu.VMEM((width, TILE, order), jnp.bfloat16),
            pltpu.VMEM((width, count + 1, TILE, TILE), jnp.bfloat16),
            pltpu.SemaphoreType.DMA((width,)),
        ],
        compiler_params=pltpu.CompilerParams(vmem_limit_bytes=56 * 2**20),
        cost_estimate=pl.CostEstimate(flops=4 * 10**9, bytes_accessed=12 * 10**6, transcendentals=0),
        name="update_trailing",
    )(ids, next_map, keep, peer, rounded, *seconds, *thirds)


def update_two_kernel(ids_ref, near_ref, far_ref, round_ref, *refs):
    firsts, (out_ref, taken, sems) = refs[:4], refs[4:]
    quarter, column = ids_ref[0] & 3, ids_ref[1]
    for i in range(3):
        take_tile((3 * quarter + i) & 3, column, firsts, True, taken.at[i], sems.at[i])
    for i in range(3):
        span = slice(i * TILE, (i + 1) * TILE)
        pltpu.make_async_copy(firsts[0], taken.at[i], sems.at[i]).wait()
        count = near_ref.shape[0]
        product = dot_lanes(round_ref[...].reshape(count * TILE, -1), taken[i])
        for s in range(count):
            total = near_ref[s, :, span].astype(jnp.float32) + far_ref[s, :, span].astype(jnp.float32)
            out_ref[s, :, span] = (total - product[s * TILE : (s + 1) * TILE]).astype(jnp.bfloat16)


def update_two(ids, near, far, rounded, firsts):
    order = rounded.shape[-1]
    return pl.pallas_call(
        update_two_kernel,
        out_shape=jax.ShapeDtypeStruct(near.shape, jnp.bfloat16),
        in_specs=[SMEM, VMEM, VMEM, VMEM] + [ANY] * 4,
        out_specs=VMEM,
        scratch_shapes=[pltpu.VMEM((3, TILE, order), jnp.bfloat16), pltpu.SemaphoreType.DMA((3,))],
        compiler_params=pltpu.CompilerParams(vmem_limit_bytes=56 * 2**20),
        cost_estimate=pl.CostEstimate(flops=2 * 10**9, bytes_accessed=10**7, transcendentals=0),
        name="update_two",
    )(ids, near, far, rounded, *firsts)


def over_square(pack, beside):
    half = pack.shape[0] // 2
    x, y, core = swapped(pack, "leaf", 1), swapped(pack, "front", 2), swapped(pack, "front", 1)
    x, y = lax.optimization_barrier((x, y, beside))[:2]
    top = swapped(y[:half], "leaf", 1)
    low = swapped(x[half:], "front", 2)
    x_core, y_core = swapped(x, "front", 1), swapped(y, "front", 1)
    top_core, low_core = swapped(top, "front", 1), swapped(low, "front", 1)
    return (pack, core, y, y_core, x, x_core, top, low, top_core, low_core)


def over_front(tile, y, *earlier):
    return (tile, swapped(tile, "front", 1), y, swapped(after(y, *earlier), "front", 1))


def over_heavy(tile, y, *earlier):
    return (tile, swapped_heavy(tile, 1), y, swapped_heavy(after(y, *earlier), 1))


def after(value, *earlier):
    return lax.optimization_barrier((value, *earlier))[0]


def own_mask(mask, front, column, count):
    rows = lax.dynamic_index_in_dim(mask, front, 0, keepdims=False).reshape(count, GROUPS, -1)
    return lax.dynamic_index_in_dim(rows, column, 1, keepdims=False).astype(jnp.float32)


def body(child_update, sep_one, sep_two, map_one, map_two, mask_one, mask_two):
    column = lax.axis_index("front")
    leaf = lax.axis_index("leaf")
    quad, quarter = leaf >> 2, leaf & 3
    ids = jnp.stack([leaf, column]).astype(jnp.int32)
    child = child_update[0, 0, 0]
    entries_one = sep_one[0, 0, 0]
    entries_two = sep_two[0, 0, 0]
    count = child.shape[0]
    order = GROUPS * TILE
    maps_one = map_one[:, 0]
    maps_two = map_two[:, 0]

    pivot_mine = pick_pivot(ids, maps_one, child, entries_one)
    coupling_send, coupling_keep, sep_send, near_send, far_send, sep_keep, near_keep, far_keep = pick_rest(
        ids, maps_one, maps_two, child
    )
    packs = over_square(pivot_mine, coupling_send)
    coupling_got = swapped(after(coupling_send, packs[4]), "leaf", 1)
    entries_far = swapped(entries_two[0], "leaf", 2)
    mask_first = own_mask(mask_one, leaf >> 1, column, count)
    mask_first = lax.dynamic_slice_in_dim(mask_first, 2 * (leaf & 1), 2, 1)
    mask_first = jnp.repeat(mask_first, TILE, axis=1)[:, None, :]

    lower, inverse, rest = cholesky_first(ids, packs, fill_one, order)
    coupling = (
        coupling_keep.astype(jnp.float32)
        + after(coupling_got, rest).astype(jnp.float32)
        + entries_one[1:].astype(jnp.float32) * mask_first
    )
    coupling_peer = swapped(coupling.astype(jnp.bfloat16), "leaf", 1)
    lower_rest, inverse_rest = cholesky_second(rest)
    sep_peer = swapped(after(sep_send, lower_rest), "leaf", 1)
    far_peer = swapped(after(far_send, lower_rest), "leaf", 1)
    factor_one, rounded, first, second, third = panel_one(
        ids, maps_two, coupling, coupling_peer, (lower, lower_rest), (inverse, inverse_rest)
    )
    first_y = swapped_heavy(first, 2)
    firsts = over_heavy(first, first_y, sep_peer)
    pivot_own, near_coupling, far_coupling = update_separator(ids, maps_two, sep_keep, sep_peer, rounded, firsts)
    second_y = swapped(after(second, first_y), "front", 2)
    seconds = over_front(second, second_y)
    thirds = over_heavy(third, swapped_heavy(after(third, first_y), 2))

    pivot_far = swapped(pivot_own, "leaf", 2)
    pivot_pack = pack_two(ids, pivot_own, pivot_far, entries_two[0], entries_far)
    far_trailing = update_trailing(
        ids, maps_two, far_keep, far_peer, after(rounded, pivot_far), seconds, thirds, (5, 6, 7)
    )
    packs = over_square(after(pivot_pack, far_peer), far_trailing)
    coupling_far = swapped(after(far_coupling, pivot_far), "leaf", 2)
    mask_second = lax.dynamic_index_in_dim(own_mask(mask_two, quad, column, count), quarter, 1, keepdims=False)
    coupling = (
        near_coupling.astype(jnp.float32)
        + coupling_far.astype(jnp.float32)
        + entries_two[1:].astype(jnp.float32) * mask_second[:, None, None]
    ).reshape(count * TILE, TILE)
    coupling_sent = after(coupling.astype(jnp.bfloat16), packs[4])
    coupling_x, coupling_z, coupling_xz = (swapped(coupling_sent, "leaf", mask) for mask in (1, 2, 3))
    trailing_far = swapped(after(far_trailing, packs[4]), "leaf", 2)
    near_peer = swapped(after(near_send, packs[6]), "leaf", 1)
    lower, inverse, rest = cholesky_first(ids, packs, fill_two, order)
    lower_rest, inverse_rest = cholesky_second(rest)
    factor_two, rounded_two, share = panel_two(
        ids, (coupling, coupling_x, coupling_z, coupling_xz), (lower, lower_rest), (inverse, inverse_rest)
    )
    near_trailing = update_trailing(ids, maps_two, near_keep, near_peer, rounded, seconds, thirds, (1, 2, 3))
    shares = over_front(share, swapped(share, "front", 2), near_trailing, trailing_far)
    update = update_two(ids, near_trailing, trailing_far, rounded_two, shares)
    return (factor_one[None, None, None], factor_two[None, None, None], update[None, None, None])


def solution(mesh):
    split = P("leaf", "front", None, None, None, None)
    return jax.shard_map(
        body,
        mesh=mesh,
        in_specs=(split, split, split, P(), P(), P(), P()),
        out_specs=(split, split, split),
        check_vma=False,
    )
```

```python
import functools

import jax
import jax.numpy as jnp
from jax import lax
from jax.experimental import pallas as pl
from jax.experimental.pallas import tpu as pltpu
from jax.sharding import PartitionSpec as P

VMEM = pl.BlockSpec(memory_space=pltpu.VMEM)
SMEM = pl.BlockSpec(memory_space=pltpu.SMEM)
ANY = pl.BlockSpec(memory_space=pl.ANY)
GROUPS = 4
PARAMS = pltpu.CompilerParams(vmem_limit_bytes=32 * 2**20)
BLK = 128
GRP = 8
TILE = 256
NT = (((1,), (1,)), ((), ()))


def halves(x):
    high = x.astype(jnp.bfloat16)
    low = (x - high.astype(jnp.float32)).astype(jnp.bfloat16)
    return high, low


def left_parts(x):
    high, low = halves(x)
    return jnp.concatenate([high, low, high], axis=1)


def right_rows(x):
    high, low = halves(x)
    return jnp.concatenate([high, high, low], axis=0)


def right_lanes(x):
    high, low = halves(x)
    return jnp.concatenate([high, high, low], axis=1)


def dot_rows(left, right):
    return jnp.dot(left, right, preferred_element_type=jnp.float32)


def dot_lanes(left, right):
    return lax.dot_general(left, right, NT, preferred_element_type=jnp.float32)


def spread_row(ref, index):
    return jnp.broadcast_to(ref[index], (GRP, BLK))


def tree_sum(parts):
    while len(parts) > 1:
        parts = [parts[k] + parts[k + 1] for k in range(0, len(parts), 2)]
    return parts[0]


def factor_diagonal(block, done_ref, pivot_ref, rows_ref):
    steps = BLK // GRP
    row_id = lax.broadcasted_iota(jnp.int32, (GRP, BLK), 0)
    lane_id = lax.broadcasted_iota(jnp.int32, (GRP, BLK), 1)
    matrix = [block[GRP * g : GRP * (g + 1), :] for g in range(steps)]
    inverse = [jnp.where(lane_id == row_id + GRP * g, 1.0, 0.0).astype(jnp.float32) for g in range(steps)]
    for g in range(steps):
        first = GRP * g
        slot = g % 2
        current = matrix[g]
        rows_ref[slot, :, 0:BLK] = current
        rows_ref[slot, :, BLK:] = inverse[g]
        for i in range(GRP):
            pivot_ref[slot, i] = jnp.broadcast_to(current[:, first + i : first + i + 1], (GRP, BLK))
        entry = {}
        for m in range(GRP):
            for i in range(m + 1):
                entry[m, i] = jnp.broadcast_to(pivot_ref[slot, i, m : m + 1, :], (GRP, BLK))
                entry[i, m] = entry[m, i]
        left = [jnp.broadcast_to(rows_ref[slot, m : m + 1, 0:BLK], (GRP, BLK)) for m in range(GRP)]
        right = [jnp.broadcast_to(rows_ref[slot, m : m + 1, BLK:], (GRP, BLK)) for m in range(GRP)]
        for i in range(0, GRP, 2):
            n = i + 1
            a, b, c = entry[i, i], entry[n, i], entry[n, n]
            root = lax.rsqrt(a)
            root_both = lax.rsqrt(a * c - b * b)
            scale = root_both * root_both
            second_root = root * root_both

            def solve(x, y):
                return c * x - b * y, a * y - b * x

            solved = {}
            for name, rows_now in (("left", left), ("right", right)):
                raw = solve(rows_now[i], rows_now[n])
                lanes = slice(0, BLK) if name == "left" else slice(BLK, 2 * BLK)
                done_ref[first + i : first + i + 1, lanes] = (rows_now[i] * root)[0:1]
                done_ref[first + n : first + n + 1, lanes] = (raw[1] * second_root)[0:1]
                rows_now[i], rows_now[n] = raw[0] * scale, raw[1] * scale
            for col in range(i + 2, GRP):
                raw = solve(entry[i, col], entry[n, col])
                solved[col] = (raw[0] * scale, raw[1] * scale)
            for m in range(GRP):
                if m in (i, n):
                    continue
                weight, other = entry[m, i], entry[m, n]
                for rows_now in (left, right):
                    rows_now[m] = rows_now[m] - (weight * rows_now[i] + other * rows_now[n])
                for col in range(i + 2, GRP):
                    if m > col:
                        continue
                    entry[m, col] = entry[m, col] - (weight * solved[col][0] + other * solved[col][1])
            for m in range(i + 2, GRP):
                for col in range(i + 2, m):
                    entry[m, col] = entry[col, m]
            for col in range(i + 2, GRP):
                entry[i, col], entry[n, col] = solved[col]
        for later in range(g + 1, steps):
            rows = matrix[later]
            parts_left, parts_right = [], []
            for i in range(GRP):
                weight = jnp.broadcast_to(rows[:, first + i : first + i + 1], (GRP, BLK))
                parts_left.append(weight * left[i])
                parts_right.append(weight * right[i])
            matrix[later] = rows - tree_sum(parts_left)
            inverse[later] = inverse[later] - tree_sum(parts_right)


def tile_span(index):
    return pl.ds(pl.multiple_of(index * TILE, TILE), TILE)


def block_span(index, block):
    return pl.ds(pl.multiple_of(index * TILE + block * BLK, BLK), BLK)


def put_next(work, j, tile):
    last = work.shape[0] // TILE - 1

    @pl.when(j < last)
    def _():
        work[tile_span(j), tile_span(jnp.minimum(j + 1, last))] = tile()

    @pl.when(j == last)
    def _():
        work[0:TILE, last * TILE :] = tile().T


def put_half(work, j, block):
    for b in range(2):

        @pl.when(j < 2)
        def _():
            work[block_span(j, b), block_span(jnp.minimum(j, 1) + 2, 0)] = block(b)

        @pl.when(j >= 2)
        def _():
            work[block_span(jnp.maximum(j, 2) - 2, b), block_span(j, 1)] = block(b).T


def each_pack(packs):
    own, core, y, y_core, x, x_core, top, low, top_core, low_core = packs
    return (0, own, (x,)), (1, core, (x_core,)), (2, y, (top, low)), (3, y_core, (top_core, low_core))


def rows_of(refs, b, lanes):
    if len(refs) == 2:
        return refs[b][:, lanes].astype(jnp.float32)
    return refs[0][b * BLK : (b + 1) * BLK, lanes].astype(jnp.float32)


def fill_one(ids_ref, packs, work, mixed):
    leaf, column = ids_ref[0], ids_ref[1]
    half = leaf & 1
    width = mixed.shape[1]
    for apart, mine, peers in each_pack(packs):
        j = column ^ apart
        for b in range(2):
            rows = slice(b * BLK, (b + 1) * BLK)
            mixed[rows, :] = rows_of((mine,), b, slice(0, width)) + rows_of(peers, b, slice(0, width))
        for refs, side in (((mine,), half), (peers, 1 - half)):
            for q in range(2):
                apart_columns = (2 * side + q - j) & 3
                start = width + q * TILE
                for whole in range(2):

                    @pl.when(apart_columns == whole)
                    def _():
                        for b in range(2):
                            rows = slice(b * BLK, (b + 1) * BLK)
                            lanes = slice(whole * TILE, (whole + 1) * TILE)
                            mixed[rows, lanes] = mixed[rows, lanes] + rows_of(refs, b, slice(start, start + TILE))

                for b in range(2):
                    rows = slice(b * BLK, (b + 1) * BLK)

                    @pl.when(jnp.logical_and(apart_columns == 2, j < 2))
                    def _():
                        mixed[rows, 2 * TILE :] = mixed[rows, 2 * TILE :] + rows_of(refs, b, slice(start, start + BLK))

                    @pl.when(jnp.logical_and(apart_columns == 2, j >= 2))
                    def _():
                        lanes = slice(start + b * BLK, start + (b + 1) * BLK)
                        mixed[rows, 2 * TILE :] = mixed[rows, 2 * TILE :] + rows_of(refs, 1, lanes)

        work[tile_span(j), tile_span(j)] = mixed[:, 0:TILE]
        put_next(work, j, lambda: mixed[:, TILE : 2 * TILE])
        put_half(work, j, lambda b: mixed[b * BLK : (b + 1) * BLK, 2 * TILE :])


def fill_two(ids_ref, packs, work, mixed):
    leaf, column = ids_ref[0], ids_ref[1]
    half = leaf & 1
    for apart, mine, peers in each_pack(packs):
        j = column ^ apart
        for refs, side in (((mine,), half), (peers, 1 - half)):
            for b in range(2):
                mixed[b * BLK : (b + 1) * BLK, 0 : TILE + BLK] = rows_of(refs, b, slice(0, TILE + BLK))

            @pl.when(side == (j & 1))
            def _():
                work[tile_span(j), tile_span(j)] = mixed[:, 0:TILE]
                put_half(work, j, lambda b: mixed[b * BLK : (b + 1) * BLK, TILE : TILE + BLK])

            @pl.when(side != (j & 1))
            def _():
                put_next(work, j, lambda: mixed[:, 0:TILE])


def pack_two_kernel(ids_ref, own_ref, far_ref, near_entries_ref, far_entries_ref, pack_ref, both):
    leaf, column = ids_ref[0], ids_ref[1]
    half, side = leaf & 1, (leaf >> 1) & 1
    for place, other, entries_ref in ((0, 1, near_entries_ref), (1, 0, far_entries_ref)):
        both[place] = (
            own_ref[:, place * TILE : (place + 1) * TILE].astype(jnp.float32)
            + far_ref[:, other * TILE : (other + 1) * TILE].astype(jnp.float32)
            + entries_ref[...].astype(jnp.float32)
        )
    whole = jnp.where(half == (column & 1), column, (column + 1) & 3)
    place = jnp.where((whole >> 1) == side, 0, 1)
    pack_ref[:, 0:TILE] = both[place]
    for b in range(2):
        rows = slice(b * BLK, (b + 1) * BLK)

        @pl.when(column < 2)
        def _():
            pack_ref[rows, TILE:] = both[1 - place, rows, 0:BLK]

        @pl.when(column >= 2)
        def _():
            pack_ref[rows, TILE:] = both[1 - place, BLK:, rows]


def pack_two(ids, own, far, near_entries, far_entries):
    return pl.pallas_call(
        pack_two_kernel,
        out_shape=jax.ShapeDtypeStruct((TILE, TILE + BLK), jnp.float32),
        in_specs=[SMEM] + [VMEM] * 4,
        out_specs=VMEM,
        scratch_shapes=[pltpu.VMEM((2, TILE, TILE), jnp.float32)],
        compiler_params=pltpu.CompilerParams(vmem_limit_bytes=16 * 2**20),
        name="pack_two",
    )(ids, own, far, near_entries, far_entries)


def eliminate(work, lower_ref, inverse_ref, done, block_inverse, entries, rows):
    order = work.shape[0]
    blocks = lower_ref.shape[1] // BLK
    lower_ref[...] = jnp.zeros_like(lower_ref)
    row_id = lax.broadcasted_iota(jnp.int32, (BLK, BLK), 0)
    lane_id = lax.broadcasted_iota(jnp.int32, (BLK, BLK), 1)

    def step(k, carry):
        start = pl.multiple_of(k * BLK, BLK)
        span = pl.ds(start, BLK)
        factor_diagonal(work[span, span], done, entries, rows)
        upper = jnp.where(lane_id >= row_id, done[:, 0:BLK], 0.0)
        lower_ref[span, span] = upper.T
        block_inverse[k] = done[:, BLK:]
        for fixed in range(blocks):
            after = (fixed + 1) * BLK
            if after == order:
                continue

            @pl.when(k == fixed)
            def _():
                strip = dot_rows(
                    left_parts(done[:, BLK:]), right_rows(work[after - BLK : after, after:])
                )
                column = strip.T
                lower_ref[after:, after - BLK : after] = column
                left = left_parts(column)
                right = right_rows(strip)
                width = order - after
                for top in range(0, width, TILE):
                    high = min(TILE, width - top)
                    work[after + top : after + top + high, after + top :] = work[
                        after + top : after + top + high, after + top :
                    ] - dot_rows(left[top : top + high], right[:, top:])

        return carry

    lax.fori_loop(0, blocks, step, 0)
    for tile in range(blocks * BLK // TILE):
        base = tile * TILE
        first, second = block_inverse[2 * tile], block_inverse[2 * tile + 1]
        corner = lower_ref[base + BLK : base + TILE, base : base + BLK]
        mixed = dot_rows(left_parts(corner), right_rows(first))
        mixed = -dot_rows(left_parts(second), right_rows(mixed))
        inverse_ref[tile, 0:BLK, 0:BLK] = first
        inverse_ref[tile, 0:BLK, BLK:] = jnp.zeros((BLK, BLK), jnp.float32)
        inverse_ref[tile, BLK:, 0:BLK] = mixed
        inverse_ref[tile, BLK:, BLK:] = second


def cholesky_first_kernel(fill, ids_ref, *refs):
    packs = refs[:10]
    lower_ref, inverse_ref, rest_ref, mixed, work, *scratch = refs[10:]
    fill(ids_ref, packs, work, mixed)
    eliminate(work, lower_ref, inverse_ref, *scratch)
    done = lower_ref.shape[1]
    rest_ref[...] = work[done:, done:]


def cholesky_second_kernel(rest_ref, lower_ref, inverse_ref, work, *scratch):
    work[...] = rest_ref[...]
    eliminate(work, lower_ref, inverse_ref, *scratch)


def elimination_scratch(order, blocks):
    return [
        pltpu.VMEM((order, order), jnp.float32),
        pltpu.VMEM((BLK, 2 * BLK), jnp.float32),
        pltpu.VMEM((blocks, BLK, BLK), jnp.float32),
        pltpu.VMEM((2, GRP, GRP, BLK), jnp.float32),
        pltpu.VMEM((2, GRP, 2 * BLK), jnp.float32),
    ]


def cholesky_first(ids, packs, fill, order, flops):
    done = order // 2
    return pl.pallas_call(
        functools.partial(cholesky_first_kernel, fill),
        out_shape=(
            jax.ShapeDtypeStruct((order, done), jnp.float32),
            jax.ShapeDtypeStruct((done // TILE, TILE, TILE), jnp.float32),
            jax.ShapeDtypeStruct((order - done, order - done), jnp.float32),
        ),
        in_specs=[SMEM] + [VMEM] * len(packs),
        out_specs=(VMEM,) * 3,
        scratch_shapes=[pltpu.VMEM((TILE, 2 * TILE + BLK), jnp.float32)] + elimination_scratch(order, done // BLK),
        compiler_params=pltpu.CompilerParams(vmem_limit_bytes=32 * 2**20),
        cost_estimate=pl.CostEstimate(flops=flops, bytes_accessed=10**5, transcendentals=0),
        name="cholesky_first",
    )(ids, *packs)


def cholesky_second(rest, flops):
    order = rest.shape[0]
    return pl.pallas_call(
        cholesky_second_kernel,
        out_shape=(
            jax.ShapeDtypeStruct((order, order), jnp.float32),
            jax.ShapeDtypeStruct((order // TILE, TILE, TILE), jnp.float32),
        ),
        in_specs=[VMEM],
        out_specs=(VMEM,) * 2,
        scratch_shapes=elimination_scratch(order, order // BLK),
        compiler_params=pltpu.CompilerParams(vmem_limit_bytes=24 * 2**20),
        cost_estimate=pl.CostEstimate(flops=flops, bytes_accessed=10**5, transcendentals=0),
        name="cholesky_second",
    )(rest)


def swapped(value, axis, mask):
    pairs = [(source, source ^ mask) for source in range(lax.axis_size(axis))]
    return lax.ppermute(value, axis, pairs)


def swapped_heavy(value, mask):
    groups = lax.axis_size("front")
    pairs = [
        (leaf * groups + column, leaf * groups + (column ^ mask))
        for leaf in range(lax.axis_size("leaf"))
        for column in range(groups)
        if (leaf & 1) == (column & 1)
    ]
    return lax.ppermute(value, ("leaf", "front"), pairs)


def find_tile(map_ref, owner, group, slot, count):
    found = jnp.int32(-1)
    for s in range(count):
        found = jnp.where(map_ref[owner, group, s] == slot, jnp.int32(s), found)
    return found


def column_targets(half, side):
    targets = []
    for part in (side, 1 - side):
        targets.append(2 * part + half)
        targets += [4 + 3 * (2 * part + half) + i for i in range(3)]
    return targets


def share_place(target, half):
    place = jnp.int32(0)
    for other in column_targets(half, 0):
        earlier = jnp.logical_and((other & 3) == (target & 3), other < target)
        place = place + earlier.astype(jnp.int32)
    return place


def move_tile(live, source, target, sem):
    @pl.when(live)
    def _():
        pltpu.make_async_copy(source, target, sem).start()

    @pl.when(jnp.logical_not(live))
    def _():
        target[...] = jnp.zeros(target.shape, target.dtype)

    def wait():
        @pl.when(live)
        def _():
            pltpu.make_async_copy(source, target, sem).wait()

    return wait


def move_separator(leaf, column, map_ref, child_ref, slots, groups, target_of, sems):
    count = child_ref.shape[0]
    waits = []
    for slot in slots:
        row = find_tile(map_ref, leaf, column, slot, count)
        for position, group in enumerate(groups):
            place = find_tile(map_ref, leaf, group, 0, count)
            live = jnp.logical_and(row >= 0, place >= 0)
            span = pl.ds(pl.multiple_of((jnp.maximum(place, 0) * GROUPS + group) * TILE, TILE), TILE)
            source = child_ref.at[jnp.maximum(row, 0), :, span]
            target = target_of(slot, position)
            waits.append(move_tile(live, source, target, sems.at[len(waits)]))
    return waits


def pick_pivot_kernel(ids_ref, map_ref, child_ref, entries_ref, pivot_ref, sems, entry_sem):
    leaf, column = ids_ref[0], ids_ref[1]
    count = child_ref.shape[0]
    width = 2 * TILE + BLK
    entries = pltpu.make_async_copy(
        entries_ref.at[0], pivot_ref.at[:, pl.ds(width, entries_ref.shape[-1])], entry_sem.at[0]
    )
    entries.start()
    row = find_tile(map_ref, leaf, column, 0, count)
    waits = []
    for apart in range(3):
        group = (column + apart) & 3
        place = find_tile(map_ref, leaf, group, 0, count)
        live = jnp.logical_and(row >= 0, place >= 0)
        tile = jnp.maximum(place, 0) * GROUPS + group
        source_row = child_ref.at[jnp.maximum(row, 0)]
        if apart < 2:
            moves = [(source_row.at[:, tile_span(tile)], pivot_ref.at[:, pl.ds(apart * TILE, TILE)])]
        else:
            moves = []
            for b in range(2):
                top = pl.multiple_of(jnp.where(column < 2, b * BLK, BLK), BLK)
                lanes = pl.ds(pl.multiple_of(tile * TILE + jnp.where(column < 2, 0, b * BLK), BLK), BLK)
                target = pivot_ref.at[pl.ds(b * BLK, BLK), pl.ds(2 * TILE, BLK)]
                moves.append((source_row.at[pl.ds(top, BLK), lanes], target))
        for source, target in moves:
            waits.append(move_tile(live, source, target, sems.at[len(waits)]))
    for wait in waits:
        wait()
    entries.wait()


def pick_pivot(ids, child_map, child, entries):
    width = 2 * TILE + BLK + entries.shape[-1]
    return pl.pallas_call(
        pick_pivot_kernel,
        out_shape=jax.ShapeDtypeStruct((TILE, width), child.dtype),
        in_specs=[SMEM, SMEM, ANY, ANY],
        out_specs=VMEM,
        scratch_shapes=[pltpu.SemaphoreType.DMA((GROUPS,)), pltpu.SemaphoreType.DMA((1,))],
        compiler_params=pltpu.CompilerParams(vmem_limit_bytes=56 * 2**20),
        name="pick_pivot",
    )(ids, child_map, child, entries)


def pick_rest_kernel(ids_ref, map_ref, next_ref, child_ref, *refs):
    halves_out, outs, (first_sems, sems) = refs[:2], refs[2:8], refs[8:]
    count = child_ref.shape[0]
    leaf, column = ids_ref[0], ids_ref[1]
    half, pair = leaf & 1, leaf >> 1
    slots = range(1, count + 1)
    groups = (2 * (1 - half), 2 * (1 - half) + 1, 2 * half, 2 * half + 1)
    waits = move_separator(
        leaf, column, map_ref, child_ref, slots, groups,
        lambda slot, position: halves_out[position // 2].at[slot - 1, :, pl.ds(position % 2 * TILE, TILE)],
        first_sems,
    )
    rows = [find_tile(map_ref, leaf, column, slot, count) for slot in slots]
    used = 0
    for which, device in enumerate((leaf ^ 1, leaf)):
        for position, target in enumerate(column_targets(device & 1, (device >> 1) & 1)):
            group = target & 3
            update = find_tile(next_ref, pair, group, target >> 2, count)
            place = find_tile(map_ref, leaf, group, update + 1, count)
            column_live = jnp.logical_and(update >= 0, place >= 0)
            source_span = pl.ds(pl.multiple_of((jnp.maximum(place, 0) * GROUPS + group) * TILE, TILE), TILE)
            for slot, row in enumerate(rows):
                live = jnp.logical_and(column_live, row >= 0)
                source = child_ref.at[jnp.maximum(row, 0), :, source_span]
                if position % 4 == 0:
                    goal = outs[3 * which].at[slot, :, pl.ds(position // 4 * TILE, TILE)]
                else:
                    goal = outs[3 * which + 1 + position // 4].at[slot, :, pl.ds((position % 4 - 1) * TILE, TILE)]
                waits.append(move_tile(live, source, goal, sems.at[used]))
                used += 1
    for wait in waits:
        wait()


def pick_rest(ids, child_map, next_map, child):
    count = child.shape[0]
    widths = (2 * TILE, 2 * TILE) + (2 * TILE, 3 * TILE, 3 * TILE) * 2
    return pl.pallas_call(
        pick_rest_kernel,
        out_shape=tuple(jax.ShapeDtypeStruct((count, TILE, width), child.dtype) for width in widths),
        in_specs=[SMEM, SMEM, SMEM, ANY],
        out_specs=(VMEM,) * 8,
        scratch_shapes=[pltpu.SemaphoreType.DMA((GROUPS * count,)), pltpu.SemaphoreType.DMA((16 * count,))],
        compiler_params=pltpu.CompilerParams(vmem_limit_bytes=56 * 2**20),
        cost_estimate=pl.CostEstimate(flops=0, bytes_accessed=2 * 10**7, transcendentals=0),
        name="pick_rest",
    )(ids, child_map, next_map, child)


def solve_blocks(coupling_ref, lowers, inverses, panel_ref):
    split = lowers[0].shape[1]
    solved = []
    for k in range(panel_ref.shape[1] // TILE):
        span = slice(k * TILE, (k + 1) * TILE)
        rest = coupling_ref[:, span]
        if k:
            left = jnp.concatenate([part[0] for part in solved], axis=1)
            low = jnp.concatenate([part[1] for part in solved], axis=1)
            strip = lowers[0][span, 0 : min(k * TILE, split)]
            if k * TILE > split:
                inner = slice(k * TILE - split, (k + 1) * TILE - split)
                strip = jnp.concatenate([strip, lowers[1][inner, 0 : k * TILE - split]], axis=1)
            high_lower, low_lower = halves(strip)
            rest = rest - dot_lanes(
                jnp.concatenate([left, low, left], axis=1),
                jnp.concatenate([high_lower, high_lower, low_lower], axis=1),
            )
        tiles = split // TILE
        inverse = inverses[0][k] if k < tiles else inverses[1][k - tiles]
        block = dot_lanes(left_parts(rest), right_lanes(inverse))
        panel_ref[:, span] = block
        solved.append(halves(block))
    return jnp.concatenate([part[0] for part in solved], axis=1)


def write_factor(column, offset, lowers, panel, factor_ref):
    width = factor_ref.shape[-1]
    split = lowers[0].shape[1]
    per = split // width
    tiles = split // TILE
    span = pl.ds(pl.multiple_of(offset * width, width), width)
    factor_ref[0] = jnp.zeros(factor_ref.shape[1:], factor_ref.dtype)

    @pl.when(offset < per)
    def _():
        inner = pl.ds(pl.multiple_of(jnp.minimum(offset, per - 1) * width, width), width)
        factor_ref[0] = lowers[0][pl.ds(pl.multiple_of(column * TILE, TILE), TILE), inner]

    @pl.when(jnp.logical_and(offset >= per, column >= tiles))
    def _():
        inner = pl.ds(pl.multiple_of(jnp.maximum(offset - per, 0) * width, width), width)
        rows = pl.ds(pl.multiple_of(jnp.maximum(column - tiles, 0) * TILE, TILE), TILE)
        factor_ref[0] = lowers[1][rows, inner]

    for s in range(factor_ref.shape[0] - 1):
        factor_ref[s + 1] = panel[s * TILE : (s + 1) * TILE, span]


def panel_one_kernel(ids_ref, next_ref, mine_ref, peer_ref, *refs):
    lowers, inverses = refs[:2], refs[2:4]
    factor_ref, round_ref, first_ref, second_ref, third_ref, coupling, panel = refs[4:]
    leaf, column = ids_ref[0], ids_ref[1]
    half, pair = leaf & 1, leaf >> 1
    count, _, width = mine_ref.shape
    for ref, place in ((mine_ref, half), (peer_ref, 1 - half)):
        span = pl.ds(pl.multiple_of(place * width, width), width)
        for s in range(count):
            coupling[s * TILE : (s + 1) * TILE, span] = ref[s].astype(jnp.float32)
    rounded = solve_blocks(coupling, lowers, inverses, panel)
    for s in range(count):
        round_ref[s] = rounded[s * TILE : (s + 1) * TILE]
    write_factor(column, half, lowers, panel, factor_ref)
    heavy = half == (column & 1)
    for a, share_ref in ((0, first_ref), (jnp.where(heavy, 1, 0), second_ref), (2, third_ref)):
        slot = jnp.int32(0)
        for target in column_targets(half, 0):
            hit = jnp.logical_and((target & 3) == column, share_place(target, half) == a)
            slot = jnp.where(hit, target >> 2, slot)
        tile = find_tile(next_ref, pair, column, slot, count)
        share_ref[...] = round_ref[jnp.maximum(tile, 0)]


def panel_one(ids, next_map, mine, peer, lowers, inverses):
    count = mine.shape[0]
    order = lowers[0].shape[0]
    return pl.pallas_call(
        panel_one_kernel,
        out_shape=(
            jax.ShapeDtypeStruct((count + 1, TILE, order // 2), jnp.float32),
            jax.ShapeDtypeStruct((count, TILE, order), jnp.bfloat16),
        )
        + (jax.ShapeDtypeStruct((TILE, order), jnp.bfloat16),) * 3,
        in_specs=[SMEM, SMEM] + [VMEM] * 6,
        out_specs=(VMEM,) * 5,
        scratch_shapes=[
            pltpu.VMEM((count * TILE, order), jnp.float32),
            pltpu.VMEM((count * TILE, order), jnp.float32),
        ],
        compiler_params=PARAMS,
        cost_estimate=pl.CostEstimate(flops=10**9, bytes_accessed=10**6, transcendentals=0),
        name="panel_one",
    )(ids, next_map, mine, peer, *lowers, *inverses)


def panel_two_kernel(ids_ref, own_ref, x_ref, z_ref, both_ref, *refs):
    lowers, inverses = refs[:2], refs[2:4]
    factor_ref, round_ref, share_ref, coupling, panel = refs[4:]
    leaf, column = ids_ref[0], ids_ref[1]
    half, side = leaf & 1, (leaf >> 1) & 1
    quarter = leaf & 3
    count = round_ref.shape[0]
    for place, ref in (
        (2 * side + half, own_ref),
        (2 * side + 1 - half, x_ref),
        (2 * (1 - side) + half, z_ref),
        (2 * (1 - side) + 1 - half, both_ref),
    ):
        coupling[:, pl.ds(pl.multiple_of(place * TILE, TILE), TILE)] = ref[...].astype(jnp.float32)
    rounded = solve_blocks(coupling, lowers, inverses, panel)
    for s in range(count):
        round_ref[s] = rounded[s * TILE : (s + 1) * TILE]
    write_factor(column, quarter, lowers, panel, factor_ref)
    chosen = jnp.int32(0)
    for i in range(3):
        tile = 3 * quarter + i
        chosen = jnp.where((tile & 3) == column, tile >> 2, chosen)
    share_ref[...] = round_ref[chosen]


def panel_two(ids, parts, lowers, inverses):
    rows = parts[0].shape[0]
    count = rows // TILE
    order = lowers[0].shape[0]
    return pl.pallas_call(
        panel_two_kernel,
        out_shape=(
            jax.ShapeDtypeStruct((count + 1, TILE, order // 4), jnp.float32),
            jax.ShapeDtypeStruct((count, TILE, order), jnp.bfloat16),
            jax.ShapeDtypeStruct((TILE, order), jnp.bfloat16),
        ),
        in_specs=[SMEM] + [VMEM] * 8,
        out_specs=(VMEM, VMEM, VMEM),
        scratch_shapes=[pltpu.VMEM((rows, order), jnp.float32), pltpu.VMEM((rows, order), jnp.float32)],
        compiler_params=PARAMS,
        cost_estimate=pl.CostEstimate(flops=10**9, bytes_accessed=10**6, transcendentals=0),
        name="panel_two",
    )(ids, *parts, *lowers, *inverses)


def take_tile(owner, column, refs, live, target, sem):
    for apart, ref in enumerate(refs):

        @pl.when(jnp.logical_and(live, (owner ^ column) == apart))
        def _():
            pltpu.make_async_copy(ref, target, sem).start()


def start_shared(ids_ref, positions, firsts, thirds, taken, sems):
    leaf, column = ids_ref[0], ids_ref[1]
    half, side = leaf & 1, (leaf >> 1) & 1
    targets = column_targets(half, side)
    copies = []
    for i, position in enumerate(positions):
        target = targets[position]
        group = target & 3
        place = share_place(target, half)
        take_tile(group, column, firsts, place < 2, taken.at[i], sems.at[i])
        if thirds:
            take_tile(group, column, thirds, place == 2, taken.at[i], sems.at[i])
        copies.append(pltpu.make_async_copy(firsts[0], taken.at[i], sems.at[i]))
    return copies


class Loads:
    def __init__(self, sources, targets, sems):
        self.copies = [pltpu.make_async_copy(*each, sems.at[k]) for k, each in enumerate(zip(sources, targets))]

    def start(self, chosen):
        for k in chosen:
            self.copies[k].start()

    def wait(self, chosen):
        for k in chosen:
            self.copies[k].wait()


def update_columns(ids_ref, next_ref, positions, shared, refs, write):
    leaf, column = ids_ref[0], ids_ref[1]
    half, side, pair = leaf & 1, (leaf >> 1) & 1, leaf >> 1
    sources, (keep_in, peer_in, round_in, taken, tiles, sems, load_sems) = refs
    count = keep_in.shape[0]
    loads = Loads(sources, (keep_in, peer_in, round_in), load_sems)
    loads.start((2,))
    copies = start_shared(ids_ref, positions, *shared, taken, sems)
    loads.start((0, 1))
    targets = column_targets(half, side)
    rows = [find_tile(next_ref, pair, column, slot, count) for slot in range(count + 1)]
    tiles[:, count] = jnp.zeros_like(tiles[:, count])
    loads.wait((2,))
    for i, position in enumerate(positions):
        target = targets[position]
        live = find_tile(next_ref, pair, target & 3, target >> 2, count) >= 0
        span = slice(i * TILE, (i + 1) * TILE)
        copies[i].wait()
        for s in range(count):
            product = dot_lanes(round_in[s], taken[i])
            if i == 0 and s == 0:
                loads.wait((0, 1))
            value = keep_in[s, :, span].astype(jnp.float32) + peer_in[s, :, span].astype(jnp.float32) - product
            tiles[i, s] = jnp.where(live, value, 0.0).astype(jnp.bfloat16)
        for slot, row in enumerate(rows):
            write(i, slot, lambda row=row: tiles[i, jnp.where(row < 0, count, row)])


def update_scratch(count, width, order):
    return [
        pltpu.VMEM((count, TILE, width * TILE), jnp.bfloat16),
        pltpu.VMEM((count, TILE, width * TILE), jnp.bfloat16),
        pltpu.VMEM((count, TILE, order), jnp.bfloat16),
        pltpu.VMEM((width, TILE, order), jnp.bfloat16),
        pltpu.VMEM((width, count + 1, TILE, TILE), jnp.bfloat16),
        pltpu.SemaphoreType.DMA((width,)),
        pltpu.SemaphoreType.DMA((3,)),
    ]


def update_separator_kernel(ids_ref, next_ref, *refs):
    sources, firsts, (pivot_ref, near_ref, far_ref), scratch = refs[:3], refs[3:7], refs[7:10], refs[10:]

    def write(i, slot, tile):
        if slot == 0:
            pivot_ref[:, i * TILE : (i + 1) * TILE] = tile()
        else:
            (near_ref, far_ref)[i][slot - 1] = tile()

    update_columns(ids_ref, next_ref, (0, 4), (firsts, ()), (sources, scratch), write)


def update_separator(ids, next_map, keep, peer, rounded, firsts):
    count, _, order = rounded.shape
    tile = jax.ShapeDtypeStruct((count, TILE, TILE), jnp.bfloat16)
    return pl.pallas_call(
        update_separator_kernel,
        out_shape=(jax.ShapeDtypeStruct((TILE, 2 * TILE), jnp.bfloat16), tile, tile),
        in_specs=[SMEM, SMEM] + [ANY] * 7,
        out_specs=(VMEM, VMEM, VMEM),
        scratch_shapes=update_scratch(count, 2, order),
        compiler_params=pltpu.CompilerParams(vmem_limit_bytes=56 * 2**20),
        cost_estimate=pl.CostEstimate(flops=10**8, bytes_accessed=10**5, transcendentals=0),
        name="update_separator",
    )(ids, next_map, keep, peer, rounded, *firsts)


def update_trailing_kernel(positions, ids_ref, next_ref, *refs):
    sources, seconds, thirds, out_ref, scratch = refs[:3], refs[3:7], refs[7:11], refs[11], refs[12:]

    def write(i, slot, tile):
        if slot:
            out_ref[slot - 1, :, i * TILE : (i + 1) * TILE] = tile()

    update_columns(ids_ref, next_ref, positions, (seconds, thirds), (sources, scratch), write)


def update_trailing(ids, next_map, keep, peer, rounded, seconds, thirds, positions):
    count, _, order = rounded.shape
    width = len(positions)
    return pl.pallas_call(
        functools.partial(update_trailing_kernel, positions),
        out_shape=jax.ShapeDtypeStruct((count, TILE, width * TILE), jnp.bfloat16),
        in_specs=[SMEM, SMEM] + [ANY] * 11,
        out_specs=VMEM,
        scratch_shapes=update_scratch(count, width, order),
        compiler_params=pltpu.CompilerParams(vmem_limit_bytes=56 * 2**20),
        cost_estimate=pl.CostEstimate(flops=4 * 10**9, bytes_accessed=12 * 10**6, transcendentals=0),
        name="update_trailing",
    )(ids, next_map, keep, peer, rounded, *seconds, *thirds)


def update_two_kernel(ids_ref, *refs):
    sources, firsts, out_ref = refs[:3], refs[3:7], refs[7]
    near_in, far_in, round_in, taken, sems, load_sems = refs[8:]
    quarter, column = ids_ref[0] & 3, ids_ref[1]
    loads = Loads(sources, (near_in, far_in, round_in), load_sems)
    loads.start((2,))
    for i in range(3):
        take_tile((3 * quarter + i) & 3, column, firsts, True, taken.at[i], sems.at[i])
    loads.start((0, 1))
    loads.wait((2,))
    for i in range(3):
        span = slice(i * TILE, (i + 1) * TILE)
        pltpu.make_async_copy(firsts[0], taken.at[i], sems.at[i]).wait()
        for s in range(near_in.shape[0]):
            product = dot_lanes(round_in[s], taken[i])
            if i == 0 and s == 0:
                loads.wait((0, 1))
            total = near_in[s, :, span].astype(jnp.float32) + far_in[s, :, span].astype(jnp.float32)
            out_ref[s, :, span] = (total - product).astype(jnp.bfloat16)


def update_two(ids, near, far, rounded, firsts):
    order = rounded.shape[-1]
    return pl.pallas_call(
        update_two_kernel,
        out_shape=jax.ShapeDtypeStruct(near.shape, jnp.bfloat16),
        in_specs=[SMEM] + [ANY] * 7,
        out_specs=VMEM,
        scratch_shapes=[
            pltpu.VMEM(near.shape, jnp.bfloat16),
            pltpu.VMEM(far.shape, jnp.bfloat16),
            pltpu.VMEM(rounded.shape, jnp.bfloat16),
            pltpu.VMEM((3, TILE, order), jnp.bfloat16),
            pltpu.SemaphoreType.DMA((3,)),
            pltpu.SemaphoreType.DMA((3,)),
        ],
        compiler_params=pltpu.CompilerParams(vmem_limit_bytes=56 * 2**20),
        cost_estimate=pl.CostEstimate(flops=2 * 10**9, bytes_accessed=10**7, transcendentals=0),
        name="update_two",
    )(ids, near, far, rounded, *firsts)


def over_square(pack, beside):
    half = pack.shape[0] // 2
    x, y, core = swapped(pack, "leaf", 1), swapped(pack, "front", 2), swapped(pack, "front", 1)
    x, y = lax.optimization_barrier((x, y, beside))[:2]
    top = swapped(y[:half], "leaf", 1)
    low = swapped(x[half:], "front", 2)
    x_core, y_core = swapped(x, "front", 1), swapped(y, "front", 1)
    top_core, low_core = swapped(top, "front", 1), swapped(low, "front", 1)
    return (pack, core, y, y_core, x, x_core, top, low, top_core, low_core)


def over_front(tile, y, *earlier):
    return (tile, swapped(tile, "front", 1), y, swapped(after(y, *earlier), "front", 1))


def over_heavy(tile, y, *earlier):
    return (tile, swapped_heavy(tile, 1), y, swapped_heavy(after(y, *earlier), 1))


def after(value, *earlier):
    return lax.optimization_barrier((value, *earlier))[0]


def own_mask(mask, front, column, count):
    rows = lax.dynamic_index_in_dim(mask, front, 0, keepdims=False).reshape(count, GROUPS, -1)
    return lax.dynamic_index_in_dim(rows, column, 1, keepdims=False).astype(jnp.float32)


def body(child_update, sep_one, sep_two, map_one, map_two, mask_one, mask_two):
    column = lax.axis_index("front")
    leaf = lax.axis_index("leaf")
    quad, quarter = leaf >> 2, leaf & 3
    ids = jnp.stack([leaf, column]).astype(jnp.int32)
    child = child_update[0, 0, 0]
    entries_one = sep_one[0, 0, 0]
    entries_two = sep_two[0, 0, 0]
    count = child.shape[0]
    order = GROUPS * TILE
    maps_one = map_one[:, 0]
    maps_two = map_two[:, 0]

    pivot_mine = pick_pivot(ids, maps_one, child, entries_one)
    mask_first = own_mask(mask_one, leaf >> 1, column, count)
    mask_first = lax.dynamic_slice_in_dim(mask_first, 2 * (leaf & 1), 2, 1)
    mask_first = jnp.repeat(mask_first, TILE, axis=1)[:, None, :]
    mask_second = lax.dynamic_index_in_dim(own_mask(mask_two, quad, column, count), quarter, 1, keepdims=False)
    coupling_send, coupling_keep, sep_send, near_send, far_send, sep_keep, near_keep, far_keep = pick_rest(
        after(ids, mask_first, mask_second), maps_one, maps_two, child
    )
    packs = over_square(pivot_mine, coupling_send)
    coupling_got = swapped(after(coupling_send, packs[4]), "leaf", 1)
    entries_far = swapped(entries_two[0], "leaf", 2)
    lower, inverse, rest = cholesky_first(ids, packs, fill_one, order, 2 * 10**10)
    coupling = (
        coupling_keep.astype(jnp.float32)
        + after(coupling_got, rest).astype(jnp.float32)
        + entries_one[1:].astype(jnp.float32) * mask_first
    )
    coupling_peer = swapped(coupling.astype(jnp.bfloat16), "leaf", 1)
    lower_rest, inverse_rest = cholesky_second(rest, 2 * 10**10)
    sep_peer = swapped(after(sep_send, lower_rest), "leaf", 1)
    far_peer = swapped(after(far_send, lower_rest), "leaf", 1)
    factor_one, rounded, first, second, third = panel_one(
        ids, maps_two, coupling, coupling_peer, (lower, lower_rest), (inverse, inverse_rest)
    )
    first_y = swapped_heavy(first, 2)
    firsts = over_heavy(first, first_y, sep_peer)
    pivot_own, near_coupling, far_coupling = update_separator(ids, maps_two, sep_keep, sep_peer, rounded, firsts)
    second_y = swapped(after(second, first_y), "front", 2)
    third_y = swapped_heavy(after(third, first_y), 2)

    pivot_far = swapped(pivot_own, "leaf", 2)
    seconds = over_front(second, second_y, pivot_far)
    thirds = over_heavy(third, third_y, pivot_far)
    pivot_pack = pack_two(ids, pivot_own, pivot_far, entries_two[0], entries_far)
    far_trailing = update_trailing(
        ids, maps_two, far_keep, far_peer, after(rounded, pivot_far), seconds, thirds, (5, 6, 7)
    )
    packs = over_square(after(pivot_pack, far_peer), far_trailing)
    coupling_far = swapped(after(far_coupling, pivot_far), "leaf", 2)
    coupling = (
        near_coupling.astype(jnp.float32)
        + coupling_far.astype(jnp.float32)
        + entries_two[1:].astype(jnp.float32) * mask_second[:, None, None]
    ).reshape(count * TILE, TILE)
    coupling_sent = after(coupling.astype(jnp.bfloat16), packs[5])
    coupling_x, coupling_z, coupling_xz = (swapped(coupling_sent, "leaf", mask) for mask in (1, 2, 3))
    trailing_far = swapped(after(far_trailing, packs[5]), "leaf", 2)
    near_peer = swapped(after(near_send, packs[6]), "leaf", 1)
    lower, inverse, rest = cholesky_first(ids, packs, fill_two, order, 2 * 10**10)
    lower_rest, inverse_rest = cholesky_second(rest, 2 * 10**10)
    factor_two, rounded_two, share = panel_two(
        ids, (coupling, coupling_x, coupling_z, coupling_xz), (lower, lower_rest), (inverse, inverse_rest)
    )
    near_trailing = update_trailing(ids, maps_two, near_keep, near_peer, rounded, seconds, thirds, (1, 2, 3))
    shares = over_front(share, swapped(share, "front", 2), near_trailing, trailing_far)
    update = update_two(ids, near_trailing, trailing_far, rounded_two, shares)
    return (factor_one[None, None, None], factor_two[None, None, None], update[None, None, None])


def solution(mesh):
    split = P("leaf", "front", None, None, None, None)
    return jax.shard_map(
        body,
        mesh=mesh,
        in_specs=(split, split, split, P(), P(), P(), P()),
        out_specs=(split, split, split),
        check_vma=False,
    )
```

```python
import functools

import jax
import jax.numpy as jnp
from jax import lax
from jax.experimental import pallas as pl
from jax.experimental.pallas import tpu as pltpu
from jax.sharding import PartitionSpec as P

VMEM = pl.BlockSpec(memory_space=pltpu.VMEM)
SMEM = pl.BlockSpec(memory_space=pltpu.SMEM)
ANY = pl.BlockSpec(memory_space=pl.ANY)
HBM = pl.BlockSpec(memory_space=pltpu.HBM)
GROUPS = 4
PARAMS = pltpu.CompilerParams(vmem_limit_bytes=32 * 2**20)
BLK = 128
GRP = 8
TILE = 256
NT = (((1,), (1,)), ((), ()))


def halves(x):
    high = x.astype(jnp.bfloat16)
    low = (x - high.astype(jnp.float32)).astype(jnp.bfloat16)
    return high, low


def left_parts(x):
    high, low = halves(x)
    return jnp.concatenate([high, low, high], axis=1)


def right_rows(x):
    high, low = halves(x)
    return jnp.concatenate([high, high, low], axis=0)


def right_lanes(x):
    high, low = halves(x)
    return jnp.concatenate([high, high, low], axis=1)


def dot_rows(left, right):
    return jnp.dot(left, right, preferred_element_type=jnp.float32)


def dot_lanes(left, right):
    return lax.dot_general(left, right, NT, preferred_element_type=jnp.float32)


def spread_row(ref, index):
    return jnp.broadcast_to(ref[index], (GRP, BLK))


def tree_sum(parts):
    while len(parts) > 1:
        parts = [parts[k] + parts[k + 1] for k in range(0, len(parts), 2)]
    return parts[0]


def factor_diagonal(block, done_ref, pivot_ref, rows_ref):
    steps = BLK // GRP
    row_id = lax.broadcasted_iota(jnp.int32, (GRP, BLK), 0)
    lane_id = lax.broadcasted_iota(jnp.int32, (GRP, BLK), 1)
    matrix = [block[GRP * g : GRP * (g + 1), :] for g in range(steps)]
    inverse = [jnp.where(lane_id == row_id + GRP * g, 1.0, 0.0).astype(jnp.float32) for g in range(steps)]
    for g in range(steps):
        first = GRP * g
        slot = g % 2
        current = matrix[g]
        rows_ref[slot, :, 0:BLK] = current
        rows_ref[slot, :, BLK:] = inverse[g]
        for i in range(GRP):
            pivot_ref[slot, i] = jnp.broadcast_to(current[:, first + i : first + i + 1], (GRP, BLK))
        entry = {}
        for m in range(GRP):
            for i in range(m + 1):
                entry[m, i] = jnp.broadcast_to(pivot_ref[slot, i, m : m + 1, :], (GRP, BLK))
                entry[i, m] = entry[m, i]
        left = [jnp.broadcast_to(rows_ref[slot, m : m + 1, 0:BLK], (GRP, BLK)) for m in range(GRP)]
        right = [jnp.broadcast_to(rows_ref[slot, m : m + 1, BLK:], (GRP, BLK)) for m in range(GRP)]
        for i in range(0, GRP, 2):
            n = i + 1
            a, b, c = entry[i, i], entry[n, i], entry[n, n]
            root = lax.rsqrt(a)
            root_both = lax.rsqrt(a * c - b * b)
            scale = root_both * root_both
            second_root = root * root_both

            def solve(x, y):
                return c * x - b * y, a * y - b * x

            solved = {}
            for name, rows_now in (("left", left), ("right", right)):
                raw = solve(rows_now[i], rows_now[n])
                lanes = slice(0, BLK) if name == "left" else slice(BLK, 2 * BLK)
                done_ref[first + i : first + i + 1, lanes] = (rows_now[i] * root)[0:1]
                done_ref[first + n : first + n + 1, lanes] = (raw[1] * second_root)[0:1]
                rows_now[i], rows_now[n] = raw[0] * scale, raw[1] * scale
            for col in range(i + 2, GRP):
                raw = solve(entry[i, col], entry[n, col])
                solved[col] = (raw[0] * scale, raw[1] * scale)
            for m in range(GRP):
                if m in (i, n):
                    continue
                weight, other = entry[m, i], entry[m, n]
                for rows_now in (left, right):
                    rows_now[m] = rows_now[m] - (weight * rows_now[i] + other * rows_now[n])
                for col in range(i + 2, GRP):
                    if m > col:
                        continue
                    entry[m, col] = entry[m, col] - (weight * solved[col][0] + other * solved[col][1])
            for m in range(i + 2, GRP):
                for col in range(i + 2, m):
                    entry[m, col] = entry[col, m]
            for col in range(i + 2, GRP):
                entry[i, col], entry[n, col] = solved[col]
        for later in range(g + 1, steps):
            rows = matrix[later]
            parts_left, parts_right = [], []
            for i in range(GRP):
                weight = jnp.broadcast_to(rows[:, first + i : first + i + 1], (GRP, BLK))
                parts_left.append(weight * left[i])
                parts_right.append(weight * right[i])
            matrix[later] = rows - tree_sum(parts_left)
            inverse[later] = inverse[later] - tree_sum(parts_right)


def tile_span(index):
    return pl.ds(pl.multiple_of(index * TILE, TILE), TILE)


def block_span(index, block):
    return pl.ds(pl.multiple_of(index * TILE + block * BLK, BLK), BLK)


def put_next(work, j, tile):
    last = work.shape[0] // TILE - 1

    @pl.when(j < last)
    def _():
        work[tile_span(j), tile_span(jnp.minimum(j + 1, last))] = tile()

    @pl.when(j == last)
    def _():
        work[0:TILE, last * TILE :] = tile().T


def put_half(work, j, block):
    for b in range(2):

        @pl.when(j < 2)
        def _():
            work[block_span(j, b), block_span(jnp.minimum(j, 1) + 2, 0)] = block(b)

        @pl.when(j >= 2)
        def _():
            work[block_span(jnp.maximum(j, 2) - 2, b), block_span(j, 1)] = block(b).T


def each_pack(packs):
    own, core, y, y_core, x, x_core, top, low, top_core, low_core = packs
    return (0, own, (x,)), (1, core, (x_core,)), (2, y, (top, low)), (3, y_core, (top_core, low_core))


def rows_of(refs, b, lanes):
    if len(refs) == 2:
        return refs[b][:, lanes].astype(jnp.float32)
    return refs[0][b * BLK : (b + 1) * BLK, lanes].astype(jnp.float32)


def fill_one(ids_ref, packs, work, mixed):
    leaf, column = ids_ref[0], ids_ref[1]
    half = leaf & 1
    width = mixed.shape[1]
    for apart, mine, peers in each_pack(packs):
        j = column ^ apart
        for b in range(2):
            rows = slice(b * BLK, (b + 1) * BLK)
            mixed[rows, :] = rows_of((mine,), b, slice(0, width)) + rows_of(peers, b, slice(0, width))
        for refs, side in (((mine,), half), (peers, 1 - half)):
            for q in range(2):
                apart_columns = (2 * side + q - j) & 3
                start = width + q * TILE
                for whole in range(2):

                    @pl.when(apart_columns == whole)
                    def _():
                        for b in range(2):
                            rows = slice(b * BLK, (b + 1) * BLK)
                            lanes = slice(whole * TILE, (whole + 1) * TILE)
                            mixed[rows, lanes] = mixed[rows, lanes] + rows_of(refs, b, slice(start, start + TILE))

                for b in range(2):
                    rows = slice(b * BLK, (b + 1) * BLK)

                    @pl.when(jnp.logical_and(apart_columns == 2, j < 2))
                    def _():
                        mixed[rows, 2 * TILE :] = mixed[rows, 2 * TILE :] + rows_of(refs, b, slice(start, start + BLK))

                    @pl.when(jnp.logical_and(apart_columns == 2, j >= 2))
                    def _():
                        lanes = slice(start + b * BLK, start + (b + 1) * BLK)
                        mixed[rows, 2 * TILE :] = mixed[rows, 2 * TILE :] + rows_of(refs, 1, lanes)

        work[tile_span(j), tile_span(j)] = mixed[:, 0:TILE]
        put_next(work, j, lambda: mixed[:, TILE : 2 * TILE])
        put_half(work, j, lambda b: mixed[b * BLK : (b + 1) * BLK, 2 * TILE :])


def fill_two(ids_ref, packs, work, mixed):
    leaf, column = ids_ref[0], ids_ref[1]
    half = leaf & 1
    for apart, mine, peers in each_pack(packs):
        j = column ^ apart
        for refs, side in (((mine,), half), (peers, 1 - half)):
            for b in range(2):
                mixed[b * BLK : (b + 1) * BLK, 0 : TILE + BLK] = rows_of(refs, b, slice(0, TILE + BLK))

            @pl.when(side == (j & 1))
            def _():
                work[tile_span(j), tile_span(j)] = mixed[:, 0:TILE]
                put_half(work, j, lambda b: mixed[b * BLK : (b + 1) * BLK, TILE : TILE + BLK])

            @pl.when(side != (j & 1))
            def _():
                put_next(work, j, lambda: mixed[:, 0:TILE])


def pack_two_kernel(ids_ref, own_ref, far_ref, near_entries_ref, far_entries_ref, pack_ref, both):
    leaf, column = ids_ref[0], ids_ref[1]
    half, side = leaf & 1, (leaf >> 1) & 1
    for place, other, entries_ref in ((0, 1, near_entries_ref), (1, 0, far_entries_ref)):
        both[place] = (
            own_ref[:, place * TILE : (place + 1) * TILE].astype(jnp.float32)
            + far_ref[:, other * TILE : (other + 1) * TILE].astype(jnp.float32)
            + entries_ref[...].astype(jnp.float32)
        )
    whole = jnp.where(half == (column & 1), column, (column + 1) & 3)
    place = jnp.where((whole >> 1) == side, 0, 1)
    pack_ref[:, 0:TILE] = both[place]
    for b in range(2):
        rows = slice(b * BLK, (b + 1) * BLK)

        @pl.when(column < 2)
        def _():
            pack_ref[rows, TILE:] = both[1 - place, rows, 0:BLK]

        @pl.when(column >= 2)
        def _():
            pack_ref[rows, TILE:] = both[1 - place, BLK:, rows]


def pack_two(ids, own, far, near_entries, far_entries):
    return pl.pallas_call(
        pack_two_kernel,
        out_shape=jax.ShapeDtypeStruct((TILE, TILE + BLK), jnp.float32),
        in_specs=[SMEM] + [VMEM] * 4,
        out_specs=VMEM,
        scratch_shapes=[pltpu.VMEM((2, TILE, TILE), jnp.float32)],
        compiler_params=pltpu.CompilerParams(vmem_limit_bytes=56 * 2**20),
        name="pack_two",
    )(ids, own, far, near_entries, far_entries)


def eliminate(work, lower_ref, inverse_ref, done, block_inverse, entries, rows):
    order = work.shape[0]
    blocks = lower_ref.shape[1] // BLK
    lower_ref[...] = jnp.zeros_like(lower_ref)
    row_id = lax.broadcasted_iota(jnp.int32, (BLK, BLK), 0)
    lane_id = lax.broadcasted_iota(jnp.int32, (BLK, BLK), 1)

    def step(k, carry):
        start = pl.multiple_of(k * BLK, BLK)
        span = pl.ds(start, BLK)
        factor_diagonal(work[span, span], done, entries, rows)
        upper = jnp.where(lane_id >= row_id, done[:, 0:BLK], 0.0)
        lower_ref[span, span] = upper.T
        block_inverse[k] = done[:, BLK:]
        for fixed in range(blocks):
            after = (fixed + 1) * BLK
            if after == order:
                continue

            @pl.when(k == fixed)
            def _():
                strip = dot_rows(
                    left_parts(done[:, BLK:]), right_rows(work[after - BLK : after, after:])
                )
                column = strip.T
                lower_ref[after:, after - BLK : after] = column
                left = left_parts(column)
                right = right_rows(strip)
                width = order - after
                for top in range(0, width, TILE):
                    high = min(TILE, width - top)
                    work[after + top : after + top + high, after + top :] = work[
                        after + top : after + top + high, after + top :
                    ] - dot_rows(left[top : top + high], right[:, top:])

        return carry

    lax.fori_loop(0, blocks, step, 0)
    for tile in range(blocks * BLK // TILE):
        base = tile * TILE
        first, second = block_inverse[2 * tile], block_inverse[2 * tile + 1]
        corner = lower_ref[base + BLK : base + TILE, base : base + BLK]
        mixed = dot_rows(left_parts(corner), right_rows(first))
        mixed = -dot_rows(left_parts(second), right_rows(mixed))
        inverse_ref[tile, 0:BLK, 0:BLK] = first
        inverse_ref[tile, 0:BLK, BLK:] = jnp.zeros((BLK, BLK), jnp.float32)
        inverse_ref[tile, BLK:, 0:BLK] = mixed
        inverse_ref[tile, BLK:, BLK:] = second


def cholesky_first_kernel(fill, ids_ref, *refs):
    packs = refs[:10]
    lower_ref, inverse_ref, rest_ref, mixed, work, *scratch = refs[10:]
    fill(ids_ref, packs, work, mixed)
    eliminate(work, lower_ref, inverse_ref, *scratch)
    done = lower_ref.shape[1]
    rest_ref[...] = work[done:, done:]


def cholesky_second_kernel(rest_ref, lower_ref, inverse_ref, work, *scratch):
    work[...] = rest_ref[...]
    eliminate(work, lower_ref, inverse_ref, *scratch)


def elimination_scratch(order, blocks):
    return [
        pltpu.VMEM((order, order), jnp.float32),
        pltpu.VMEM((BLK, 2 * BLK), jnp.float32),
        pltpu.VMEM((blocks, BLK, BLK), jnp.float32),
        pltpu.VMEM((2, GRP, GRP, BLK), jnp.float32),
        pltpu.VMEM((2, GRP, 2 * BLK), jnp.float32),
    ]


def cholesky_first(ids, packs, fill, order, flops):
    done = order // 2
    return pl.pallas_call(
        functools.partial(cholesky_first_kernel, fill),
        out_shape=(
            jax.ShapeDtypeStruct((order, done), jnp.float32),
            jax.ShapeDtypeStruct((done // TILE, TILE, TILE), jnp.float32),
            jax.ShapeDtypeStruct((order - done, order - done), jnp.float32),
        ),
        in_specs=[SMEM] + [VMEM] * len(packs),
        out_specs=(VMEM,) * 3,
        scratch_shapes=[pltpu.VMEM((TILE, 2 * TILE + BLK), jnp.float32)] + elimination_scratch(order, done // BLK),
        compiler_params=pltpu.CompilerParams(vmem_limit_bytes=32 * 2**20),
        cost_estimate=pl.CostEstimate(flops=flops, bytes_accessed=10**5, transcendentals=0),
        name="cholesky_first",
    )(ids, *packs)


def cholesky_second(rest, flops):
    order = rest.shape[0]
    return pl.pallas_call(
        cholesky_second_kernel,
        out_shape=(
            jax.ShapeDtypeStruct((order, order), jnp.float32),
            jax.ShapeDtypeStruct((order // TILE, TILE, TILE), jnp.float32),
        ),
        in_specs=[VMEM],
        out_specs=(VMEM,) * 2,
        scratch_shapes=elimination_scratch(order, order // BLK),
        compiler_params=pltpu.CompilerParams(vmem_limit_bytes=24 * 2**20),
        cost_estimate=pl.CostEstimate(flops=flops, bytes_accessed=10**5, transcendentals=0),
        name="cholesky_second",
    )(rest)


def swapped(value, axis, mask):
    pairs = [(source, source ^ mask) for source in range(lax.axis_size(axis))]
    return lax.ppermute(value, axis, pairs)


def swapped_heavy(value, mask):
    groups = lax.axis_size("front")
    pairs = [
        (leaf * groups + column, leaf * groups + (column ^ mask))
        for leaf in range(lax.axis_size("leaf"))
        for column in range(groups)
        if (leaf & 1) == (column & 1)
    ]
    return lax.ppermute(value, ("leaf", "front"), pairs)


def find_tile(map_ref, owner, group, slot, count):
    found = jnp.int32(-1)
    for s in range(count):
        found = jnp.where(map_ref[owner, group, s] == slot, jnp.int32(s), found)
    return found


def column_targets(half, side):
    targets = []
    for part in (side, 1 - side):
        targets.append(2 * part + half)
        targets += [4 + 3 * (2 * part + half) + i for i in range(3)]
    return targets


def share_place(target, half):
    place = jnp.int32(0)
    for other in column_targets(half, 0):
        earlier = jnp.logical_and((other & 3) == (target & 3), other < target)
        place = place + earlier.astype(jnp.int32)
    return place


def move_tile(live, source, target, sem):
    @pl.when(live)
    def _():
        pltpu.make_async_copy(source, target, sem).start()

    @pl.when(jnp.logical_not(live))
    def _():
        target[...] = jnp.zeros(target.shape, target.dtype)

    def wait():
        @pl.when(live)
        def _():
            pltpu.make_async_copy(source, target, sem).wait()

    return wait


def move_separator(leaf, column, map_ref, child_ref, slots, groups, target_of, sems):
    count = child_ref.shape[0]
    waits = []
    for slot in slots:
        row = find_tile(map_ref, leaf, column, slot, count)
        for position, group in enumerate(groups):
            place = find_tile(map_ref, leaf, group, 0, count)
            live = jnp.logical_and(row >= 0, place >= 0)
            span = pl.ds(pl.multiple_of((jnp.maximum(place, 0) * GROUPS + group) * TILE, TILE), TILE)
            source = child_ref.at[jnp.maximum(row, 0), :, span]
            target = target_of(slot, position)
            waits.append(move_tile(live, source, target, sems.at[len(waits)]))
    return waits


def pick_pivot_kernel(ids_ref, map_ref, child_ref, entries_ref, pivot_ref, sems, entry_sem):
    leaf, column = ids_ref[0], ids_ref[1]
    count = child_ref.shape[0]
    width = 2 * TILE + BLK
    entries = pltpu.make_async_copy(
        entries_ref.at[0], pivot_ref.at[:, pl.ds(width, entries_ref.shape[-1])], entry_sem.at[0]
    )
    entries.start()
    row = find_tile(map_ref, leaf, column, 0, count)
    waits = []
    for apart in range(3):
        group = (column + apart) & 3
        place = find_tile(map_ref, leaf, group, 0, count)
        live = jnp.logical_and(row >= 0, place >= 0)
        tile = jnp.maximum(place, 0) * GROUPS + group
        source_row = child_ref.at[jnp.maximum(row, 0)]
        if apart < 2:
            moves = [(source_row.at[:, tile_span(tile)], pivot_ref.at[:, pl.ds(apart * TILE, TILE)])]
        else:
            moves = []
            for b in range(2):
                top = pl.multiple_of(jnp.where(column < 2, b * BLK, BLK), BLK)
                lanes = pl.ds(pl.multiple_of(tile * TILE + jnp.where(column < 2, 0, b * BLK), BLK), BLK)
                target = pivot_ref.at[pl.ds(b * BLK, BLK), pl.ds(2 * TILE, BLK)]
                moves.append((source_row.at[pl.ds(top, BLK), lanes], target))
        for source, target in moves:
            waits.append(move_tile(live, source, target, sems.at[len(waits)]))
    for wait in waits:
        wait()
    entries.wait()


def pick_pivot(ids, child_map, child, entries):
    width = 2 * TILE + BLK + entries.shape[-1]
    return pl.pallas_call(
        pick_pivot_kernel,
        out_shape=jax.ShapeDtypeStruct((TILE, width), child.dtype),
        in_specs=[SMEM, SMEM, ANY, ANY],
        out_specs=VMEM,
        scratch_shapes=[pltpu.SemaphoreType.DMA((GROUPS,)), pltpu.SemaphoreType.DMA((1,))],
        compiler_params=pltpu.CompilerParams(vmem_limit_bytes=56 * 2**20),
        name="pick_pivot",
    )(ids, child_map, child, entries)


def pick_rest_kernel(ids_ref, map_ref, next_ref, child_ref, *refs):
    halves_out, outs, (first_sems, sems) = refs[:2], refs[2:8], refs[8:]
    count = child_ref.shape[0]
    leaf, column = ids_ref[0], ids_ref[1]
    half, pair = leaf & 1, leaf >> 1
    slots = range(1, count + 1)
    groups = (2 * (1 - half), 2 * (1 - half) + 1, 2 * half, 2 * half + 1)
    waits = move_separator(
        leaf, column, map_ref, child_ref, slots, groups,
        lambda slot, position: halves_out[position // 2].at[slot - 1, :, pl.ds(position % 2 * TILE, TILE)],
        first_sems,
    )
    rows = [find_tile(map_ref, leaf, column, slot, count) for slot in slots]
    used = 0
    for which, device in enumerate((leaf ^ 1, leaf)):
        for position, target in enumerate(column_targets(device & 1, (device >> 1) & 1)):
            group = target & 3
            update = find_tile(next_ref, pair, group, target >> 2, count)
            place = find_tile(map_ref, leaf, group, update + 1, count)
            column_live = jnp.logical_and(update >= 0, place >= 0)
            source_span = pl.ds(pl.multiple_of((jnp.maximum(place, 0) * GROUPS + group) * TILE, TILE), TILE)
            for slot, row in enumerate(rows):
                live = jnp.logical_and(column_live, row >= 0)
                source = child_ref.at[jnp.maximum(row, 0), :, source_span]
                if position % 4 == 0:
                    goal = outs[3 * which].at[slot, :, pl.ds(position // 4 * TILE, TILE)]
                else:
                    goal = outs[3 * which + 1 + position // 4].at[slot, :, pl.ds((position % 4 - 1) * TILE, TILE)]
                waits.append(move_tile(live, source, goal, sems.at[used]))
                used += 1
    for wait in waits:
        wait()


def pick_rest(ids, child_map, next_map, child):
    count = child.shape[0]
    widths = (2 * TILE, 2 * TILE) + (2 * TILE, 3 * TILE, 3 * TILE) * 2
    return pl.pallas_call(
        pick_rest_kernel,
        out_shape=tuple(jax.ShapeDtypeStruct((count, TILE, width), child.dtype) for width in widths),
        in_specs=[SMEM, SMEM, SMEM, ANY],
        out_specs=(VMEM,) * 8,
        scratch_shapes=[pltpu.SemaphoreType.DMA((GROUPS * count,)), pltpu.SemaphoreType.DMA((16 * count,))],
        compiler_params=pltpu.CompilerParams(vmem_limit_bytes=56 * 2**20),
        cost_estimate=pl.CostEstimate(flops=0, bytes_accessed=2 * 10**7, transcendentals=0),
        name="pick_rest",
    )(ids, child_map, next_map, child)


def solve_blocks(coupling_ref, lowers, inverses, panel_ref):
    split = lowers[0].shape[1]
    solved = []
    for k in range(panel_ref.shape[1] // TILE):
        span = slice(k * TILE, (k + 1) * TILE)
        rest = coupling_ref[:, span]
        if k:
            left = jnp.concatenate([part[0] for part in solved], axis=1)
            low = jnp.concatenate([part[1] for part in solved], axis=1)
            strip = lowers[0][span, 0 : min(k * TILE, split)]
            if k * TILE > split:
                inner = slice(k * TILE - split, (k + 1) * TILE - split)
                strip = jnp.concatenate([strip, lowers[1][inner, 0 : k * TILE - split]], axis=1)
            high_lower, low_lower = halves(strip)
            rest = rest - dot_lanes(
                jnp.concatenate([left, low, left], axis=1),
                jnp.concatenate([high_lower, high_lower, low_lower], axis=1),
            )
        tiles = split // TILE
        inverse = inverses[0][k] if k < tiles else inverses[1][k - tiles]
        block = dot_lanes(left_parts(rest), right_lanes(inverse))
        panel_ref[:, span] = block
        solved.append(halves(block))
    return jnp.concatenate([part[0] for part in solved], axis=1)


def write_factor(column, offset, lowers, panel, factor_ref):
    width = factor_ref.shape[-1]
    split = lowers[0].shape[1]
    per = split // width
    tiles = split // TILE
    span = pl.ds(pl.multiple_of(offset * width, width), width)
    factor_ref[0] = jnp.zeros(factor_ref.shape[1:], factor_ref.dtype)

    @pl.when(offset < per)
    def _():
        inner = pl.ds(pl.multiple_of(jnp.minimum(offset, per - 1) * width, width), width)
        factor_ref[0] = lowers[0][pl.ds(pl.multiple_of(column * TILE, TILE), TILE), inner]

    @pl.when(jnp.logical_and(offset >= per, column >= tiles))
    def _():
        inner = pl.ds(pl.multiple_of(jnp.maximum(offset - per, 0) * width, width), width)
        rows = pl.ds(pl.multiple_of(jnp.maximum(column - tiles, 0) * TILE, TILE), TILE)
        factor_ref[0] = lowers[1][rows, inner]

    for s in range(factor_ref.shape[0] - 1):
        factor_ref[s + 1] = panel[s * TILE : (s + 1) * TILE, span]


def panel_one_kernel(ids_ref, next_ref, mine_ref, peer_ref, *refs):
    lowers, inverses = refs[:2], refs[2:4]
    factor_ref, round_ref, first_ref, second_ref, third_ref, coupling, panel, round_in, sems = refs[4:]
    leaf, column = ids_ref[0], ids_ref[1]
    half, pair = leaf & 1, leaf >> 1
    count, _, width = mine_ref.shape
    for ref, place in ((mine_ref, half), (peer_ref, 1 - half)):
        span = pl.ds(pl.multiple_of(place * width, width), width)
        for s in range(count):
            coupling[s * TILE : (s + 1) * TILE, span] = ref[s].astype(jnp.float32)
    rounded = solve_blocks(coupling, lowers, inverses, panel)
    for s in range(count):
        round_in[s] = rounded[s * TILE : (s + 1) * TILE]
    copy = pltpu.make_async_copy(round_in, round_ref, sems.at[0])
    copy.start()
    write_factor(column, half, lowers, panel, factor_ref)
    heavy = half == (column & 1)
    for a, share_ref in ((0, first_ref), (jnp.where(heavy, 1, 0), second_ref), (2, third_ref)):
        slot = jnp.int32(0)
        for target in column_targets(half, 0):
            hit = jnp.logical_and((target & 3) == column, share_place(target, half) == a)
            slot = jnp.where(hit, target >> 2, slot)
        tile = find_tile(next_ref, pair, column, slot, count)
        share_ref[...] = round_in[jnp.maximum(tile, 0)]
    copy.wait()


def panel_one(ids, next_map, mine, peer, lowers, inverses):
    count = mine.shape[0]
    order = lowers[0].shape[0]
    return pl.pallas_call(
        panel_one_kernel,
        out_shape=(
            jax.ShapeDtypeStruct((count + 1, TILE, order // 2), jnp.float32),
            jax.ShapeDtypeStruct((count, TILE, order), jnp.bfloat16),
        )
        + (jax.ShapeDtypeStruct((TILE, order), jnp.bfloat16),) * 3,
        in_specs=[SMEM, SMEM] + [VMEM] * 6,
        out_specs=(VMEM, HBM, VMEM, VMEM, VMEM),
        scratch_shapes=[
            pltpu.VMEM((count * TILE, order), jnp.float32),
            pltpu.VMEM((count * TILE, order), jnp.float32),
            pltpu.VMEM((count, TILE, order), jnp.bfloat16),
            pltpu.SemaphoreType.DMA((1,)),
        ],
        compiler_params=PARAMS,
        cost_estimate=pl.CostEstimate(flops=10**9, bytes_accessed=10**6, transcendentals=0),
        name="panel_one",
    )(ids, next_map, mine, peer, *lowers, *inverses)


def panel_two_kernel(ids_ref, own_ref, x_ref, z_ref, both_ref, *refs):
    lowers, inverses = refs[:2], refs[2:4]
    factor_ref, round_ref, share_ref, coupling, panel, round_in, sems = refs[4:]
    leaf, column = ids_ref[0], ids_ref[1]
    half, side = leaf & 1, (leaf >> 1) & 1
    quarter = leaf & 3
    count = round_ref.shape[0]
    for place, ref in (
        (2 * side + half, own_ref),
        (2 * side + 1 - half, x_ref),
        (2 * (1 - side) + half, z_ref),
        (2 * (1 - side) + 1 - half, both_ref),
    ):
        coupling[:, pl.ds(pl.multiple_of(place * TILE, TILE), TILE)] = ref[...].astype(jnp.float32)
    rounded = solve_blocks(coupling, lowers, inverses, panel)
    for s in range(count):
        round_in[s] = rounded[s * TILE : (s + 1) * TILE]
    copy = pltpu.make_async_copy(round_in, round_ref, sems.at[0])
    copy.start()
    write_factor(column, quarter, lowers, panel, factor_ref)
    chosen = jnp.int32(0)
    for i in range(3):
        tile = 3 * quarter + i
        chosen = jnp.where((tile & 3) == column, tile >> 2, chosen)
    share_ref[...] = round_in[chosen]
    copy.wait()


def panel_two(ids, parts, lowers, inverses):
    rows = parts[0].shape[0]
    count = rows // TILE
    order = lowers[0].shape[0]
    return pl.pallas_call(
        panel_two_kernel,
        out_shape=(
            jax.ShapeDtypeStruct((count + 1, TILE, order // 4), jnp.float32),
            jax.ShapeDtypeStruct((count, TILE, order), jnp.bfloat16),
            jax.ShapeDtypeStruct((TILE, order), jnp.bfloat16),
        ),
        in_specs=[SMEM] + [VMEM] * 8,
        out_specs=(VMEM, HBM, VMEM),
        scratch_shapes=[
            pltpu.VMEM((rows, order), jnp.float32),
            pltpu.VMEM((rows, order), jnp.float32),
            pltpu.VMEM((count, TILE, order), jnp.bfloat16),
            pltpu.SemaphoreType.DMA((1,)),
        ],
        compiler_params=PARAMS,
        cost_estimate=pl.CostEstimate(flops=10**9, bytes_accessed=10**6, transcendentals=0),
        name="panel_two",
    )(ids, *parts, *lowers, *inverses)


def take_tile(owner, column, refs, live, target, sem):
    for apart, ref in enumerate(refs):

        @pl.when(jnp.logical_and(live, (owner ^ column) == apart))
        def _():
            pltpu.make_async_copy(ref, target, sem).start()


def start_shared(ids_ref, positions, firsts, thirds, taken, sems):
    leaf, column = ids_ref[0], ids_ref[1]
    half, side = leaf & 1, (leaf >> 1) & 1
    targets = column_targets(half, side)
    copies = []
    for i, position in enumerate(positions):
        target = targets[position]
        group = target & 3
        place = share_place(target, half)
        take_tile(group, column, firsts, place < 2, taken.at[i], sems.at[i])
        if thirds:
            take_tile(group, column, thirds, place == 2, taken.at[i], sems.at[i])
        copies.append(pltpu.make_async_copy(firsts[0], taken.at[i], sems.at[i]))
    return copies


class Loads:
    def __init__(self, sources, targets, sems):
        self.copies = [pltpu.make_async_copy(*each, sems.at[k]) for k, each in enumerate(zip(sources, targets))]

    def start(self, chosen):
        for k in chosen:
            self.copies[k].start()

    def wait(self, chosen):
        for k in chosen:
            self.copies[k].wait()


def update_columns(ids_ref, next_ref, positions, shared, refs, write):
    leaf, column = ids_ref[0], ids_ref[1]
    half, side, pair = leaf & 1, (leaf >> 1) & 1, leaf >> 1
    sources, (keep_in, peer_in, round_in, taken, tiles, sems, load_sems) = refs
    count = keep_in.shape[0]
    loads = Loads(sources, (keep_in, peer_in, round_in), load_sems)
    loads.start((2,))
    copies = start_shared(ids_ref, positions, *shared, taken, sems)
    loads.start((0, 1))
    targets = column_targets(half, side)
    rows = [find_tile(next_ref, pair, column, slot, count) for slot in range(count + 1)]
    tiles[:, count] = jnp.zeros_like(tiles[:, count])
    loads.wait((2,))
    for i, position in enumerate(positions):
        target = targets[position]
        live = find_tile(next_ref, pair, target & 3, target >> 2, count) >= 0
        span = slice(i * TILE, (i + 1) * TILE)
        copies[i].wait()
        for s in range(count):
            product = dot_lanes(round_in[s], taken[i])
            if i == 0 and s == 0:
                loads.wait((0, 1))
            value = keep_in[s, :, span].astype(jnp.float32) + peer_in[s, :, span].astype(jnp.float32) - product
            tiles[i, s] = jnp.where(live, value, 0.0).astype(jnp.bfloat16)
        for slot, row in enumerate(rows):
            write(i, slot, lambda row=row: tiles[i, jnp.where(row < 0, count, row)])


def update_scratch(count, width, order):
    return [
        pltpu.VMEM((count, TILE, width * TILE), jnp.bfloat16),
        pltpu.VMEM((count, TILE, width * TILE), jnp.bfloat16),
        pltpu.VMEM((count, TILE, order), jnp.bfloat16),
        pltpu.VMEM((width, TILE, order), jnp.bfloat16),
        pltpu.VMEM((width, count + 1, TILE, TILE), jnp.bfloat16),
        pltpu.SemaphoreType.DMA((width,)),
        pltpu.SemaphoreType.DMA((3,)),
    ]


def update_separator_kernel(ids_ref, next_ref, *refs):
    sources, firsts, (pivot_ref, near_ref, far_ref), scratch = refs[:3], refs[3:7], refs[7:10], refs[10:]

    def write(i, slot, tile):
        if slot == 0:
            pivot_ref[:, i * TILE : (i + 1) * TILE] = tile()
        else:
            (near_ref, far_ref)[i][slot - 1] = tile()

    update_columns(ids_ref, next_ref, (0, 4), (firsts, ()), (sources, scratch), write)


def update_separator(ids, next_map, keep, peer, rounded, firsts):
    count, _, order = rounded.shape
    tile = jax.ShapeDtypeStruct((count, TILE, TILE), jnp.bfloat16)
    return pl.pallas_call(
        update_separator_kernel,
        out_shape=(jax.ShapeDtypeStruct((TILE, 2 * TILE), jnp.bfloat16), tile, tile),
        in_specs=[SMEM, SMEM] + [ANY] * 7,
        out_specs=(VMEM, VMEM, VMEM),
        scratch_shapes=update_scratch(count, 2, order),
        compiler_params=pltpu.CompilerParams(vmem_limit_bytes=56 * 2**20),
        cost_estimate=pl.CostEstimate(flops=10**8, bytes_accessed=10**5, transcendentals=0),
        name="update_separator",
    )(ids, next_map, keep, peer, rounded, *firsts)


def update_trailing_kernel(positions, ids_ref, next_ref, *refs):
    sources, seconds, thirds, out_ref, scratch = refs[:3], refs[3:7], refs[7:11], refs[11], refs[12:]

    def write(i, slot, tile):
        if slot:
            out_ref[slot - 1, :, i * TILE : (i + 1) * TILE] = tile()

    update_columns(ids_ref, next_ref, positions, (seconds, thirds), (sources, scratch), write)


def update_trailing(ids, next_map, keep, peer, rounded, seconds, thirds, positions):
    count, _, order = rounded.shape
    width = len(positions)
    return pl.pallas_call(
        functools.partial(update_trailing_kernel, positions),
        out_shape=jax.ShapeDtypeStruct((count, TILE, width * TILE), jnp.bfloat16),
        in_specs=[SMEM, SMEM] + [ANY] * 11,
        out_specs=VMEM,
        scratch_shapes=update_scratch(count, width, order),
        compiler_params=pltpu.CompilerParams(vmem_limit_bytes=56 * 2**20),
        cost_estimate=pl.CostEstimate(flops=10**8, bytes_accessed=10**5, transcendentals=0),
        name="update_trailing",
    )(ids, next_map, keep, peer, rounded, *seconds, *thirds)


def update_two_kernel(ids_ref, *refs):
    sources, firsts, out_ref = refs[:3], refs[3:7], refs[7]
    near_in, far_in, round_in, taken, sems, load_sems = refs[8:]
    quarter, column = ids_ref[0] & 3, ids_ref[1]
    loads = Loads(sources, (near_in, far_in, round_in), load_sems)
    loads.start((2,))
    for i in range(3):
        take_tile((3 * quarter + i) & 3, column, firsts, True, taken.at[i], sems.at[i])
    loads.start((0, 1))
    loads.wait((2,))
    for i in range(3):
        span = slice(i * TILE, (i + 1) * TILE)
        pltpu.make_async_copy(firsts[0], taken.at[i], sems.at[i]).wait()
        for s in range(near_in.shape[0]):
            product = dot_lanes(round_in[s], taken[i])
            if i == 0 and s == 0:
                loads.wait((0, 1))
            total = near_in[s, :, span].astype(jnp.float32) + far_in[s, :, span].astype(jnp.float32)
            out_ref[s, :, span] = (total - product).astype(jnp.bfloat16)


def update_two(ids, near, far, rounded, firsts):
    order = rounded.shape[-1]
    return pl.pallas_call(
        update_two_kernel,
        out_shape=jax.ShapeDtypeStruct(near.shape, jnp.bfloat16),
        in_specs=[SMEM] + [ANY] * 7,
        out_specs=VMEM,
        scratch_shapes=[
            pltpu.VMEM(near.shape, jnp.bfloat16),
            pltpu.VMEM(far.shape, jnp.bfloat16),
            pltpu.VMEM(rounded.shape, jnp.bfloat16),
            pltpu.VMEM((3, TILE, order), jnp.bfloat16),
            pltpu.SemaphoreType.DMA((3,)),
            pltpu.SemaphoreType.DMA((3,)),
        ],
        compiler_params=pltpu.CompilerParams(vmem_limit_bytes=56 * 2**20),
        cost_estimate=pl.CostEstimate(flops=2 * 10**9, bytes_accessed=10**7, transcendentals=0),
        name="update_two",
    )(ids, near, far, rounded, *firsts)


def first_hop(pack):
    return swapped(pack, "leaf", 1), swapped(pack, "front", 2), swapped(pack, "front", 1)


def over_square(pack, hop, beside):
    half = pack.shape[0] // 2
    x, y, core = hop
    x, y = lax.optimization_barrier((x, y, beside))[:2]
    top = swapped(y[:half], "leaf", 1)
    low = swapped(x[half:], "front", 2)
    x_core, y_core = swapped(x, "front", 1), swapped(y, "front", 1)
    top_core, low_core = swapped(top, "front", 1), swapped(low, "front", 1)
    return (pack, core, y, y_core, x, x_core, top, low, top_core, low_core)


def over_front(tile, y, *earlier):
    return (tile, swapped(tile, "front", 1), y, swapped(after(y, *earlier), "front", 1))


def over_heavy(tile, y, *earlier):
    return (tile, swapped_heavy(tile, 1), y, swapped_heavy(after(y, *earlier), 1))


def after(value, *earlier):
    return lax.optimization_barrier((value, *earlier))[0]


def own_mask(mask, front, column, count):
    rows = lax.dynamic_index_in_dim(mask, front, 0, keepdims=False).reshape(count, GROUPS, -1)
    return lax.dynamic_index_in_dim(rows, column, 1, keepdims=False).astype(jnp.float32)


def body(child_update, sep_one, sep_two, map_one, map_two, mask_one, mask_two):
    column = lax.axis_index("front")
    leaf = lax.axis_index("leaf")
    quad, quarter = leaf >> 2, leaf & 3
    ids = jnp.stack([leaf, column]).astype(jnp.int32)
    child = child_update[0, 0, 0]
    entries_one = sep_one[0, 0, 0]
    entries_two = sep_two[0, 0, 0]
    count = child.shape[0]
    order = GROUPS * TILE
    maps_one = map_one[:, 0]
    maps_two = map_two[:, 0]

    pivot_mine = pick_pivot(ids, maps_one, child, entries_one)
    mask_first = own_mask(mask_one, leaf >> 1, column, count)
    mask_first = lax.dynamic_slice_in_dim(mask_first, 2 * (leaf & 1), 2, 1)
    mask_first = jnp.repeat(mask_first, TILE, axis=1)[:, None, :]
    mask_second = lax.dynamic_index_in_dim(own_mask(mask_two, quad, column, count), quarter, 1, keepdims=False)
    ids_early, mask_first, mask_second = lax.optimization_barrier((ids, mask_first, mask_second))
    coupling_send, coupling_keep, sep_send, near_send, far_send, sep_keep, near_keep, far_keep = pick_rest(
        ids_early, maps_one, maps_two, child
    )
    packs = over_square(pivot_mine, first_hop(pivot_mine), coupling_send)
    coupling_got = swapped(after(coupling_send, packs[4]), "leaf", 1)
    entries_far = swapped(entries_two[0], "leaf", 2)
    lower, inverse, rest = cholesky_first(ids, packs, fill_one, order, 2 * 10**10)
    coupling = (
        coupling_keep.astype(jnp.float32)
        + after(coupling_got, rest).astype(jnp.float32)
        + entries_one[1:].astype(jnp.float32) * mask_first
    )
    coupling_peer = swapped(coupling.astype(jnp.bfloat16), "leaf", 1)
    lower_rest, inverse_rest = cholesky_second(rest, 2 * 10**10)
    sep_peer = swapped(after(sep_send, lower_rest), "leaf", 1)
    far_peer = swapped(after(far_send, lower_rest), "leaf", 1)
    factor_one, rounded, first, second, third = panel_one(
        ids, maps_two, coupling, coupling_peer, (lower, lower_rest), (inverse, inverse_rest)
    )
    first_y = swapped_heavy(first, 2)
    firsts = over_heavy(first, first_y, sep_peer)
    pivot_own, near_coupling, far_coupling = update_separator(ids, maps_two, sep_keep, sep_peer, rounded, firsts)
    second_y = swapped(after(second, first_y), "front", 2)
    third_y = swapped_heavy(after(third, first_y), 2)

    pivot_far = swapped(pivot_own, "leaf", 2)
    pivot_pack = pack_two(ids, pivot_own, pivot_far, entries_two[0], entries_far)
    hop = first_hop(after(pivot_pack, far_peer))
    seconds = over_front(second, second_y, pivot_pack)
    thirds = over_heavy(third, third_y, pivot_pack)
    far_trailing = update_trailing(
        ids, maps_two, far_keep, far_peer, after(rounded, pivot_far), seconds, thirds, (5, 6, 7)
    )
    packs = over_square(pivot_pack, hop, far_trailing)
    coupling_far = swapped(after(far_coupling, pivot_far), "leaf", 2)
    coupling = (
        near_coupling.astype(jnp.float32)
        + coupling_far.astype(jnp.float32)
        + entries_two[1:].astype(jnp.float32) * mask_second[:, None, None]
    ).reshape(count * TILE, TILE)
    coupling_sent = after(coupling.astype(jnp.bfloat16), packs[4])
    coupling_x, coupling_z, coupling_xz = (swapped(coupling_sent, "leaf", mask) for mask in (1, 2, 3))
    lower, inverse, rest = cholesky_first(ids, packs, fill_two, order, 2 * 10**10)
    trailing_far = swapped(after(far_trailing, rest), "leaf", 2)
    near_peer = swapped(after(near_send, rest), "leaf", 1)
    lower_rest, inverse_rest = cholesky_second(rest, 2 * 10**10)
    factor_two, rounded_two, share = panel_two(
        ids, (coupling, coupling_x, coupling_z, coupling_xz), (lower, lower_rest), (inverse, inverse_rest)
    )
    near_trailing = update_trailing(ids, maps_two, near_keep, near_peer, rounded, seconds, thirds, (1, 2, 3))
    shares = over_front(share, swapped(share, "front", 2), near_trailing, trailing_far)
    update = update_two(ids, near_trailing, trailing_far, rounded_two, shares)
    return (factor_one[None, None, None], factor_two[None, None, None], update[None, None, None])


def solution(mesh):
    split = P("leaf", "front", None, None, None, None)
    return jax.shard_map(
        body,
        mesh=mesh,
        in_specs=(split, split, split, P(), P(), P(), P()),
        out_specs=(split, split, split),
        check_vma=False,
    )
```

```python
import functools

import jax
import jax.numpy as jnp
from jax import lax
from jax.experimental import pallas as pl
from jax.experimental.pallas import tpu as pltpu
from jax.sharding import PartitionSpec as P

VMEM = pl.BlockSpec(memory_space=pltpu.VMEM)
SMEM = pl.BlockSpec(memory_space=pltpu.SMEM)
ANY = pl.BlockSpec(memory_space=pl.ANY)
HBM = pl.BlockSpec(memory_space=pltpu.HBM)
GROUPS = 4
PARAMS = pltpu.CompilerParams(vmem_limit_bytes=32 * 2**20)
BLK = 128
GRP = 8
TILE = 256
NT = (((1,), (1,)), ((), ()))


def halves(x):
    high = x.astype(jnp.bfloat16)
    low = (x - high.astype(jnp.float32)).astype(jnp.bfloat16)
    return high, low


def left_parts(x):
    high, low = halves(x)
    return jnp.concatenate([high, low, high], axis=1)


def right_rows(x):
    high, low = halves(x)
    return jnp.concatenate([high, high, low], axis=0)


def right_lanes(x):
    high, low = halves(x)
    return jnp.concatenate([high, high, low], axis=1)


def dot_rows(left, right):
    return jnp.dot(left, right, preferred_element_type=jnp.float32)


def dot_lanes(left, right):
    return lax.dot_general(left, right, NT, preferred_element_type=jnp.float32)


def spread_row(ref, index):
    return jnp.broadcast_to(ref[index], (GRP, BLK))


def tree_sum(parts):
    while len(parts) > 1:
        parts = [parts[k] + parts[k + 1] for k in range(0, len(parts), 2)]
    return parts[0]


def factor_diagonal(block, done_ref, pivot_ref, rows_ref):
    steps = BLK // GRP
    row_id = lax.broadcasted_iota(jnp.int32, (GRP, BLK), 0)
    lane_id = lax.broadcasted_iota(jnp.int32, (GRP, BLK), 1)
    matrix = [block[GRP * g : GRP * (g + 1), :] for g in range(steps)]
    inverse = [jnp.where(lane_id == row_id + GRP * g, 1.0, 0.0).astype(jnp.float32) for g in range(steps)]
    for g in range(steps):
        first = GRP * g
        slot = g % 2
        current = matrix[g]
        rows_ref[slot, :, 0:BLK] = current
        rows_ref[slot, :, BLK:] = inverse[g]
        for i in range(GRP):
            pivot_ref[slot, i] = jnp.broadcast_to(current[:, first + i : first + i + 1], (GRP, BLK))
        entry = {}
        for m in range(GRP):
            for i in range(m + 1):
                entry[m, i] = jnp.broadcast_to(pivot_ref[slot, i, m : m + 1, :], (GRP, BLK))
                entry[i, m] = entry[m, i]
        left = [jnp.broadcast_to(rows_ref[slot, m : m + 1, 0:BLK], (GRP, BLK)) for m in range(GRP)]
        right = [jnp.broadcast_to(rows_ref[slot, m : m + 1, BLK:], (GRP, BLK)) for m in range(GRP)]
        for i in range(0, GRP, 2):
            n = i + 1
            a, b, c = entry[i, i], entry[n, i], entry[n, n]
            root = lax.rsqrt(a)
            root_both = lax.rsqrt(a * c - b * b)
            scale = root_both * root_both
            second_root = root * root_both

            def solve(x, y):
                return c * x - b * y, a * y - b * x

            solved = {}
            for name, rows_now in (("left", left), ("right", right)):
                raw = solve(rows_now[i], rows_now[n])
                lanes = slice(0, BLK) if name == "left" else slice(BLK, 2 * BLK)
                done_ref[first + i : first + i + 1, lanes] = (rows_now[i] * root)[0:1]
                done_ref[first + n : first + n + 1, lanes] = (raw[1] * second_root)[0:1]
                rows_now[i], rows_now[n] = raw[0] * scale, raw[1] * scale
            for col in range(i + 2, GRP):
                raw = solve(entry[i, col], entry[n, col])
                solved[col] = (raw[0] * scale, raw[1] * scale)
            for m in range(GRP):
                if m in (i, n):
                    continue
                weight, other = entry[m, i], entry[m, n]
                for rows_now in (left, right):
                    rows_now[m] = rows_now[m] - (weight * rows_now[i] + other * rows_now[n])
                for col in range(i + 2, GRP):
                    if m > col:
                        continue
                    entry[m, col] = entry[m, col] - (weight * solved[col][0] + other * solved[col][1])
            for m in range(i + 2, GRP):
                for col in range(i + 2, m):
                    entry[m, col] = entry[col, m]
            for col in range(i + 2, GRP):
                entry[i, col], entry[n, col] = solved[col]
        for later in range(g + 1, steps):
            rows = matrix[later]
            parts_left, parts_right = [], []
            for i in range(GRP):
                weight = jnp.broadcast_to(rows[:, first + i : first + i + 1], (GRP, BLK))
                parts_left.append(weight * left[i])
                parts_right.append(weight * right[i])
            matrix[later] = rows - tree_sum(parts_left)
            inverse[later] = inverse[later] - tree_sum(parts_right)


def tile_span(index):
    return pl.ds(pl.multiple_of(index * TILE, TILE), TILE)


def block_span(index, block):
    return pl.ds(pl.multiple_of(index * TILE + block * BLK, BLK), BLK)


def put_next(work, j, tile):
    last = work.shape[0] // TILE - 1

    @pl.when(j < last)
    def _():
        work[tile_span(j), tile_span(jnp.minimum(j + 1, last))] = tile()

    @pl.when(j == last)
    def _():
        work[0:TILE, last * TILE :] = tile().T


def put_half(work, j, block):
    for b in range(2):

        @pl.when(j < 2)
        def _():
            work[block_span(j, b), block_span(jnp.minimum(j, 1) + 2, 0)] = block(b)

        @pl.when(j >= 2)
        def _():
            work[block_span(jnp.maximum(j, 2) - 2, b), block_span(j, 1)] = block(b).T


def each_pack(packs):
    own, core, y, y_core, x, x_core, top, low, top_core, low_core = packs
    return (0, own, (x,)), (1, core, (x_core,)), (2, y, (top, low)), (3, y_core, (top_core, low_core))


def rows_of(refs, b, lanes):
    if len(refs) == 2:
        return refs[b][:, lanes].astype(jnp.float32)
    return refs[0][b * BLK : (b + 1) * BLK, lanes].astype(jnp.float32)


def fill_one(ids_ref, packs, work, mixed):
    leaf, column = ids_ref[0], ids_ref[1]
    half = leaf & 1
    width = mixed.shape[1]
    for apart, mine, peers in each_pack(packs):
        j = column ^ apart
        for b in range(2):
            rows = slice(b * BLK, (b + 1) * BLK)
            mixed[rows, :] = rows_of((mine,), b, slice(0, width)) + rows_of(peers, b, slice(0, width))
        for refs, side in (((mine,), half), (peers, 1 - half)):
            for q in range(2):
                apart_columns = (2 * side + q - j) & 3
                start = width + q * TILE
                for whole in range(2):

                    @pl.when(apart_columns == whole)
                    def _():
                        for b in range(2):
                            rows = slice(b * BLK, (b + 1) * BLK)
                            lanes = slice(whole * TILE, (whole + 1) * TILE)
                            mixed[rows, lanes] = mixed[rows, lanes] + rows_of(refs, b, slice(start, start + TILE))

                for b in range(2):
                    rows = slice(b * BLK, (b + 1) * BLK)

                    @pl.when(jnp.logical_and(apart_columns == 2, j < 2))
                    def _():
                        mixed[rows, 2 * TILE :] = mixed[rows, 2 * TILE :] + rows_of(refs, b, slice(start, start + BLK))

                    @pl.when(jnp.logical_and(apart_columns == 2, j >= 2))
                    def _():
                        lanes = slice(start + b * BLK, start + (b + 1) * BLK)
                        mixed[rows, 2 * TILE :] = mixed[rows, 2 * TILE :] + rows_of(refs, 1, lanes)

        work[tile_span(j), tile_span(j)] = mixed[:, 0:TILE]
        put_next(work, j, lambda: mixed[:, TILE : 2 * TILE])
        put_half(work, j, lambda b: mixed[b * BLK : (b + 1) * BLK, 2 * TILE :])


def fill_two(ids_ref, packs, work, mixed):
    leaf, column = ids_ref[0], ids_ref[1]
    half = leaf & 1
    for apart, mine, peers in each_pack(packs):
        j = column ^ apart
        for refs, side in (((mine,), half), (peers, 1 - half)):
            for b in range(2):
                mixed[b * BLK : (b + 1) * BLK, 0 : TILE + BLK] = rows_of(refs, b, slice(0, TILE + BLK))

            @pl.when(side == (j & 1))
            def _():
                work[tile_span(j), tile_span(j)] = mixed[:, 0:TILE]
                put_half(work, j, lambda b: mixed[b * BLK : (b + 1) * BLK, TILE : TILE + BLK])

            @pl.when(side != (j & 1))
            def _():
                put_next(work, j, lambda: mixed[:, 0:TILE])


def pack_two_kernel(ids_ref, own_ref, far_ref, near_entries_ref, far_entries_ref, pack_ref, both):
    leaf, column = ids_ref[0], ids_ref[1]
    half, side = leaf & 1, (leaf >> 1) & 1
    for place, other, entries_ref in ((0, 1, near_entries_ref), (1, 0, far_entries_ref)):
        both[place] = (
            own_ref[:, place * TILE : (place + 1) * TILE].astype(jnp.float32)
            + far_ref[:, other * TILE : (other + 1) * TILE].astype(jnp.float32)
            + entries_ref[...].astype(jnp.float32)
        )
    whole = jnp.where(half == (column & 1), column, (column + 1) & 3)
    place = jnp.where((whole >> 1) == side, 0, 1)
    pack_ref[:, 0:TILE] = both[place]
    for b in range(2):
        rows = slice(b * BLK, (b + 1) * BLK)

        @pl.when(column < 2)
        def _():
            pack_ref[rows, TILE:] = both[1 - place, rows, 0:BLK]

        @pl.when(column >= 2)
        def _():
            pack_ref[rows, TILE:] = both[1 - place, BLK:, rows]


def pack_two(ids, own, far, near_entries, far_entries):
    return pl.pallas_call(
        pack_two_kernel,
        out_shape=jax.ShapeDtypeStruct((TILE, TILE + BLK), jnp.float32),
        in_specs=[SMEM] + [VMEM] * 4,
        out_specs=VMEM,
        scratch_shapes=[pltpu.VMEM((2, TILE, TILE), jnp.float32)],
        compiler_params=pltpu.CompilerParams(vmem_limit_bytes=56 * 2**20),
        name="pack_two",
    )(ids, own, far, near_entries, far_entries)


def eliminate(work, lower_ref, inverse_ref, done, block_inverse, entries, rows):
    order = work.shape[0]
    blocks = lower_ref.shape[1] // BLK
    lower_ref[...] = jnp.zeros_like(lower_ref)
    row_id = lax.broadcasted_iota(jnp.int32, (BLK, BLK), 0)
    lane_id = lax.broadcasted_iota(jnp.int32, (BLK, BLK), 1)

    def step(k, carry):
        start = pl.multiple_of(k * BLK, BLK)
        span = pl.ds(start, BLK)
        factor_diagonal(work[span, span], done, entries, rows)
        upper = jnp.where(lane_id >= row_id, done[:, 0:BLK], 0.0)
        lower_ref[span, span] = upper.T
        block_inverse[k] = done[:, BLK:]
        for fixed in range(blocks):
            after = (fixed + 1) * BLK
            if after == order:
                continue

            @pl.when(k == fixed)
            def _():
                strip = dot_rows(
                    left_parts(done[:, BLK:]), right_rows(work[after - BLK : after, after:])
                )
                column = strip.T
                lower_ref[after:, after - BLK : after] = column
                left = left_parts(column)
                right = right_rows(strip)
                width = order - after
                for top in range(0, width, TILE):
                    high = min(TILE, width - top)
                    work[after + top : after + top + high, after + top :] = work[
                        after + top : after + top + high, after + top :
                    ] - dot_rows(left[top : top + high], right[:, top:])

        return carry

    lax.fori_loop(0, blocks, step, 0)
    for tile in range(blocks * BLK // TILE):
        base = tile * TILE
        first, second = block_inverse[2 * tile], block_inverse[2 * tile + 1]
        corner = lower_ref[base + BLK : base + TILE, base : base + BLK]
        mixed = dot_rows(left_parts(corner), right_rows(first))
        mixed = -dot_rows(left_parts(second), right_rows(mixed))
        inverse_ref[tile, 0:BLK, 0:BLK] = first
        inverse_ref[tile, 0:BLK, BLK:] = jnp.zeros((BLK, BLK), jnp.float32)
        inverse_ref[tile, BLK:, 0:BLK] = mixed
        inverse_ref[tile, BLK:, BLK:] = second


def cholesky_first_kernel(fill, ids_ref, *refs):
    packs = refs[:10]
    lower_ref, inverse_ref, rest_ref, mixed, work, *scratch = refs[10:]
    fill(ids_ref, packs, work, mixed)
    eliminate(work, lower_ref, inverse_ref, *scratch)
    done = lower_ref.shape[1]
    rest_ref[...] = work[done:, done:]


def cholesky_second_kernel(rest_ref, lower_ref, inverse_ref, work, *scratch):
    work[...] = rest_ref[...]
    eliminate(work, lower_ref, inverse_ref, *scratch)


def elimination_scratch(order, blocks):
    return [
        pltpu.VMEM((order, order), jnp.float32),
        pltpu.VMEM((BLK, 2 * BLK), jnp.float32),
        pltpu.VMEM((blocks, BLK, BLK), jnp.float32),
        pltpu.VMEM((2, GRP, GRP, BLK), jnp.float32),
        pltpu.VMEM((2, GRP, 2 * BLK), jnp.float32),
    ]


def cholesky_first(ids, packs, fill, order, flops):
    done = order // 2
    return pl.pallas_call(
        functools.partial(cholesky_first_kernel, fill),
        out_shape=(
            jax.ShapeDtypeStruct((order, done), jnp.float32),
            jax.ShapeDtypeStruct((done // TILE, TILE, TILE), jnp.float32),
            jax.ShapeDtypeStruct((order - done, order - done), jnp.float32),
        ),
        in_specs=[SMEM] + [VMEM] * len(packs),
        out_specs=(VMEM,) * 3,
        scratch_shapes=[pltpu.VMEM((TILE, 2 * TILE + BLK), jnp.float32)] + elimination_scratch(order, done // BLK),
        compiler_params=pltpu.CompilerParams(vmem_limit_bytes=32 * 2**20),
        cost_estimate=pl.CostEstimate(flops=flops, bytes_accessed=10**5, transcendentals=0),
        name="cholesky_first",
    )(ids, *packs)


def cholesky_second(rest, flops):
    order = rest.shape[0]
    return pl.pallas_call(
        cholesky_second_kernel,
        out_shape=(
            jax.ShapeDtypeStruct((order, order), jnp.float32),
            jax.ShapeDtypeStruct((order // TILE, TILE, TILE), jnp.float32),
        ),
        in_specs=[VMEM],
        out_specs=(VMEM,) * 2,
        scratch_shapes=elimination_scratch(order, order // BLK),
        compiler_params=pltpu.CompilerParams(vmem_limit_bytes=24 * 2**20),
        cost_estimate=pl.CostEstimate(flops=flops, bytes_accessed=10**5, transcendentals=0),
        name="cholesky_second",
    )(rest)


def swapped(value, axis, mask):
    pairs = [(source, source ^ mask) for source in range(lax.axis_size(axis))]
    return lax.ppermute(value, axis, pairs)


def swapped_heavy(value, mask):
    groups = lax.axis_size("front")
    pairs = [
        (leaf * groups + column, leaf * groups + (column ^ mask))
        for leaf in range(lax.axis_size("leaf"))
        for column in range(groups)
        if (leaf & 1) == (column & 1)
    ]
    return lax.ppermute(value, ("leaf", "front"), pairs)


def find_tile(map_ref, owner, group, slot, count):
    found = jnp.int32(-1)
    for s in range(count):
        found = jnp.where(map_ref[owner, group, s] == slot, jnp.int32(s), found)
    return found


def column_targets(half, side):
    targets = []
    for part in (side, 1 - side):
        targets.append(2 * part + half)
        targets += [4 + 3 * (2 * part + half) + i for i in range(3)]
    return targets


def share_place(target, half):
    place = jnp.int32(0)
    for other in column_targets(half, 0):
        earlier = jnp.logical_and((other & 3) == (target & 3), other < target)
        place = place + earlier.astype(jnp.int32)
    return place


def move_tile(live, source, target, sem):
    @pl.when(live)
    def _():
        pltpu.make_async_copy(source, target, sem).start()

    @pl.when(jnp.logical_not(live))
    def _():
        target[...] = jnp.zeros(target.shape, target.dtype)

    def wait():
        @pl.when(live)
        def _():
            pltpu.make_async_copy(source, target, sem).wait()

    return wait


def move_separator(leaf, column, map_ref, child_ref, slots, groups, target_of, sems):
    count = child_ref.shape[0]
    waits = []
    for slot in slots:
        row = find_tile(map_ref, leaf, column, slot, count)
        for position, group in enumerate(groups):
            place = find_tile(map_ref, leaf, group, 0, count)
            live = jnp.logical_and(row >= 0, place >= 0)
            span = pl.ds(pl.multiple_of((jnp.maximum(place, 0) * GROUPS + group) * TILE, TILE), TILE)
            source = child_ref.at[jnp.maximum(row, 0), :, span]
            target = target_of(slot, position)
            waits.append(move_tile(live, source, target, sems.at[len(waits)]))
    return waits


def pick_pivot_kernel(ids_ref, map_ref, child_ref, entries_ref, pivot_ref, sems, entry_sem):
    leaf, column = ids_ref[0], ids_ref[1]
    count = child_ref.shape[0]
    width = 2 * TILE + BLK
    entries = pltpu.make_async_copy(
        entries_ref.at[0], pivot_ref.at[:, pl.ds(width, entries_ref.shape[-1])], entry_sem.at[0]
    )
    entries.start()
    row = find_tile(map_ref, leaf, column, 0, count)
    waits = []
    for apart in range(3):
        group = (column + apart) & 3
        place = find_tile(map_ref, leaf, group, 0, count)
        live = jnp.logical_and(row >= 0, place >= 0)
        tile = jnp.maximum(place, 0) * GROUPS + group
        source_row = child_ref.at[jnp.maximum(row, 0)]
        if apart < 2:
            moves = [(source_row.at[:, tile_span(tile)], pivot_ref.at[:, pl.ds(apart * TILE, TILE)])]
        else:
            moves = []
            for b in range(2):
                top = pl.multiple_of(jnp.where(column < 2, b * BLK, BLK), BLK)
                lanes = pl.ds(pl.multiple_of(tile * TILE + jnp.where(column < 2, 0, b * BLK), BLK), BLK)
                target = pivot_ref.at[pl.ds(b * BLK, BLK), pl.ds(2 * TILE, BLK)]
                moves.append((source_row.at[pl.ds(top, BLK), lanes], target))
        for source, target in moves:
            waits.append(move_tile(live, source, target, sems.at[len(waits)]))
    for wait in waits:
        wait()
    entries.wait()


def pick_pivot(ids, child_map, child, entries):
    width = 2 * TILE + BLK + entries.shape[-1]
    return pl.pallas_call(
        pick_pivot_kernel,
        out_shape=jax.ShapeDtypeStruct((TILE, width), child.dtype),
        in_specs=[SMEM, SMEM, ANY, ANY],
        out_specs=VMEM,
        scratch_shapes=[pltpu.SemaphoreType.DMA((GROUPS,)), pltpu.SemaphoreType.DMA((1,))],
        compiler_params=pltpu.CompilerParams(vmem_limit_bytes=56 * 2**20),
        name="pick_pivot",
    )(ids, child_map, child, entries)


def pick_rest_kernel(ids_ref, map_ref, next_ref, child_ref, *refs):
    halves_out, outs, (first_sems, sems) = refs[:2], refs[2:8], refs[8:]
    count = child_ref.shape[0]
    leaf, column = ids_ref[0], ids_ref[1]
    half, pair = leaf & 1, leaf >> 1
    slots = range(1, count + 1)
    groups = (2 * (1 - half), 2 * (1 - half) + 1, 2 * half, 2 * half + 1)
    waits = move_separator(
        leaf, column, map_ref, child_ref, slots, groups,
        lambda slot, position: halves_out[position // 2].at[slot - 1, :, pl.ds(position % 2 * TILE, TILE)],
        first_sems,
    )
    rows = [find_tile(map_ref, leaf, column, slot, count) for slot in slots]
    used = 0
    for which, device in enumerate((leaf ^ 1, leaf)):
        for position, target in enumerate(column_targets(device & 1, (device >> 1) & 1)):
            group = target & 3
            update = find_tile(next_ref, pair, group, target >> 2, count)
            place = find_tile(map_ref, leaf, group, update + 1, count)
            column_live = jnp.logical_and(update >= 0, place >= 0)
            source_span = pl.ds(pl.multiple_of((jnp.maximum(place, 0) * GROUPS + group) * TILE, TILE), TILE)
            for slot, row in enumerate(rows):
                live = jnp.logical_and(column_live, row >= 0)
                source = child_ref.at[jnp.maximum(row, 0), :, source_span]
                if position % 4 == 0:
                    goal = outs[3 * which].at[slot, :, pl.ds(position // 4 * TILE, TILE)]
                else:
                    goal = outs[3 * which + 1 + position // 4].at[slot, :, pl.ds((position % 4 - 1) * TILE, TILE)]
                waits.append(move_tile(live, source, goal, sems.at[used]))
                used += 1
    for wait in waits:
        wait()


def pick_rest(ids, child_map, next_map, child):
    count = child.shape[0]
    widths = (2 * TILE, 2 * TILE) + (2 * TILE, 3 * TILE, 3 * TILE) * 2
    return pl.pallas_call(
        pick_rest_kernel,
        out_shape=tuple(jax.ShapeDtypeStruct((count, TILE, width), child.dtype) for width in widths),
        in_specs=[SMEM, SMEM, SMEM, ANY],
        out_specs=(VMEM,) * 8,
        scratch_shapes=[pltpu.SemaphoreType.DMA((GROUPS * count,)), pltpu.SemaphoreType.DMA((16 * count,))],
        compiler_params=pltpu.CompilerParams(vmem_limit_bytes=56 * 2**20),
        cost_estimate=pl.CostEstimate(flops=0, bytes_accessed=2 * 10**7, transcendentals=0),
        name="pick_rest",
    )(ids, child_map, next_map, child)


def solve_blocks(coupling_ref, lowers, inverses, panel_ref):
    split = lowers[0].shape[1]
    solved = []
    for k in range(panel_ref.shape[1] // TILE):
        span = slice(k * TILE, (k + 1) * TILE)
        rest = coupling_ref[:, span]
        if k:
            left = jnp.concatenate([part[0] for part in solved], axis=1)
            low = jnp.concatenate([part[1] for part in solved], axis=1)
            strip = lowers[0][span, 0 : min(k * TILE, split)]
            if k * TILE > split:
                inner = slice(k * TILE - split, (k + 1) * TILE - split)
                strip = jnp.concatenate([strip, lowers[1][inner, 0 : k * TILE - split]], axis=1)
            high_lower, low_lower = halves(strip)
            rest = rest - dot_lanes(
                jnp.concatenate([left, low, left], axis=1),
                jnp.concatenate([high_lower, high_lower, low_lower], axis=1),
            )
        tiles = split // TILE
        inverse = inverses[0][k] if k < tiles else inverses[1][k - tiles]
        block = dot_lanes(left_parts(rest), right_lanes(inverse))
        panel_ref[:, span] = block
        solved.append(halves(block))
    return jnp.concatenate([part[0] for part in solved], axis=1)


def write_factor(column, offset, lowers, panel, factor_ref):
    width = factor_ref.shape[-1]
    split = lowers[0].shape[1]
    per = split // width
    tiles = split // TILE
    span = pl.ds(pl.multiple_of(offset * width, width), width)
    factor_ref[0] = jnp.zeros(factor_ref.shape[1:], factor_ref.dtype)

    @pl.when(offset < per)
    def _():
        inner = pl.ds(pl.multiple_of(jnp.minimum(offset, per - 1) * width, width), width)
        factor_ref[0] = lowers[0][pl.ds(pl.multiple_of(column * TILE, TILE), TILE), inner]

    @pl.when(jnp.logical_and(offset >= per, column >= tiles))
    def _():
        inner = pl.ds(pl.multiple_of(jnp.maximum(offset - per, 0) * width, width), width)
        rows = pl.ds(pl.multiple_of(jnp.maximum(column - tiles, 0) * TILE, TILE), TILE)
        factor_ref[0] = lowers[1][rows, inner]

    for s in range(factor_ref.shape[0] - 1):
        factor_ref[s + 1] = panel[s * TILE : (s + 1) * TILE, span]


def panel_one_kernel(ids_ref, next_ref, mine_ref, peer_ref, *refs):
    lowers, inverses = refs[:2], refs[2:4]
    factor_ref, round_ref, first_ref, second_ref, third_ref, coupling, panel, round_in, sems = refs[4:]
    leaf, column = ids_ref[0], ids_ref[1]
    half, pair = leaf & 1, leaf >> 1
    count, _, width = mine_ref.shape
    for ref, place in ((mine_ref, half), (peer_ref, 1 - half)):
        span = pl.ds(pl.multiple_of(place * width, width), width)
        for s in range(count):
            coupling[s * TILE : (s + 1) * TILE, span] = ref[s].astype(jnp.float32)
    rounded = solve_blocks(coupling, lowers, inverses, panel)
    for s in range(count):
        round_in[s] = rounded[s * TILE : (s + 1) * TILE]
    copy = pltpu.make_async_copy(round_in, round_ref, sems.at[0])
    copy.start()
    write_factor(column, half, lowers, panel, factor_ref)
    heavy = half == (column & 1)
    for a, share_ref in ((0, first_ref), (jnp.where(heavy, 1, 0), second_ref), (2, third_ref)):
        slot = jnp.int32(0)
        for target in column_targets(half, 0):
            hit = jnp.logical_and((target & 3) == column, share_place(target, half) == a)
            slot = jnp.where(hit, target >> 2, slot)
        tile = find_tile(next_ref, pair, column, slot, count)
        share_ref[...] = round_in[jnp.maximum(tile, 0)]
    copy.wait()


def panel_one(ids, next_map, mine, peer, lowers, inverses):
    count = mine.shape[0]
    order = lowers[0].shape[0]
    return pl.pallas_call(
        panel_one_kernel,
        out_shape=(
            jax.ShapeDtypeStruct((count + 1, TILE, order // 2), jnp.float32),
            jax.ShapeDtypeStruct((count, TILE, order), jnp.bfloat16),
        )
        + (jax.ShapeDtypeStruct((TILE, order), jnp.bfloat16),) * 3,
        in_specs=[SMEM, SMEM] + [VMEM] * 6,
        out_specs=(VMEM, HBM, VMEM, VMEM, VMEM),
        scratch_shapes=[
            pltpu.VMEM((count * TILE, order), jnp.float32),
            pltpu.VMEM((count * TILE, order), jnp.float32),
            pltpu.VMEM((count, TILE, order), jnp.bfloat16),
            pltpu.SemaphoreType.DMA((1,)),
        ],
        compiler_params=PARAMS,
        cost_estimate=pl.CostEstimate(flops=10**9, bytes_accessed=10**6, transcendentals=0),
        name="panel_one",
    )(ids, next_map, mine, peer, *lowers, *inverses)


def panel_two_kernel(ids_ref, own_ref, x_ref, z_ref, both_ref, *refs):
    lowers, inverses = refs[:2], refs[2:4]
    factor_ref, round_ref, share_ref, coupling, panel, round_in, sems = refs[4:]
    leaf, column = ids_ref[0], ids_ref[1]
    half, side = leaf & 1, (leaf >> 1) & 1
    quarter = leaf & 3
    count = round_ref.shape[0]
    for place, ref in (
        (2 * side + half, own_ref),
        (2 * side + 1 - half, x_ref),
        (2 * (1 - side) + half, z_ref),
        (2 * (1 - side) + 1 - half, both_ref),
    ):
        coupling[:, pl.ds(pl.multiple_of(place * TILE, TILE), TILE)] = ref[...].astype(jnp.float32)
    rounded = solve_blocks(coupling, lowers, inverses, panel)
    for s in range(count):
        round_in[s] = rounded[s * TILE : (s + 1) * TILE]
    copy = pltpu.make_async_copy(round_in, round_ref, sems.at[0])
    copy.start()
    write_factor(column, quarter, lowers, panel, factor_ref)
    chosen = jnp.int32(0)
    for i in range(3):
        tile = 3 * quarter + i
        chosen = jnp.where((tile & 3) == column, tile >> 2, chosen)
    share_ref[...] = round_in[chosen]
    copy.wait()


def panel_two(ids, parts, lowers, inverses):
    rows = parts[0].shape[0]
    count = rows // TILE
    order = lowers[0].shape[0]
    return pl.pallas_call(
        panel_two_kernel,
        out_shape=(
            jax.ShapeDtypeStruct((count + 1, TILE, order // 4), jnp.float32),
            jax.ShapeDtypeStruct((count, TILE, order), jnp.bfloat16),
            jax.ShapeDtypeStruct((TILE, order), jnp.bfloat16),
        ),
        in_specs=[SMEM] + [VMEM] * 8,
        out_specs=(VMEM, HBM, VMEM),
        scratch_shapes=[
            pltpu.VMEM((rows, order), jnp.float32),
            pltpu.VMEM((rows, order), jnp.float32),
            pltpu.VMEM((count, TILE, order), jnp.bfloat16),
            pltpu.SemaphoreType.DMA((1,)),
        ],
        compiler_params=PARAMS,
        cost_estimate=pl.CostEstimate(flops=10**9, bytes_accessed=10**6, transcendentals=0),
        name="panel_two",
    )(ids, *parts, *lowers, *inverses)


def take_tile(owner, column, refs, live, target, sem):
    for apart, ref in enumerate(refs):

        @pl.when(jnp.logical_and(live, (owner ^ column) == apart))
        def _():
            pltpu.make_async_copy(ref, target, sem).start()


def start_shared(ids_ref, positions, firsts, thirds, taken, sems):
    leaf, column = ids_ref[0], ids_ref[1]
    half, side = leaf & 1, (leaf >> 1) & 1
    targets = column_targets(half, side)
    copies = []
    for i, position in enumerate(positions):
        target = targets[position]
        group = target & 3
        place = share_place(target, half)
        take_tile(group, column, firsts, place < 2, taken.at[i], sems.at[i])
        if thirds:
            take_tile(group, column, thirds, place == 2, taken.at[i], sems.at[i])
        copies.append(pltpu.make_async_copy(firsts[0], taken.at[i], sems.at[i]))
    return copies


class Loads:
    def __init__(self, sources, targets, sems):
        self.copies = [pltpu.make_async_copy(*each, sems.at[k]) for k, each in enumerate(zip(sources, targets))]

    def start(self, chosen):
        for k in chosen:
            self.copies[k].start()

    def wait(self, chosen):
        for k in chosen:
            self.copies[k].wait()


def update_columns(ids_ref, next_ref, positions, shared, refs, write):
    leaf, column = ids_ref[0], ids_ref[1]
    half, side, pair = leaf & 1, (leaf >> 1) & 1, leaf >> 1
    sources, (keep_in, peer_in, round_in, taken, tiles, sems, load_sems) = refs
    count = keep_in.shape[0]
    loads = Loads(sources, (keep_in, peer_in, round_in), load_sems)
    loads.start((2,))
    copies = start_shared(ids_ref, positions, *shared, taken, sems)
    loads.start((0, 1))
    targets = column_targets(half, side)
    rows = [find_tile(next_ref, pair, column, slot, count) for slot in range(count + 1)]
    tiles[:, count] = jnp.zeros_like(tiles[:, count])
    loads.wait((2,))
    for i, position in enumerate(positions):
        target = targets[position]
        live = find_tile(next_ref, pair, target & 3, target >> 2, count) >= 0
        span = slice(i * TILE, (i + 1) * TILE)
        copies[i].wait()
        for s in range(count):
            product = dot_lanes(round_in[s], taken[i])
            if i == 0 and s == 0:
                loads.wait((0, 1))
            value = keep_in[s, :, span].astype(jnp.float32) + peer_in[s, :, span].astype(jnp.float32) - product
            tiles[i, s] = jnp.where(live, value, 0.0).astype(jnp.bfloat16)
        for slot, row in enumerate(rows):
            write(i, slot, lambda row=row: tiles[i, jnp.where(row < 0, count, row)])


def update_scratch(count, width, order):
    return [
        pltpu.VMEM((count, TILE, width * TILE), jnp.bfloat16),
        pltpu.VMEM((count, TILE, width * TILE), jnp.bfloat16),
        pltpu.VMEM((count, TILE, order), jnp.bfloat16),
        pltpu.VMEM((width, TILE, order), jnp.bfloat16),
        pltpu.VMEM((width, count + 1, TILE, TILE), jnp.bfloat16),
        pltpu.SemaphoreType.DMA((width,)),
        pltpu.SemaphoreType.DMA((3,)),
    ]


def update_separator_kernel(ids_ref, next_ref, *refs):
    sources, firsts, (pivot_ref, near_ref, far_ref), scratch = refs[:3], refs[3:7], refs[7:10], refs[10:]

    def write(i, slot, tile):
        if slot == 0:
            pivot_ref[:, i * TILE : (i + 1) * TILE] = tile()
        else:
            (near_ref, far_ref)[i][slot - 1] = tile()

    update_columns(ids_ref, next_ref, (0, 4), (firsts, ()), (sources, scratch), write)


def update_separator(ids, next_map, keep, peer, rounded, firsts):
    count, _, order = rounded.shape
    tile = jax.ShapeDtypeStruct((count, TILE, TILE), jnp.bfloat16)
    return pl.pallas_call(
        update_separator_kernel,
        out_shape=(jax.ShapeDtypeStruct((TILE, 2 * TILE), jnp.bfloat16), tile, tile),
        in_specs=[SMEM, SMEM] + [ANY] * 7,
        out_specs=(VMEM, VMEM, VMEM),
        scratch_shapes=update_scratch(count, 2, order),
        compiler_params=pltpu.CompilerParams(vmem_limit_bytes=56 * 2**20),
        cost_estimate=pl.CostEstimate(flops=10**8, bytes_accessed=10**5, transcendentals=0),
        name="update_separator",
    )(ids, next_map, keep, peer, rounded, *firsts)


def update_trailing_kernel(positions, ids_ref, next_ref, *refs):
    sources, seconds, thirds, out_ref, scratch = refs[:3], refs[3:7], refs[7:11], refs[11], refs[12:]

    def write(i, slot, tile):
        if slot:
            out_ref[slot - 1, :, i * TILE : (i + 1) * TILE] = tile()

    update_columns(ids_ref, next_ref, positions, (seconds, thirds), (sources, scratch), write)


def update_trailing(ids, next_map, keep, peer, rounded, seconds, thirds, positions):
    count, _, order = rounded.shape
    width = len(positions)
    return pl.pallas_call(
        functools.partial(update_trailing_kernel, positions),
        out_shape=jax.ShapeDtypeStruct((count, TILE, width * TILE), jnp.bfloat16),
        in_specs=[SMEM, SMEM] + [ANY] * 11,
        out_specs=VMEM,
        scratch_shapes=update_scratch(count, width, order),
        compiler_params=pltpu.CompilerParams(vmem_limit_bytes=56 * 2**20),
        cost_estimate=pl.CostEstimate(flops=10**8, bytes_accessed=10**5, transcendentals=0),
        name="update_trailing",
    )(ids, next_map, keep, peer, rounded, *seconds, *thirds)


def update_two_kernel(ids_ref, *refs):
    sources, firsts, out_ref = refs[:3], refs[3:7], refs[7]
    near_in, far_in, round_in, taken, sems, load_sems = refs[8:]
    quarter, column = ids_ref[0] & 3, ids_ref[1]
    loads = Loads(sources, (near_in, far_in, round_in), load_sems)
    loads.start((2,))
    for i in range(3):
        take_tile((3 * quarter + i) & 3, column, firsts, True, taken.at[i], sems.at[i])
    loads.start((0, 1))
    loads.wait((2,))
    for i in range(3):
        span = slice(i * TILE, (i + 1) * TILE)
        pltpu.make_async_copy(firsts[0], taken.at[i], sems.at[i]).wait()
        for s in range(near_in.shape[0]):
            product = dot_lanes(round_in[s], taken[i])
            if i == 0 and s == 0:
                loads.wait((0, 1))
            total = near_in[s, :, span].astype(jnp.float32) + far_in[s, :, span].astype(jnp.float32)
            out_ref[s, :, span] = (total - product).astype(jnp.bfloat16)


def update_two(ids, near, far, rounded, firsts):
    order = rounded.shape[-1]
    return pl.pallas_call(
        update_two_kernel,
        out_shape=jax.ShapeDtypeStruct(near.shape, jnp.bfloat16),
        in_specs=[SMEM] + [ANY] * 7,
        out_specs=VMEM,
        scratch_shapes=[
            pltpu.VMEM(near.shape, jnp.bfloat16),
            pltpu.VMEM(far.shape, jnp.bfloat16),
            pltpu.VMEM(rounded.shape, jnp.bfloat16),
            pltpu.VMEM((3, TILE, order), jnp.bfloat16),
            pltpu.SemaphoreType.DMA((3,)),
            pltpu.SemaphoreType.DMA((3,)),
        ],
        compiler_params=pltpu.CompilerParams(vmem_limit_bytes=56 * 2**20),
        cost_estimate=pl.CostEstimate(flops=2 * 10**9, bytes_accessed=10**7, transcendentals=0),
        name="update_two",
    )(ids, near, far, rounded, *firsts)


def first_hop(pack):
    return swapped(pack, "leaf", 1), swapped(pack, "front", 2), swapped(pack, "front", 1)


def over_square(pack, hop, beside):
    half = pack.shape[0] // 2
    x, y, core = hop
    x, y = lax.optimization_barrier((x, y, beside))[:2]
    top = swapped(y[:half], "leaf", 1)
    low = swapped(x[half:], "front", 2)
    x_core, y_core = swapped(x, "front", 1), swapped(y, "front", 1)
    top_core, low_core = swapped(top, "front", 1), swapped(low, "front", 1)
    return (pack, core, y, y_core, x, x_core, top, low, top_core, low_core)


def over_front(tile, y, *earlier):
    return (tile, swapped(tile, "front", 1), y, swapped(after(y, *earlier), "front", 1))


def over_heavy(tile, y, *earlier):
    return (tile, swapped_heavy(tile, 1), y, swapped_heavy(after(y, *earlier), 1))


def after(value, *earlier):
    return lax.optimization_barrier((value, *earlier))[0]


def own_mask(mask, front, column, count):
    rows = lax.dynamic_index_in_dim(mask, front, 0, keepdims=False).reshape(count, GROUPS, -1)
    return lax.dynamic_index_in_dim(rows, column, 1, keepdims=False).astype(jnp.float32)


def body(child_update, sep_one, sep_two, map_one, map_two, mask_one, mask_two):
    column = lax.axis_index("front")
    leaf = lax.axis_index("leaf")
    quad, quarter = leaf >> 2, leaf & 3
    ids = jnp.stack([leaf, column]).astype(jnp.int32)
    child = child_update[0, 0, 0]
    entries_one = sep_one[0, 0, 0]
    entries_two = sep_two[0, 0, 0]
    count = child.shape[0]
    order = GROUPS * TILE
    maps_one = map_one[:, 0]
    maps_two = map_two[:, 0]

    pivot_mine = pick_pivot(ids, maps_one, child, entries_one)
    mask_first = own_mask(mask_one, leaf >> 1, column, count)
    mask_first = lax.dynamic_slice_in_dim(mask_first, 2 * (leaf & 1), 2, 1)
    mask_first = jnp.repeat(mask_first, TILE, axis=1)[:, None, :]
    mask_second = lax.dynamic_index_in_dim(own_mask(mask_two, quad, column, count), quarter, 1, keepdims=False)
    ids_early, mask_first, mask_second = lax.optimization_barrier((ids, mask_first, mask_second))
    coupling_send, coupling_keep, sep_send, near_send, far_send, sep_keep, near_keep, far_keep = pick_rest(
        ids_early, maps_one, maps_two, child
    )
    packs = over_square(pivot_mine, first_hop(pivot_mine), coupling_send)
    coupling_got = swapped(after(coupling_send, packs[4]), "leaf", 1)
    entries_far = swapped(entries_two[0], "leaf", 2)
    lower, inverse, rest = cholesky_first(ids, packs, fill_one, order, 2 * 10**10)
    coupling = (
        coupling_keep.astype(jnp.float32)
        + after(coupling_got, rest).astype(jnp.float32)
        + entries_one[1:].astype(jnp.float32) * mask_first
    )
    coupling_peer = swapped(coupling.astype(jnp.bfloat16), "leaf", 1)
    lower_rest, inverse_rest = cholesky_second(rest, 2 * 10**10)
    sep_peer = swapped(after(sep_send, lower_rest), "leaf", 1)
    far_peer = swapped(after(far_send, lower_rest), "leaf", 1)
    factor_one, rounded, first, second, third = panel_one(
        ids, maps_two, coupling, coupling_peer, (lower, lower_rest), (inverse, inverse_rest)
    )
    first_y = swapped_heavy(first, 2)
    firsts = over_heavy(first, first_y, sep_peer)
    pivot_own, near_coupling, far_coupling = update_separator(
        after(ids, entries_far), maps_two, sep_keep, sep_peer, rounded, firsts
    )
    second_y = swapped(after(second, first_y), "front", 2)
    third_y = swapped_heavy(after(third, first_y), 2)

    pivot_far = swapped(pivot_own, "leaf", 2)
    pivot_pack = pack_two(ids, pivot_own, after(pivot_far, second_y), entries_two[0], entries_far)
    hop = first_hop(after(pivot_pack, far_peer))
    seconds = over_front(second, second_y, pivot_pack)
    thirds = over_heavy(third, third_y, pivot_pack)
    far_trailing = update_trailing(
        ids, maps_two, far_keep, far_peer, after(rounded, pivot_far), seconds, thirds, (5, 6, 7)
    )
    packs = over_square(pivot_pack, hop, far_trailing)
    coupling_far = swapped(after(far_coupling, pivot_far), "leaf", 2)
    coupling = (
        near_coupling.astype(jnp.float32)
        + coupling_far.astype(jnp.float32)
        + entries_two[1:].astype(jnp.float32) * mask_second[:, None, None]
    ).reshape(count * TILE, TILE)
    coupling_sent = after(coupling.astype(jnp.bfloat16), packs[4])
    coupling_x, coupling_z, coupling_xz = (swapped(coupling_sent, "leaf", mask) for mask in (1, 2, 3))
    lower, inverse, rest = cholesky_first(ids, packs, fill_two, order, 2 * 10**10)
    trailing_far = swapped(after(far_trailing, rest), "leaf", 2)
    near_peer = swapped(after(near_send, rest), "leaf", 1)
    lower_rest, inverse_rest = cholesky_second(rest, 2 * 10**10)
    factor_two, rounded_two, share = panel_two(
        ids, (coupling, coupling_x, coupling_z, coupling_xz), (lower, lower_rest), (inverse, inverse_rest)
    )
    near_trailing = update_trailing(ids, maps_two, near_keep, near_peer, rounded, seconds, thirds, (1, 2, 3))
    shares = over_front(share, swapped(share, "front", 2), near_trailing, trailing_far)
    update = update_two(ids, near_trailing, trailing_far, rounded_two, shares)
    return (factor_one[None, None, None], factor_two[None, None, None], update[None, None, None])


def solution(mesh):
    split = P("leaf", "front", None, None, None, None)
    return jax.shard_map(
        body,
        mesh=mesh,
        in_specs=(split, split, split, P(), P(), P(), P()),
        out_specs=(split, split, split),
        check_vma=False,
    )
```
